128 devices in a mesh: tm: 8 (over z, core), tile: 16 (over x, y).
Axes of the slice: x: 4, y: 4, z: 4, core: 2. Of those that a mesh axis runs over, the one named last changes fastest.
Arguments:
- pix_grad: bfloat16 [128, 3, 256, 320], P(('tm', 'tile')), may hold values from -6 to 6
- frame_ids: int32 [128], P(('tm', 'tile')), may hold values from 0 to 15
- pre_norm: bfloat16 [16, 256, 30720], P('tm', None, 'tile'), may hold values from -6 to 6
- group_norm_gain: float32 [96], replicated, may hold values from 0.1 to 1.9
- group_norm_bias: float32 [96], replicated, may hold values from -3 to 3
- out_weight: bfloat16 [96, 3], replicated, may hold values from -0.625 to 0.625
- conv_weight: bfloat16 [27, 96, 384], replicated, may hold values from -0.0625 to 0.0625
- in_weight: bfloat16 [16, 384], replicated, may hold values from -1.5 to 1.5
Outputs:
- latent_grad: float32 [1024, 5120], P(('tm', 'tile'))
The draws below stay inside these ranges and needn't reach their ends.
All inputs are finite; a program needn't handle non-finite values.
Results may differ from the reference program's by a relative error of at most 0.0029.
Values may be sent and summed in bfloat16 or wider, within the bound.
A program may use at most 320 MiB of HBM per device.

```python
import math
import jax
import jax.numpy as jnp
import numpy as np
from jax import lax

OUTPUT_CHANNELS = 96
C1 = 384
LAT = 16
NORM_GROUPS = 32
HL = 128
LATENT_FRAMES = 16
OUTPUT_ROWS = 256
WL = 160
OUTPUT_COLUMNS = 320
SAMPLES = 128
HP = 64
WP = 80


def with_ends(result, own_key, low, high):
    longest = result.shape.index(max(result.shape))
    spots = []
    for shift in (0, 1):
        where = [jax.random.randint(jax.random.fold_in(own_key, axis), (), 0, length) for axis, length in enumerate(result.shape)]
        where[longest] = (where[longest] + shift) % result.shape[longest]
        spots.append(tuple(where))
    return result.at[spots[0]].set(low).at[spots[1]].set(high)


def shard_levels(key, extent, shards, low, largest):
    loudness, own = 1.0, jax.random.fold_in(key, 6)
    for axis_at, shards_of in shards:
        draws = jnp.exp(jax.random.uniform(jax.random.fold_in(own, axis_at), (shards_of,), jnp.float32, low / len(shards), largest / len(shards)))
        loudness = loudness * jnp.repeat(draws, extent[axis_at] // shards_of).reshape([-1 if axis == axis_at else 1 for axis in range(len(extent))])
    return loudness


def cumulative_ranks(number_of, lean):
    portions = [(1 << 20) // math.isqrt(rank ** lean) + 1 for rank in range(1, number_of + 1)]
    scale = 1 + sum(portions) // (1 << 30)
    return np.cumsum(np.array([max(1, weight // scale) for weight in portions]))


def ranked_ids(stream_key, extent, amount, slope):
    table = cumulative_ranks(amount, slope)
    lot = jax.random.randint(jax.random.fold_in(stream_key, 1), extent, 0, int(table[amount - 1]))
    standing = jnp.searchsorted(jnp.asarray(table, jnp.int32), lot, side="right")
    return jax.random.permutation(jax.random.fold_in(stream_key, 2), amount)[standing].astype(jnp.int32)


def scatter_about(rng, extent, scale, limit, cuts=(), kind=jnp.bfloat16):
    level = shard_levels(rng, extent, cuts, -0.22, 0.18) if cuts else 1.0
    values = jax.random.normal(rng, extent, jnp.float32) * scale * level
    return jnp.minimum(jnp.maximum(values, -limit), limit).astype(kind)


def setup_inputs(seed: int = 0) -> dict:
    key_list = jax.random.split(jax.random.key(seed), 9)
    pix_grad = scatter_about(key_list[0], (SAMPLES, 3, OUTPUT_ROWS, OUTPUT_COLUMNS), 1.0, 6.0, ((0, 128),))
    frame_ids = with_ends(ranked_ids(key_list[1], (SAMPLES,), LATENT_FRAMES, 2), jax.random.fold_in(key_list[1], 3), 0, LATENT_FRAMES - 1).astype(jnp.int32)
    pre_norm = scatter_about(key_list[2], (LATENT_FRAMES, OUTPUT_ROWS, OUTPUT_COLUMNS * OUTPUT_CHANNELS), 1.0, 6.0, ((0, 8), (2, 16)))
    group_norm_gain = jnp.clip(1.0 + 0.18 * jax.random.normal(key_list[3], (OUTPUT_CHANNELS,), jnp.float32), 0.1, 1.9)
    group_norm_bias = scatter_about(key_list[4], (OUTPUT_CHANNELS,), 0.5, 3.0, (), jnp.float32)
    out_weight = scatter_about(key_list[5], (OUTPUT_CHANNELS, 3), OUTPUT_CHANNELS ** -0.5, 0.625)
    conv_weight = scatter_about(key_list[6], (27, OUTPUT_CHANNELS, C1), (27 * C1) ** -0.5, 0.0625)
    in_weight = scatter_about(key_list[7], (LAT, C1), LAT ** -0.5, 1.5)
    return dict(pix_grad=pix_grad, frame_ids=frame_ids, pre_norm=pre_norm, group_norm_gain=group_norm_gain, group_norm_bias=group_norm_bias, out_weight=out_weight, conv_weight=conv_weight, in_weight=in_weight)


def reference(pix_grad, frame_ids, pre_norm, group_norm_gain, group_norm_bias, out_weight, conv_weight, in_weight):
    highest = lax.Precision.HIGHEST
    onehot = (frame_ids[None, :] == jnp.arange(LATENT_FRAMES, dtype=jnp.int32)[:, None]).astype(jnp.bfloat16)
    dpix = jnp.dot(onehot, pix_grad.reshape(SAMPLES, -1), preferred_element_type=jnp.float32)
    dpix = dpix.reshape(LATENT_FRAMES, 3, OUTPUT_ROWS, OUTPUT_COLUMNS)
    x = pre_norm.astype(jnp.float32).reshape(LATENT_FRAMES, OUTPUT_ROWS, OUTPUT_COLUMNS, OUTPUT_CHANNELS)
    da = jnp.einsum('fkhw,mk->fhwm', dpix, out_weight.astype(jnp.float32), precision=highest)
    grouped_input = x.reshape(LATENT_FRAMES, OUTPUT_ROWS, OUTPUT_COLUMNS, NORM_GROUPS, OUTPUT_CHANNELS // NORM_GROUPS)
    group_mean = lax.optimization_barrier(jnp.mean(grouped_input, axis=(1, 2, 4), keepdims=True))
    meansq = lax.optimization_barrier(jnp.mean(grouped_input * grouped_input, axis=(1, 2, 4), keepdims=True))
    inverse_deviation = lax.rsqrt(meansq - group_mean * group_mean + 1e-05)
    normalized_input = ((grouped_input - group_mean) * inverse_deviation).reshape(LATENT_FRAMES, OUTPUT_ROWS, OUTPUT_COLUMNS, OUTPUT_CHANNELS)
    norm_output = normalized_input * group_norm_gain + group_norm_bias
    sig = jax.nn.sigmoid(norm_output)
    dxh = (da * sig * (1.0 + norm_output * (1.0 - sig)) * group_norm_gain).reshape(LATENT_FRAMES, OUTPUT_ROWS, OUTPUT_COLUMNS, NORM_GROUPS, OUTPUT_CHANNELS // NORM_GROUPS)
    grouped_normalized = normalized_input.reshape(LATENT_FRAMES, OUTPUT_ROWS, OUTPUT_COLUMNS, NORM_GROUPS, OUTPUT_CHANNELS // NORM_GROUPS)
    first = lax.optimization_barrier(jnp.mean(dxh, axis=(1, 2, 4), keepdims=True))
    second = lax.optimization_barrier(jnp.mean(dxh * grouped_normalized, axis=(1, 2, 4), keepdims=True))
    dconv = (inverse_deviation * (dxh - first - grouped_normalized * second)).reshape(LATENT_FRAMES, OUTPUT_ROWS, OUTPUT_COLUMNS, OUTPUT_CHANNELS).astype(jnp.bfloat16)
    padded = jnp.pad(dconv, ((0, 2), (1, 1), (1, 1), (0, 0)))
    weights = conv_weight.reshape(27 * OUTPUT_CHANNELS, C1)
    in_f32 = in_weight.astype(jnp.float32)

    def one_frame(frame):
        block = lax.dynamic_slice_in_dim(padded, frame, 3, 0)
        pieces = []
        for tdel in range(3):
            for hdel in range(3):
                for wdel in range(3):
                    pieces.append(block[2 - tdel, 2 - hdel:2 - hdel + OUTPUT_ROWS, 2 - wdel:2 - wdel + OUTPUT_COLUMNS])
        cols = jnp.concatenate(pieces, axis=-1).reshape(OUTPUT_ROWS * OUTPUT_COLUMNS, 27 * OUTPUT_CHANNELS)
        dup = jnp.dot(cols, weights, preferred_element_type=jnp.float32)
        dfeat = dup.reshape(HL, 2, WL, 2, C1).sum(axis=(1, 3))
        return jnp.einsum('ijc,lc->ijl', dfeat, in_f32, precision=highest)
    dlat = lax.map(one_frame, jnp.arange(LATENT_FRAMES, dtype=jnp.int32))
    tokens = dlat.reshape(LATENT_FRAMES, HP, 2, WP, 2, LAT).transpose(0, 1, 3, 5, 2, 4)
    return tokens.reshape(LATENT_FRAMES * HP, WP * LAT * 4)
```

```python
import functools

import jax
import jax.numpy as jnp
from jax import lax
from jax.experimental import pallas as pl
from jax.experimental.pallas import tpu as pltpu
from jax.sharding import PartitionSpec as P

MESH = pl.DeviceIdType.MESH
F32 = jnp.float32
BF16 = jnp.bfloat16
HIGHEST = lax.Precision.HIGHEST
COUNT = 256.0 * 320.0 * 3.0
EPS = 1e-05
BLK = 384
PIECES = 10


def iota(shape, dim):
    return lax.broadcasted_iota(jnp.int32, shape, dim)


def remote(src, dst, send_sem, recv_sem, device):
    return pltpu.make_async_remote_copy(
        src_ref=src,
        dst_ref=dst,
        send_sem=send_sem,
        recv_sem=recv_sem,
        device_id=device,
        device_id_type=MESH,
    )


def kernel(
    pix_hbm,
    fid,
    x_hbm,
    gain,
    bias,
    ow,
    cw_hbm,
    iw,
    out,
    pixv,
    xb,
    cwv,
    sbuf,
    rbuf,
    sums,
    cbuf,
    part,
    zbuf,
    dpx,
    rmat,
    xs,
    fs,
    gmat,
    emat,
    stin,
    stsend,
    strecv,
    cst,
    gred,
    bmat,
    lhs,
    ys,
    tok,
    trecv,
    pix_sem,
    x_sem,
    cw_sem,
    s1s,
    s1r,
    cs,
    cr,
    zs,
    zr,
    sts,
    strs,
    tks,
    tkr,
):
    tm = lax.axis_index("tm")
    tl = lax.axis_index("tile")
    z = lax.div(tm, 2)
    c = lax.rem(tm, 2)
    below = lax.rem(tm + 7, 8)
    above = lax.rem(tm + 1, 8)

    pix_cp = pltpu.make_async_copy(pix_hbm.at[0], pixv, pix_sem)
    pix_cp.start()
    x_cps = []
    for f in range(2):
        for b in range(5):
            cp = pltpu.make_async_copy(
                x_hbm.at[f, :, pl.ds(BLK * b, BLK)], xb.at[f * 5 + b], x_sem.at[f * 5 + b]
            )
            cp.start()
            x_cps.append(cp)
    cw_cp = pltpu.make_async_copy(cw_hbm, cwv, cw_sem)
    cw_cp.start()

    barrier = pltpu.get_barrier_semaphore()

    def greet(device):
        pl.semaphore_signal(barrier, inc=1, device_id=device, device_id_type=MESH)

    def greet_tile(d, _):
        j = lax.rem(tl + d, 16)
        greet((tm, j))
        return 0

    lax.fori_loop(1, 16, greet_tile, 0)

    def greet_span(j, _):
        greet((below, j))
        greet((above, j))
        return 0

    lax.fori_loop(0, 16, greet_span, 0)
    for d in range(1, 4):
        greet((lax.rem(z + d, 4) * 2 + c, tl))

    lam = iota((BLK, 128), 0)
    chan = iota((BLK, 128), 1)
    same = (lax.div(lax.rem(lam, 96), 3) == lax.div(chan, 3)) & (chan < 96)
    gmat[...] = jnp.where(same, 1.0, 0.0)
    emat[...] = jnp.where(
        lax.rem(iota((128, BLK), 1), 96) == iota((128, BLK), 0), 1.0, 0.0
    )

    pix_cp.wait()
    frame_id = fid[0].astype(F32)
    lane = iota((128, 128), 1)
    low = lane < 64
    spare = lax.rem(lane, 64) >= 60
    lam1 = iota((1, 256), 1)
    q1 = lax.rem(lam1, 64)
    windows = ((0, 128), (0, 256), (128, 256), (128, 320))
    for n in range(4):
        acc = jnp.zeros((256, 256), F32)
        lo, hi = windows[n]
        for k in range(3):
            w1 = q1 - 20 * k
            target = 80 * n + 20 * lax.div(lam1, 64) + w1
            target = jnp.where((w1 >= 0) & (w1 < 20), target, -1)
            for base in range(lo, hi, 128):
                top = min(base + 128, hi)
                pick = jnp.where(iota((top - base, 256), 0) + base == target, 1.0, 0.0)
                acc = acc + jnp.dot(
                    pixv[k, :, base:top], pick.astype(BF16), preferred_element_type=F32
                )
        for pair in range(2):
            upper = acc[0:128, 128 * pair : 128 * pair + 128]
            lower = acc[128:256, 128 * pair : 128 * pair + 128]
            j = 4 * n + 2 * pair
            even = jnp.where(low, upper, pltpu.roll(lower, 64, 1))
            odd = jnp.where(low, pltpu.roll(upper, 64, 1), lower)
            sbuf[j] = jnp.where(spare, frame_id, even).astype(BF16)
            sbuf[j + 1] = jnp.where(spare, frame_id, odd).astype(BF16)

    pl.semaphore_wait(barrier, 15 + 32 + 3)

    def strip_copy(ch, d):
        j = lax.rem(tl + d, 16)
        rows = pl.ds(64 * ch, 64)
        return remote(
            sbuf.at[j, rows], rbuf.at[d, rows], s1s.at[ch, d], s1r.at[ch, d], (tm, j)
        )

    for ch in range(2):

        def send_strip(d, _, ch=ch):
            strip_copy(ch, d).start()
            return 0

        lax.fori_loop(1, 16, send_strip, 0)
    rbuf[0] = sbuf[tl]

    for cp in x_cps:
        cp.wait()

    def fold(v):
        return v.reshape(v.shape[0] // 8, 8, v.shape[1]).sum(axis=0)

    stin[...] = jnp.zeros((8, BLK), F32)
    for f in range(2):

        def stat_step(i, carry, f=f):
            s, ss = carry
            b = lax.div(i, 8)
            r = pl.multiple_of(lax.rem(i, 8) * 32, 32)
            v = xb[f * 5 + b, pl.ds(r, 32), :].astype(F32)
            return s + fold(v), ss + fold(v * v)

        zero = jnp.zeros((8, BLK), F32)
        s, ss = lax.fori_loop(0, 40, stat_step, (zero, zero))
        stin[2 * f : 2 * f + 1, :] = jnp.sum(s, axis=0, keepdims=True)
        stin[2 * f + 1 : 2 * f + 2, :] = jnp.sum(ss, axis=0, keepdims=True)

    def stat_copy(which, d):
        j = lax.rem(tl + d, 16)
        return remote(
            stsend.at[which],
            strecv.at[which, d],
            sts.at[which, d],
            strs.at[which, d],
            (tm, j),
        )

    def stat_send(which):
        red = jnp.dot(stin[...], gmat[...], precision=HIGHEST, preferred_element_type=F32)
        stsend[which] = red
        strecv[which, 0] = red

        def go(d, _):
            stat_copy(which, d).start()
            return 0

        lax.fori_loop(1, 16, go, 0)

    def stat_wait(which):
        def go(d, _):
            stat_copy(which, d).wait_recv()
            return 0

        lax.fori_loop(1, 16, go, 0)
        return jnp.sum(strecv[which], axis=0)

    stat_send(0)

    spread = jnp.where(lax.div(lax.rem(iota((128, 16), 0), 64), 4) == iota((128, 16), 1), 1.0, 0.0)
    iwr = jnp.dot(spread.astype(BF16), iw[...], preferred_element_type=F32).astype(BF16)
    cw_cp.wait()

    def reduce_tap(k, _):
        gred[k] = lax.dot_general(
            cwv[k], iwr, (((1,), (1,)), ((), ())), preferred_element_type=F32
        )
        return 0

    lax.fori_loop(0, 27, reduce_tap, 0)

    ln = iota((16, 128), 1)
    main = ln < 64
    b0 = lax.rem(ln, 2) == 0
    a0 = lax.rem(lax.div(ln, 2), 2) == 0

    def combine(mc, _):
        r = pl.multiple_of(mc * 16, 16)
        for dt in range(3):
            cols = []
            for dh in range(3):
                g = [gred[9 * dt + 3 * dh + dw, pl.ds(r, 16), :] for dw in range(3)]
                g01 = g[0] + g[1]
                g12 = g[1] + g[2]
                zero = jnp.zeros_like(g01)
                cols.append(
                    (
                        jnp.where(main, jnp.where(b0, g12, zero), jnp.where(b0, zero, g[0])),
                        jnp.where(main, jnp.where(b0, g01, g[2]), zero),
                        jnp.where(main, jnp.where(b0, g[0], g12), zero),
                        jnp.where(main, jnp.where(b0, zero, g01), jnp.where(b0, g[2], zero)),
                    )
                )
            for w in range(4):
                h0, h1, h2 = (cols[dh][w] for dh in range(3))
                h01 = h0 + h1
                h12 = h1 + h2
                zero = jnp.zeros_like(h01)
                taps = (
                    jnp.where(a0, h2, zero),
                    jnp.where(a0, h12, zero),
                    jnp.where(a0, h01, h2),
                    jnp.where(a0, h0, h12),
                    jnp.where(a0, zero, h01),
                    jnp.where(a0, zero, h0),
                )
                for t in range(6):
                    row = pl.multiple_of(t * BLK + w * 96 + r, 16)
                    top = taps[t].astype(BF16)
                    rest = (taps[t] - top.astype(F32)).astype(BF16)
                    bmat[pl.ds(row, 16), 128 * dt : 128 * dt + 128] = top
                    bmat[pl.ds(row, 16), BLK + 128 * dt : BLK + 128 * dt + 128] = rest
        return 0

    lax.fori_loop(0, 6, combine, 0)

    owe = lax.dot_general(
        ow[...].astype(F32), emat[0:96, :], (((0,), (0,)), ((), ())), preferred_element_type=F32
    )
    q = iota((64, BLK), 0)
    kq = lax.div(q, 20)
    wq = lax.rem(q, 20)
    wl = lax.div(iota((64, BLK), 1), 96)
    small = jnp.where(
        kq == 0, owe[0:1, :], jnp.where(kq == 1, owe[1:2, :], jnp.where(kq == 2, owe[2:3, :], 0.0))
    )
    none = jnp.zeros((64, BLK), BF16)
    for b in range(5):
        core = jnp.where(wq == wl + 4 * b, small, 0.0).astype(BF16)
        for half in range(2):
            for copy in range(2):
                at = 128 * copy
                rmat[half, b, at + 64 * half : at + 64 * half + 64, :] = core
                at = at + 64 * (1 - half)
                rmat[half, b, at : at + 64, :] = none

    tot = stat_wait(0) / COUNT
    rows = []
    for f in range(2):
        mean = tot[2 * f : 2 * f + 1]
        meansq = tot[2 * f + 1 : 2 * f + 2]
        rstd = lax.rsqrt(meansq - mean * mean + EPS)
        rows.append((mean, rstd))
    gn = gain[...]
    hb = 0.5 * bias[...]
    table = jnp.concatenate(
        [
            rows[0][0],
            rows[1][0],
            rows[0][1],
            rows[1][1],
            gn,
            hb,
            0.5 * rows[0][1] * gn,
            0.5 * rows[1][1] * gn,
        ],
        axis=0,
    )
    cst[...] = jnp.dot(table, emat[...], precision=HIGHEST, preferred_element_type=F32)

    for f in range(2):
        mean_l = cst[f : f + 1, :]
        a_l = cst[6 + f : 7 + f, :]
        hb_l = cst[5:6, :]
        g2_l = 0.5 * cst[4:5, :]

        def factor_step(i, _, f=f, mean_l=mean_l, a_l=a_l, hb_l=hb_l, g2_l=g2_l):
            b = lax.div(i, 8)
            r = pl.multiple_of(lax.rem(i, 8) * 32, 32)
            v = xb[f * 5 + b, pl.ds(r, 32), :].astype(F32) - mean_l
            u = v * a_l + hb_l
            h = jnp.tanh(u)
            w = (1.0 + u * (1.0 - h)) * ((1.0 + h) * g2_l)
            for i in range(3):
                xs[f * 5 + b, i, pl.ds(r, 32), :] = v[:, 128 * i : 128 * i + 128]
                fs[f * 5 + b, i, pl.ds(r, 32), :] = w[:, 128 * i : 128 * i + 128]
            return 0

        lax.fori_loop(0, 40, factor_step, 0)

    def core_copy(ch):
        return remote(
            sums.at[ch, 1 - c], cbuf.at[ch], cs.at[ch], cr.at[ch], (tm + 1 - 2 * c, tl)
        )

    def z_copy(ch, d):
        zz = lax.rem(z + d, 4)
        return remote(
            part.at[ch, zz],
            zbuf.at[ch, d - 1],
            zs.at[ch, d - 1],
            zr.at[ch, d - 1],
            (zz * 2 + c, tl),
        )

    onehot = None
    for ch in range(2):

        def recv_strip(d, _, ch=ch):
            strip_copy(ch, d).wait_recv()
            return 0

        lax.fori_loop(1, 16, recv_strip, 0)
        if onehot is None:
            ids = rbuf[:, 0:16, :].astype(F32).reshape(256, 128)
            ids = jnp.sum(jnp.where(iota((256, 128), 1) == 60, ids, 0.0), axis=1, keepdims=True)
            at = iota((256, 256), 1)
            order = lax.div(at, 16)
            frame = (
                4 * lax.rem(lax.div(order, 2), 4) + 2 * lax.div(order, 8) + lax.rem(order, 2)
            )
            hit = (ids == frame.astype(F32)) & (
                lax.rem(iota((256, 256), 0), 16) == lax.rem(at, 16)
            )
            onehot = jnp.where(hit, 1.0, 0.0).T.astype(BF16)
        stack = jnp.concatenate(
            [
                rbuf[:, 64 * ch + 16 * g : 64 * ch + 16 * g + 16, :].reshape(256, 128)
                for g in range(4)
            ],
            axis=1,
        )
        total = jnp.dot(onehot, stack, preferred_element_type=F32)
        for g in range(4):
            sums[ch, :, :, :, 16 * g : 16 * g + 16, :] = total[
                :, 128 * g : 128 * g + 128
            ].reshape(2, 4, 2, 16, 128)
        core_copy(ch).start()

    for ch in range(2):
        core_copy(ch).wait_recv()
        part[ch] = sums[ch, c] + cbuf[ch]
        for d in range(1, 4):
            z_copy(ch, d).start()

    for ch in range(2):
        for d in range(1, 4):
            z_copy(ch, d).wait_recv()
        dp = part[ch, z] + (zbuf[ch, 0] + zbuf[ch, 1] + zbuf[ch, 2])
        top = dp.astype(BF16)
        rest = (dp - top.astype(F32)).astype(BF16)
        for f in range(2):
            dpx[128 * f + 64 * ch : 128 * f + 64 * ch + 64, 0:128] = top[f]
            dpx[128 * f + 64 * ch : 128 * f + 64 * ch + 64, 128:256] = rest[f]

    carry = tuple(jnp.zeros((8, 128), F32) for _ in range(12))
    for half in range(2):

        def dxh_step(b, carry, half=half):
            da = jnp.dot(dpx[...], rmat[half, b], preferred_element_type=F32)
            new = []
            for f in range(2):
                at = pl.ds(128 * half, 128)
                s, sx = [], []
                for i in range(3):
                    v = da[128 * f : 128 * f + 128, 128 * i : 128 * i + 128]
                    v = v * fs[f * 5 + b, i, at, :]
                    fs[f * 5 + b, i, at, :] = v
                    s.append(carry[6 * f + i] + fold(v))
                    sx.append(carry[6 * f + 3 + i] + fold(v * xs[f * 5 + b, i, at, :]))
                new += s + sx
            return tuple(new)

        carry = lax.fori_loop(0, 5, dxh_step, carry)
    for i in range(12):
        stin[i // 3 : i // 3 + 1, 128 * (i % 3) : 128 * (i % 3) + 128] = jnp.sum(
            carry[i], axis=0, keepdims=True
        )
    stat_send(1)
    tot = stat_wait(1) / COUNT
    table = []
    for f in range(2):
        rstd = rows[f][1]
        first = tot[2 * f : 2 * f + 1]
        second = tot[2 * f + 1 : 2 * f + 2] * rstd
        table += [rstd, -rstd * rstd * second, -rstd * first, jnp.zeros_like(rstd)]
    cst[...] = jnp.dot(
        jnp.concatenate(table, axis=0), emat[...], precision=HIGHEST, preferred_element_type=F32
    )

    for f in range(2):
        p_l = cst[4 * f : 4 * f + 1, :]
        q_l = cst[4 * f + 1 : 4 * f + 2, :]
        r_l = cst[4 * f + 2 : 4 * f + 3, :]

        def lhs_step(b, _, f=f, p_l=p_l, q_l=q_l, r_l=r_l):
            fb = f * 5 + b
            row = iota((64, 128), 0)
            for rho in range(4):
                sel = pl.ds(rho, 64, stride=4)
                for i in range(3):
                    ls = slice(128 * i, 128 * i + 128)
                    d = p_l[:, ls] * fs[fb, i, sel, :] + q_l[:, ls] * xs[fb, i, sel, :] + r_l[:, ls]
                    at = BLK * (rho + 1) + 128 * i
                    lhs[fb, :, at : at + 128] = d.astype(BF16)
                    if rho == 0:
                        d = jnp.where(row == 63, 0.0, pltpu.roll(d, 63, 0))
                        lhs[fb, :, BLK * 5 + 128 * i : BLK * 5 + 128 * i + 128] = d.astype(BF16)
                    if rho == 3:
                        d = jnp.where(row == 0, 0.0, pltpu.roll(d, 1, 0))
                        lhs[fb, :, 128 * i : 128 * i + 128] = d.astype(BF16)
            return 0

        lax.fori_loop(0, 5, lhs_step, 0)

    left = lhs[...].reshape(640, 6 * BLK)
    ys[...] = jnp.dot(left, bmat[...], preferred_element_type=F32)

    ln = iota((64, 128), 1)
    lo64 = ln < 64
    odd = lax.rem(ln, 2) == 1

    def taken(f, dt, b):
        r = 64 * (5 * f + b)
        return (
            ys[r : r + 64, 128 * dt : 128 * dt + 128]
            + ys[r : r + 64, BLK + 128 * dt : BLK + 128 * dt + 128]
        )

    plans = (
        (1, 0, ((0, 0),)),
        (1, 1, ((0, 1), (1, 0))),
        (0, 0, ((0, 2), (1, 1))),
        (0, 1, ((1, 2),)),
    )
    for group, t, terms in plans:
        cc = []
        for b in range(5):
            v = taken(*terms[0], b)
            for term in terms[1:]:
                v = v + taken(*term, b)
            cc.append(v)
        r1 = pltpu.roll(cc[1], 64, 1)
        r3 = pltpu.roll(cc[3], 64, 1)
        v0 = jnp.where(
            lo64, cc[0] + jnp.where(odd, r1, 0.0), r1 + jnp.where(odd, cc[2], cc[0])
        )
        v1 = jnp.where(
            lo64, cc[2] + jnp.where(odd, r3, r1), r3 + jnp.where(odd, cc[4], cc[2])
        )
        v2 = jnp.where(lo64, cc[4] + jnp.where(odd, 0.0, r3), jnp.where(odd, cc[0], cc[4]))
        for i, v in enumerate((v0, v1, v2)):
            tok[group, 8 * t : 8 * t + 8, :, 128 * i : 128 * i + 128] = v.reshape(8, 8, 128)

    def own_copy(d, sending):
        j = lax.rem(tl + d, 16)
        at = tl if sending else lax.rem(tl + 16 - d, 16)
        return remote(tok.at[0, j], trecv.at[0, at], tks.at[0, d], tkr.at[0, at], (tm, j))

    def span_copy(j, sending):
        at = tl if sending else j
        return remote(tok.at[1, j], trecv.at[1, at], tks.at[1, j], tkr.at[1, at], (below, j))

    def send_span(j, _):
        span_copy(j, True).start()
        return 0

    lax.fori_loop(0, 16, send_span, 0)

    def send_own(d, _):
        own_copy(d, True).start()
        return 0

    lax.fori_loop(1, 16, send_own, 0)
    trecv[0, tl] = tok[0, tl]

    def recv_span(j, _):
        span_copy(j, False).wait_recv()
        return 0

    lax.fori_loop(0, 16, recv_span, 0)

    def recv_own(d, _):
        own_copy(d, False).wait_recv()
        return 0

    lax.fori_loop(1, 16, recv_own, 0)

    ln = iota((8, 128), 1)
    lo8 = ln < 64
    odd8 = lax.rem(ln, 2) == 1
    strips = []
    for j in range(16):
        strips.append(
            [
                trecv[0, j, :, 128 * i : 128 * i + 128]
                + jnp.where(tm < 7, trecv[1, j, :, 128 * i : 128 * i + 128], 0.0)
                for i in range(3)
            ]
        )
    halo = [pltpu.roll(s[2], 64, 1) for s in strips]
    for j in range(16):
        if j > 0:
            strips[j][0] = strips[j][0] + jnp.where(lo8 & ~odd8, halo[j - 1], 0.0)
    done = []
    for j in range(16):
        v2 = strips[j][2]
        if j < 15:
            v2 = v2 + jnp.where(odd8, halo[j + 1], 0.0)
        done.append((strips[j][0], strips[j][1], v2))
    for pair in range(8):
        e = done[2 * pair]
        o = [pltpu.roll(v, 64, 1) for v in done[2 * pair + 1]]
        at = 640 * pair
        out[:, at : at + 128] = e[0]
        out[:, at + 128 : at + 256] = e[1]
        out[:, at + 256 : at + 384] = jnp.where(lo8, e[2], o[0])
        out[:, at + 384 : at + 512] = jnp.where(lo8, o[0], o[1])
        out[:, at + 512 : at + 640] = jnp.where(lo8, o[1], o[2])

    for ch in range(2):

        def sent_strip(d, _, ch=ch):
            strip_copy(ch, d).wait_send()
            stat_copy(ch, d).wait_send()
            return 0

        lax.fori_loop(1, 16, sent_strip, 0)
        core_copy(ch).wait_send()
        for d in range(1, 4):
            z_copy(ch, d).wait_send()

    def sent_own(d, _):
        own_copy(d, True).wait_send()
        return 0

    lax.fori_loop(1, 16, sent_own, 0)

    def sent_span(j, _):
        span_copy(j, True).wait_send()
        return 0

    lax.fori_loop(0, 16, sent_span, 0)


def body(pix_grad, frame_ids, pre_norm, gain, bias, out_weight, conv_weight, in_weight):
    vmem = pl.BlockSpec(memory_space=pltpu.VMEM)
    anyspace = pl.BlockSpec(memory_space=pl.ANY)
    smem = pl.BlockSpec(memory_space=pltpu.SMEM)
    dma = pltpu.SemaphoreType.DMA
    gain = jnp.pad(gain, (0, 32)).reshape(1, 128)
    bias = jnp.pad(bias, (0, 32)).reshape(1, 128)
    return pl.pallas_call(
        kernel,
        out_shape=jax.ShapeDtypeStruct((8, 5120), F32),
        in_specs=[anyspace, smem, anyspace, vmem, vmem, vmem, anyspace, vmem],
        out_specs=vmem,
        scratch_shapes=[
            pltpu.VMEM((3, 256, 320), BF16),
            pltpu.VMEM((PIECES, 256, BLK), BF16),
            pltpu.VMEM((27, 96, 384), BF16),
            pltpu.VMEM((16, 128, 128), BF16),
            pltpu.VMEM((16, 128, 128), BF16),
            pltpu.VMEM((2, 2, 4, 2, 64, 128), F32),
            pltpu.VMEM((2, 4, 2, 64, 128), F32),
            pltpu.VMEM((2, 4, 2, 64, 128), F32),
            pltpu.VMEM((2, 3, 2, 64, 128), F32),
            pltpu.VMEM((256, 256), BF16),
            pltpu.VMEM((2, 5, 256, BLK), BF16),
            pltpu.VMEM((PIECES, 3, 256, 128), F32),
            pltpu.VMEM((PIECES, 3, 256, 128), F32),
            pltpu.VMEM((BLK, 128), F32),
            pltpu.VMEM((128, BLK), F32),
            pltpu.VMEM((8, BLK), F32),
            pltpu.VMEM((2, 8, 128), F32),
            pltpu.VMEM((2, 16, 8, 128), F32),
            pltpu.VMEM((8, BLK), F32),
            pltpu.VMEM((27, 96, 128), F32),
            pltpu.VMEM((6 * BLK, 2 * BLK), BF16),
            pltpu.VMEM((PIECES, 64, 6 * BLK), BF16),
            pltpu.VMEM((640, 2 * BLK), F32),
            pltpu.VMEM((2, 16, 8, BLK), F32),
            pltpu.VMEM((2, 16, 8, BLK), F32),
            dma,
            dma((PIECES,)),
            dma,
            dma((2, 16)),
            dma((2, 16)),
            dma((2,)),
            dma((2,)),
            dma((2, 3)),
            dma((2, 3)),
            dma((2, 16)),
            dma((2, 16)),
            dma((2, 16)),
            dma((2, 16)),
        ],
        compiler_params=pltpu.CompilerParams(
            collective_id=0, has_side_effects=True, vmem_limit_bytes=52 * 1024 * 1024
        ),
    )(pix_grad, frame_ids, pre_norm, gain, bias, out_weight, conv_weight, in_weight)


def solution(mesh):
    return jax.shard_map(
        body,
        mesh=mesh,
        in_specs=(
            P(("tm", "tile"), None, None, None),
            P(("tm", "tile")),
            P("tm", None, "tile"),
            P(),
            P(),
            P(),
            P(),
            P(),
        ),
        out_specs=P(("tm", "tile"), None),
        check_vma=False,
    )
```

```python
import functools

import jax
import jax.numpy as jnp
from jax import lax
from jax.experimental import pallas as pl
from jax.experimental.pallas import tpu as pltpu
from jax.sharding import PartitionSpec as P

MESH = pl.DeviceIdType.MESH
F32 = jnp.float32
BF16 = jnp.bfloat16
HIGHEST = lax.Precision.HIGHEST
COUNT = 256.0 * 320.0 * 3.0
EPS = 1e-05
BLK = 384
PIECES = 10


def iota(shape, dim):
    return lax.broadcasted_iota(jnp.int32, shape, dim)


def remote(src, dst, send_sem, recv_sem, device):
    return pltpu.make_async_remote_copy(
        src_ref=src,
        dst_ref=dst,
        send_sem=send_sem,
        recv_sem=recv_sem,
        device_id=device,
        device_id_type=MESH,
    )


def kernel(
    pix_hbm,
    fid,
    x_hbm,
    gain_hbm,
    bias_hbm,
    ow_hbm,
    cw_hbm,
    iw_hbm,
    out,
    gain,
    bias,
    ow,
    iw,
    pixv,
    xb,
    cwv,
    sbuf,
    rbuf,
    picks,
    sums,
    cbuf,
    part,
    zbuf,
    dpx,
    rmat,
    xs,
    fs,
    gmat,
    emat,
    stin,
    stsend,
    strecv,
    table,
    cst,
    gred,
    bmat,
    lhs,
    ys,
    tok,
    trecv,
    pix_sem,
    x_sem,
    cw_sem,
    small_sem,
    s1s,
    s1r,
    cs,
    cr,
    zs,
    zr,
    sts,
    strs,
    tks,
    tkr,
):
    tm = lax.axis_index("tm")
    tl = lax.axis_index("tile")
    z = lax.div(tm, 2)
    c = lax.rem(tm, 2)
    below = lax.rem(tm + 7, 8)
    above = lax.rem(tm + 1, 8)

    pix_cp = pltpu.make_async_copy(pix_hbm.at[0], pixv, pix_sem)
    pix_cp.start()
    x_cps = []
    for f in range(2):
        for b in range(5):
            cp = pltpu.make_async_copy(
                x_hbm.at[f, :, pl.ds(BLK * b, BLK)], xb.at[f * 5 + b], x_sem.at[f * 5 + b]
            )
            cp.start()
            x_cps.append(cp)
    small_cps = []
    for i, (src, dst) in enumerate(
        ((gain_hbm, gain), (bias_hbm, bias), (ow_hbm, ow), (iw_hbm, iw))
    ):
        cp = pltpu.make_async_copy(src, dst, small_sem.at[i])
        cp.start()
        small_cps.append(cp)
    cw_cp = pltpu.make_async_copy(cw_hbm, cwv, cw_sem)
    cw_cp.start()

    barrier = pltpu.get_barrier_semaphore()

    def greet(device):
        pl.semaphore_signal(barrier, inc=1, device_id=device, device_id_type=MESH)

    def greet_tile(d, _):
        j = lax.rem(tl + d, 16)
        greet((tm, j))
        return 0

    lax.fori_loop(1, 16, greet_tile, 0)

    def greet_span(j, _):
        greet((below, j))
        greet((above, j))
        return 0

    lax.fori_loop(0, 16, greet_span, 0)
    for d in range(1, 4):
        greet((lax.rem(z + d, 4) * 2 + c, tl))

    lam = iota((BLK, 128), 0)
    chan = iota((BLK, 128), 1)
    same = (lax.div(lax.rem(lam, 96), 3) == lax.div(chan, 3)) & (chan < 96)
    gmat[...] = jnp.where(same, 1.0, 0.0)
    emat[...] = jnp.where(
        lax.rem(iota((128, BLK), 1), 96) == iota((128, BLK), 0), 1.0, 0.0
    )

    def pack():
        pix_cp.wait()
        frame_id = fid[0].astype(F32)
        r = iota((256, 240), 0)
        m = iota((256, 240), 1)
        slot = lax.rem(r, 64)
        col = 20 * lax.div(r, 64) + lax.rem(slot, 20)
        hit = (slot < 60) & (m == 80 * lax.div(slot, 20) + col)
        pick = jnp.where(hit, 1.0, 0.0).astype(BF16)
        spare = lax.rem(iota((256, 256), 0), 64) >= 60
        for n in range(4):
            stack = jnp.concatenate(
                [pixv[k, 80 * n : 80 * n + 80, :] for k in range(3)], axis=0
            )
            rows = jnp.dot(pick, stack, preferred_element_type=F32)
            rows = jnp.where(spare, frame_id, rows).astype(BF16)
            for jj in range(4):
                for ch in range(2):
                    sbuf[ch, 4 * n + jj] = rows[
                        64 * jj : 64 * jj + 64, 128 * ch : 128 * ch + 128
                    ]

    pack()
    pl.semaphore_wait(barrier, 15 + 32 + 3)

    def strip_copy(ch, d):
        j = lax.rem(tl + d, 16)
        return remote(
            sbuf.at[ch, j], rbuf.at[ch, d], s1s.at[ch, d], s1r.at[ch, d], (tm, j)
        )

    for ch in range(2):

        def send_strip(d, _, ch=ch):
            strip_copy(ch, d).start()
            return 0

        lax.fori_loop(1, 16, send_strip, 0)
    for ch in range(2):
        rbuf[ch, 0] = sbuf[ch, tl]

    for cp in x_cps:
        cp.wait()

    def fold(v):
        return v.reshape(v.shape[0] // 8, 8, v.shape[1]).sum(axis=0)

    def stats():
        stin[...] = jnp.zeros((8, BLK), F32)
        for f in range(2):

            def stat_step(i, carry, f=f):
                s, ss = carry
                b = lax.div(i, 8)
                r = pl.multiple_of(lax.rem(i, 8) * 32, 32)
                v = xb[f * 5 + b, pl.ds(r, 32), :].astype(F32)
                return s + fold(v), ss + fold(v * v)

            zero = jnp.zeros((8, BLK), F32)
            s, ss = lax.fori_loop(0, 40, stat_step, (zero, zero))
            stin[2 * f : 2 * f + 1, :] = jnp.sum(s, axis=0, keepdims=True)
            stin[2 * f + 1 : 2 * f + 2, :] = jnp.sum(ss, axis=0, keepdims=True)

    stats()

    def stat_copy(which, d):
        j = lax.rem(tl + d, 16)
        return remote(
            stsend.at[which],
            strecv.at[which, d],
            sts.at[which, d],
            strs.at[which, d],
            (tm, j),
        )

    def stat_send(which):
        red = jnp.dot(stin[...], gmat[...], precision=HIGHEST, preferred_element_type=F32)
        stsend[which] = red
        strecv[which, 0] = red

        def go(d, _):
            stat_copy(which, d).start()
            return 0

        lax.fori_loop(1, 16, go, 0)

    def stat_wait(which):
        def go(d, _):
            stat_copy(which, d).wait_recv()
            return 0

        lax.fori_loop(1, 16, go, 0)
        return jnp.sum(strecv[which], axis=0)

    stat_send(0)

    cw_cp.wait()
    for cp in small_cps:
        cp.wait()

    spread = jnp.where(lax.div(lax.rem(iota((128, 16), 0), 64), 4) == iota((128, 16), 1), 1.0, 0.0)
    iwr = jnp.dot(spread.astype(BF16), iw[...], preferred_element_type=F32).astype(BF16)

    def reduce_tap(k, _):
        gred[k] = lax.dot_general(
            cwv[k], iwr, (((1,), (1,)), ((), ())), preferred_element_type=F32
        )
        return 0

    def taps_reduced():
        lax.fori_loop(0, 27, reduce_tap, 0)

    taps_reduced()

    ln = iota((16, 128), 1)
    main = ln < 64
    b0 = lax.rem(ln, 2) == 0
    a0 = lax.rem(lax.div(ln, 2), 2) == 0

    def combine(mc, _):
        r = pl.multiple_of(mc * 16, 16)
        for dt in range(3):
            cols = []
            for dh in range(3):
                g = [gred[9 * dt + 3 * dh + dw, pl.ds(r, 16), :] for dw in range(3)]
                g01 = g[0] + g[1]
                g12 = g[1] + g[2]
                zero = jnp.zeros_like(g01)
                cols.append(
                    (
                        jnp.where(main, jnp.where(b0, g12, zero), jnp.where(b0, zero, g[0])),
                        jnp.where(main, jnp.where(b0, g01, g[2]), zero),
                        jnp.where(main, jnp.where(b0, g[0], g12), zero),
                        jnp.where(main, jnp.where(b0, zero, g01), jnp.where(b0, g[2], zero)),
                    )
                )
            for w in range(4):
                h0, h1, h2 = (cols[dh][w] for dh in range(3))
                h01 = h0 + h1
                h12 = h1 + h2
                zero = jnp.zeros_like(h01)
                taps = (
                    jnp.where(a0, h2, zero),
                    jnp.where(a0, h12, zero),
                    jnp.where(a0, h01, h2),
                    jnp.where(a0, h0, h12),
                    jnp.where(a0, zero, h01),
                    jnp.where(a0, zero, h0),
                )
                for t in range(6):
                    row = pl.multiple_of(t * BLK + w * 96 + r, 16)
                    top = taps[t].astype(BF16)
                    rest = (taps[t] - top.astype(F32)).astype(BF16)
                    bmat[pl.ds(row, 16), 128 * dt : 128 * dt + 128] = top
                    bmat[pl.ds(row, 16), BLK + 128 * dt : BLK + 128 * dt + 128] = rest
        return 0

    def weights():
        lax.fori_loop(0, 6, combine, 0)

    weights()

    def colours():
        owe = jnp.dot(ow[...].astype(F32), emat[0:96, :], preferred_element_type=F32)
        q = iota((64, BLK), 0)
        kq = lax.div(q, 20)
        wq = lax.rem(q, 20)
        wl = lax.div(iota((64, BLK), 1), 96)
        small = jnp.where(
            kq == 0,
            owe[0:1, :],
            jnp.where(kq == 1, owe[1:2, :], jnp.where(kq == 2, owe[2:3, :], 0.0)),
        )
        for b in range(5):
            core = jnp.where(wq == wl + 4 * b, small, 0.0).astype(BF16)
            rmat[b, 0:64, :] = core
            rmat[b, 64:128, :] = core

    colours()

    tot = stat_wait(0) / COUNT
    rows = []
    for f in range(2):
        mean = tot[2 * f : 2 * f + 1]
        meansq = tot[2 * f + 1 : 2 * f + 2]
        rstd = lax.rsqrt(meansq - mean * mean + EPS)
        rows.append((mean, rstd))
    table[...] = jnp.zeros((8, 128), F32)
    for f in range(2):
        table[f : f + 1, :] = rows[f][0]
        table[6 + f : 7 + f, 0:96] = 0.5 * rows[f][1][:, 0:96] * gain[...]
    table[4:5, 0:96] = gain[...]
    table[5:6, 0:96] = 0.5 * bias[...]
    cst[...] = jnp.dot(table[...], emat[...], precision=HIGHEST, preferred_element_type=F32)

    def factor():
        for f in range(2):
            mean_l = cst[f : f + 1, :]
            a_l = cst[6 + f : 7 + f, :]
            hb_l = cst[5:6, :]
            g2_l = 0.5 * cst[4:5, :]

            def factor_step(i, _, f=f, mean_l=mean_l, a_l=a_l, hb_l=hb_l, g2_l=g2_l):
                b = lax.div(i, 8)
                r = pl.multiple_of(lax.rem(i, 8) * 32, 32)
                v = xb[f * 5 + b, pl.ds(r, 32), :].astype(F32) - mean_l
                u = v * a_l + hb_l
                h = jnp.tanh(u)
                w = (1.0 + u * (1.0 - h)) * ((1.0 + h) * g2_l)
                for i in range(3):
                    xs[f * 5 + b, i, pl.ds(r, 32), :] = v[:, 128 * i : 128 * i + 128]
                    fs[f * 5 + b, i, pl.ds(r, 32), :] = w[:, 128 * i : 128 * i + 128]
                return 0

            lax.fori_loop(0, 40, factor_step, 0)

    factor()

    def core_copy(ch):
        return remote(
            sums.at[ch, 1 - c], cbuf.at[ch], cs.at[ch], cr.at[ch], (tm + 1 - 2 * c, tl)
        )

    def z_copy(ch, d):
        zz = lax.rem(z + d, 4)
        return remote(
            part.at[ch, zz],
            zbuf.at[ch, d - 1],
            zs.at[ch, d - 1],
            zr.at[ch, d - 1],
            (zz * 2 + c, tl),
        )

    def frame_picks():
        ids = rbuf[0, :, 48:64, :].astype(F32)
        ids = jnp.broadcast_to(ids[:, 15:16, :], (16, 16, 128)).reshape(256, 128)
        ids = jnp.concatenate([ids, ids], axis=1)
        at = iota((256, 256), 1)
        order = lax.div(at, 16)
        frame = 4 * lax.rem(lax.div(order, 2), 4) + 2 * lax.div(order, 8) + lax.rem(order, 2)
        hit = (ids == frame.astype(F32)) & (lax.rem(iota((256, 256), 0), 16) == lax.rem(at, 16))
        picks[...] = jnp.where(hit, 1.0, 0.0).T.astype(BF16)

    def frame_sums(ch):
        stack = jnp.concatenate(
            [rbuf[ch, :, 16 * g : 16 * g + 16, :].reshape(256, 128) for g in range(4)], axis=1
        )
        total = jnp.dot(picks[...], stack, preferred_element_type=F32)
        for g in range(4):
            sums[ch, :, :, :, 16 * g : 16 * g + 16, :] = total[
                :, 128 * g : 128 * g + 128
            ].reshape(2, 4, 2, 16, 128)

    for ch in range(2):

        def recv_strip(d, _, ch=ch):
            strip_copy(ch, d).wait_recv()
            return 0

        lax.fori_loop(1, 16, recv_strip, 0)
        if ch == 0:
            frame_picks()
        frame_sums(ch)
        core_copy(ch).start()

    for ch in range(2):
        core_copy(ch).wait_recv()
        part[ch] = sums[ch, c] + cbuf[ch]
        for d in range(1, 4):
            z_copy(ch, d).start()

    for ch in range(2):
        for d in range(1, 4):
            z_copy(ch, d).wait_recv()
        def frame_rows(ch=ch):
            dp = part[ch, z] + (zbuf[ch, 0] + zbuf[ch, 1] + zbuf[ch, 2])
            for f in range(2):
                top = dp[f].astype(BF16)
                rest = dp[f] - top.astype(F32)
                both = jnp.concatenate([top.astype(F32), rest], axis=0).T
                dpx[ch, 128 * f : 128 * f + 128, :] = both.astype(BF16)

        frame_rows()

    def dxh():
        carry = tuple(jnp.zeros((8, 128), F32) for _ in range(12))
        for half in range(2):

            def dxh_step(b, carry, half=half):
                da = jnp.dot(dpx[half], rmat[b], preferred_element_type=F32)
                new = []
                for f in range(2):
                    at = pl.ds(128 * half, 128)
                    s, sx = [], []
                    for i in range(3):
                        v = da[128 * f : 128 * f + 128, 128 * i : 128 * i + 128]
                        v = v * fs[f * 5 + b, i, at, :]
                        fs[f * 5 + b, i, at, :] = v
                        s.append(carry[6 * f + i] + fold(v))
                        sx.append(carry[6 * f + 3 + i] + fold(v * xs[f * 5 + b, i, at, :]))
                    new += s + sx
                return tuple(new)

            carry = lax.fori_loop(0, 5, dxh_step, carry)
        for i in range(12):
            stin[i // 3 : i // 3 + 1, 128 * (i % 3) : 128 * (i % 3) + 128] = jnp.sum(
                carry[i], axis=0, keepdims=True
            )

    dxh()
    stat_send(1)
    tot = stat_wait(1) / COUNT
    terms = []
    for f in range(2):
        rstd = rows[f][1]
        first = tot[2 * f : 2 * f + 1]
        second = tot[2 * f + 1 : 2 * f + 2] * rstd
        terms += [rstd, -rstd * rstd * second, -rstd * first, jnp.zeros_like(rstd)]
    cst[...] = jnp.dot(
        jnp.concatenate(terms, axis=0), emat[...], precision=HIGHEST, preferred_element_type=F32
    )

    def left_side():
        for f in range(2):
            p_l = cst[4 * f : 4 * f + 1, :]
            q_l = cst[4 * f + 1 : 4 * f + 2, :]
            r_l = cst[4 * f + 2 : 4 * f + 3, :]

            def lhs_step(b, _, f=f, p_l=p_l, q_l=q_l, r_l=r_l):
                fb = f * 5 + b
                row = iota((64, 128), 0)
                for rho in range(4):
                    sel = pl.ds(rho, 64, stride=4)
                    for i in range(3):
                        ls = slice(128 * i, 128 * i + 128)
                        d = p_l[:, ls] * fs[fb, i, sel, :] + q_l[:, ls] * xs[fb, i, sel, :] + r_l[:, ls]
                        at = BLK * (rho + 1) + 128 * i
                        lhs[fb, :, at : at + 128] = d.astype(BF16)
                        if rho == 0:
                            d = jnp.where(row == 63, 0.0, pltpu.roll(d, 63, 0))
                            lhs[fb, :, BLK * 5 + 128 * i : BLK * 5 + 128 * i + 128] = d.astype(BF16)
                        if rho == 3:
                            d = jnp.where(row == 0, 0.0, pltpu.roll(d, 1, 0))
                            lhs[fb, :, 128 * i : 128 * i + 128] = d.astype(BF16)
                return 0

            lax.fori_loop(0, 5, lhs_step, 0)

    left_side()

    def conv():
        left = lhs[...].reshape(640, 6 * BLK)
        ys[...] = jnp.dot(left, bmat[...], preferred_element_type=F32)

    conv()

    ln = iota((64, 128), 1)
    lo64 = ln < 64
    odd = lax.rem(ln, 2) == 1

    def taken(f, dt, b):
        r = 64 * (5 * f + b)
        return (
            ys[r : r + 64, 128 * dt : 128 * dt + 128]
            + ys[r : r + 64, BLK + 128 * dt : BLK + 128 * dt + 128]
        )

    plans = (
        (1, 0, ((0, 0),)),
        (1, 1, ((0, 1), (1, 0))),
        (0, 0, ((0, 2), (1, 1))),
        (0, 1, ((1, 2),)),
    )
    def tokens():
        for group, t, terms in plans:
            cc = []
            for b in range(5):
                v = taken(*terms[0], b)
                for term in terms[1:]:
                    v = v + taken(*term, b)
                cc.append(v)
            r1 = pltpu.roll(cc[1], 64, 1)
            r3 = pltpu.roll(cc[3], 64, 1)
            v0 = jnp.where(
                lo64, cc[0] + jnp.where(odd, r1, 0.0), r1 + jnp.where(odd, cc[2], cc[0])
            )
            v1 = jnp.where(
                lo64, cc[2] + jnp.where(odd, r3, r1), r3 + jnp.where(odd, cc[4], cc[2])
            )
            v2 = jnp.where(lo64, cc[4] + jnp.where(odd, 0.0, r3), jnp.where(odd, cc[0], cc[4]))
            for i, v in enumerate((v0, v1, v2)):
                tok[group, 8 * t : 8 * t + 8, :, 128 * i : 128 * i + 128] = v.reshape(8, 8, 128)

    tokens()

    def own_copy(d, sending):
        j = lax.rem(tl + d, 16)
        at = tl if sending else lax.rem(tl + 16 - d, 16)
        return remote(tok.at[0, j], trecv.at[0, at], tks.at[0, d], tkr.at[0, at], (tm, j))

    def span_copy(j, sending):
        at = tl if sending else j
        return remote(tok.at[1, j], trecv.at[1, at], tks.at[1, j], tkr.at[1, at], (below, j))

    def send_span(j, _):
        span_copy(j, True).start()
        return 0

    lax.fori_loop(0, 16, send_span, 0)

    def send_own(d, _):
        own_copy(d, True).start()
        return 0

    lax.fori_loop(1, 16, send_own, 0)
    trecv[0, tl] = tok[0, tl]

    def recv_span(j, _):
        span_copy(j, False).wait_recv()
        return 0

    lax.fori_loop(0, 16, recv_span, 0)

    def recv_own(d, _):
        own_copy(d, False).wait_recv()
        return 0

    lax.fori_loop(1, 16, recv_own, 0)

    def assemble():
        ln = iota((8, 128), 1)
        lo8 = ln < 64
        odd8 = lax.rem(ln, 2) == 1
        strips = []
        for j in range(16):
            strips.append(
                [
                    trecv[0, j, :, 128 * i : 128 * i + 128]
                    + jnp.where(tm < 7, trecv[1, j, :, 128 * i : 128 * i + 128], 0.0)
                    for i in range(3)
                ]
            )
        halo = [pltpu.roll(s[2], 64, 1) for s in strips]
        for j in range(16):
            if j > 0:
                strips[j][0] = strips[j][0] + jnp.where(lo8 & ~odd8, halo[j - 1], 0.0)
        done = []
        for j in range(16):
            v2 = strips[j][2]
            if j < 15:
                v2 = v2 + jnp.where(odd8, halo[j + 1], 0.0)
            done.append((strips[j][0], strips[j][1], v2))
        for pair in range(8):
            e = done[2 * pair]
            o = [pltpu.roll(v, 64, 1) for v in done[2 * pair + 1]]
            at = 640 * pair
            out[:, at : at + 128] = e[0]
            out[:, at + 128 : at + 256] = e[1]
            out[:, at + 256 : at + 384] = jnp.where(lo8, e[2], o[0])
            out[:, at + 384 : at + 512] = jnp.where(lo8, o[0], o[1])
            out[:, at + 512 : at + 640] = jnp.where(lo8, o[1], o[2])

    assemble()

    for ch in range(2):

        def sent_strip(d, _, ch=ch):
            strip_copy(ch, d).wait_send()
            stat_copy(ch, d).wait_send()
            return 0

        lax.fori_loop(1, 16, sent_strip, 0)
        core_copy(ch).wait_send()
        for d in range(1, 4):
            z_copy(ch, d).wait_send()

    def sent_own(d, _):
        own_copy(d, True).wait_send()
        return 0

    lax.fori_loop(1, 16, sent_own, 0)

    def sent_span(j, _):
        span_copy(j, True).wait_send()
        return 0

    lax.fori_loop(0, 16, sent_span, 0)


def body(pix_grad, frame_ids, pre_norm, gain, bias, out_weight, conv_weight, in_weight):
    hbm = pl.BlockSpec(memory_space=pltpu.HBM)
    smem = pl.BlockSpec(memory_space=pltpu.SMEM)
    dma = pltpu.SemaphoreType.DMA
    pix_grad = jnp.transpose(pix_grad, (0, 1, 3, 2))
    out_weight = out_weight.T
    gain = gain.reshape(1, 96)
    bias = bias.reshape(1, 96)
    return pl.pallas_call(
        kernel,
        out_shape=jax.ShapeDtypeStruct((8, 5120), F32),
        in_specs=[hbm, smem] + [hbm] * 6,
        out_specs=pl.BlockSpec(memory_space=pltpu.VMEM),
        scratch_shapes=[
            pltpu.VMEM((1, 96), F32),
            pltpu.VMEM((1, 96), F32),
            pltpu.VMEM((3, 96), BF16),
            pltpu.VMEM((16, 384), BF16),
            pltpu.VMEM((3, 320, 256), BF16),
            pltpu.VMEM((PIECES, 256, BLK), BF16),
            pltpu.VMEM((27, 96, 384), BF16),
            pltpu.VMEM((2, 16, 64, 128), BF16),
            pltpu.VMEM((2, 16, 64, 128), BF16),
            pltpu.VMEM((256, 256), BF16),
            pltpu.VMEM((2, 2, 4, 2, 64, 128), F32),
            pltpu.VMEM((2, 4, 2, 64, 128), F32),
            pltpu.VMEM((2, 4, 2, 64, 128), F32),
            pltpu.VMEM((2, 3, 2, 64, 128), F32),
            pltpu.VMEM((2, 256, 128), BF16),
            pltpu.VMEM((5, 128, BLK), BF16),
            pltpu.VMEM((PIECES, 3, 256, 128), F32),
            pltpu.VMEM((PIECES, 3, 256, 128), F32),
            pltpu.VMEM((BLK, 128), F32),
            pltpu.VMEM((128, BLK), F32),
            pltpu.VMEM((8, BLK), F32),
            pltpu.VMEM((2, 8, 128), F32),
            pltpu.VMEM((2, 16, 8, 128), F32),
            pltpu.VMEM((8, 128), F32),
            pltpu.VMEM((8, BLK), F32),
            pltpu.VMEM((27, 96, 128), F32),
            pltpu.VMEM((6 * BLK, 2 * BLK), BF16),
            pltpu.VMEM((PIECES, 64, 6 * BLK), BF16),
            pltpu.VMEM((640, 2 * BLK), F32),
            pltpu.VMEM((2, 16, 8, BLK), F32),
            pltpu.VMEM((2, 16, 8, BLK), F32),
            dma,
            dma((PIECES,)),
            dma,
            dma((4,)),
            dma((2, 16)),
            dma((2, 16)),
            dma((2,)),
            dma((2,)),
            dma((2, 3)),
            dma((2, 3)),
            dma((2, 16)),
            dma((2, 16)),
            dma((2, 16)),
            dma((2, 16)),
        ],
        compiler_params=pltpu.CompilerParams(
            collective_id=0, has_side_effects=True, vmem_limit_bytes=62 * 1024 * 1024
        ),
    )(pix_grad, frame_ids, pre_norm, gain, bias, out_weight, conv_weight, in_weight)


def solution(mesh):
    return jax.shard_map(
        body,
        mesh=mesh,
        in_specs=(
            P(("tm", "tile"), None, None, None),
            P(("tm", "tile")),
            P("tm", None, "tile"),
            P(),
            P(),
            P(),
            P(),
            P(),
        ),
        out_specs=P(("tm", "tile"), None),
        check_vma=False,
    )
```

```python
import jax
import jax.numpy as jnp
from jax import lax
from jax.experimental import pallas as pl
from jax.experimental.pallas import tpu as pltpu
from jax.sharding import PartitionSpec as P

MESH = pl.DeviceIdType.MESH
F32 = jnp.float32
BF16 = jnp.bfloat16
HIGHEST = lax.Precision.HIGHEST
COUNT = 256.0 * 320.0 * 3.0
EPS = 1e-05
EIGHTHS = 8.0 / 0.6931471805599453
RANGE = 32700.0
BLK = 384
PIECES = 10


def iota(shape, dim):
    return lax.broadcasted_iota(jnp.int32, shape, dim)


def remote(src, dst, send_sem, recv_sem, device):
    return pltpu.make_async_remote_copy(
        src_ref=src,
        dst_ref=dst,
        send_sem=send_sem,
        recv_sem=recv_sem,
        device_id=device,
        device_id_type=MESH,
    )


def kernel(
    pix_hbm,
    fid,
    x_hbm,
    gain_hbm,
    bias_hbm,
    ow_hbm,
    cw_hbm,
    iw_hbm,
    out,
    gain,
    bias,
    ow,
    iw,
    pixv,
    xb,
    cwv,
    sbuf,
    rbuf,
    picks,
    sums,
    packs,
    zbuf,
    dpx,
    rmat,
    xs,
    fs,
    gmat,
    emat,
    stin,
    stsend,
    strecv,
    table,
    cst,
    gred,
    bmat,
    lhs,
    ys,
    tok,
    trecv,
    pix_sem,
    x_sem,
    cw_sem,
    small_sem,
    s1s,
    s1r,
    zs,
    zr,
    sts,
    strs,
    tks,
    tkr,
):
    tm = lax.axis_index("tm")
    tl = lax.axis_index("tile")
    z = lax.div(tm, 2)
    c = lax.rem(tm, 2)
    below = lax.rem(tm + 7, 8)
    above = lax.rem(tm + 1, 8)

    pix_cp = pltpu.make_async_copy(pix_hbm.at[0], pixv, pix_sem)
    pix_cp.start()
    x_cps = []
    for f in range(2):
        for b in range(5):
            cp = pltpu.make_async_copy(
                x_hbm.at[f, :, pl.ds(BLK * b, BLK)], xb.at[f * 5 + b], x_sem.at[f * 5 + b]
            )
            cp.start()
            x_cps.append(cp)
    small_cps = []
    for i, (src, dst) in enumerate(
        ((gain_hbm, gain), (bias_hbm, bias), (ow_hbm, ow), (iw_hbm, iw))
    ):
        cp = pltpu.make_async_copy(src, dst, small_sem.at[i])
        cp.start()
        small_cps.append(cp)
    cw_cp = pltpu.make_async_copy(cw_hbm, cwv, cw_sem)
    cw_cp.start()

    barrier = pltpu.get_barrier_semaphore()

    def greet(device):
        pl.semaphore_signal(barrier, inc=1, device_id=device, device_id_type=MESH)

    def greet_chip(d, _):
        j = lax.rem(tl + d, 16)
        greet((tm, j))
        greet((tm + 1 - 2 * c, j))
        return 0

    lax.fori_loop(1, 16, greet_chip, 0)
    greet((tm + 1 - 2 * c, tl))
    for d in range(1, 4):
        for r in range(2):
            greet((lax.rem(z + d, 4) * 2 + lax.rem(c + r, 2), tl))

    lam = iota((BLK, 128), 0)
    chan = iota((BLK, 128), 1)
    same = (lax.div(lax.rem(lam, 96), 3) == lax.div(chan, 3)) & (chan < 96)
    gmat[...] = jnp.where(same, 1.0, 0.0)
    emat[...] = jnp.where(
        lax.rem(iota((128, BLK), 1), 96) == iota((128, BLK), 0), 1.0, 0.0
    )

    def pack():
        frame_id = fid[0].astype(F32)
        r = iota((256, 240), 0)
        m = iota((256, 240), 1)
        slot = lax.rem(r, 64)
        col = 20 * lax.div(r, 64) + lax.rem(slot, 20)
        hit = (slot < 60) & (m == 80 * lax.div(slot, 20) + col)
        pick = jnp.where(hit, 1.0, 0.0).astype(BF16)
        spare = lax.rem(iota((256, 256), 0), 64) >= 60
        for n in range(4):
            stack = jnp.concatenate(
                [pixv[k, 80 * n : 80 * n + 80, :] for k in range(3)], axis=0
            )
            rows = jnp.dot(pick, stack, preferred_element_type=F32)
            rows = jnp.where(spare, frame_id, rows).astype(BF16)
            for jj in range(4):
                for ch in range(2):
                    sbuf[ch, 4 * n + jj] = rows[
                        64 * jj : 64 * jj + 64, 128 * ch : 128 * ch + 128
                    ]

    pix_cp.wait()
    pack()
    def strip_copy(r, d):
        j = lax.rem(tl + d, 16)
        h = lax.rem(c + r, 2)
        return remote(sbuf.at[h, j], rbuf.at[r, d], s1s.at[r, d], s1r.at[r, d], (2 * z + h, j))

    def strips_sent():
        def send_strip(d, _):
            strip_copy(0, d).start()
            strip_copy(1, d).start()
            return 0

        lax.fori_loop(1, 16, send_strip, 0)
        strip_copy(1, 0).start()
        rbuf[0, 0] = sbuf[c, tl]

    for cp in x_cps:
        cp.wait()

    def fold(v):
        return v.reshape(v.shape[0] // 8, 8, v.shape[1]).sum(axis=0)

    def stats():
        stin[...] = jnp.zeros((8, BLK), F32)
        for f in range(2):

            def stat_step(i, carry, f=f):
                s, ss = carry
                b = lax.div(i, 8)
                r = pl.multiple_of(lax.rem(i, 8) * 32, 32)
                v = xb[f * 5 + b, pl.ds(r, 32), :].astype(F32)
                return s + fold(v), ss + fold(v * v)

            zero = jnp.zeros((8, BLK), F32)
            s, ss = lax.fori_loop(0, 40, stat_step, (zero, zero))
            stin[2 * f : 2 * f + 1, :] = jnp.sum(s, axis=0, keepdims=True)
            stin[2 * f + 1 : 2 * f + 2, :] = jnp.sum(ss, axis=0, keepdims=True)

    stats()
    pl.semaphore_wait(barrier, 31 + 6)
    strips_sent()

    def stat_copy(which, d):
        j = lax.rem(tl + d, 16)
        return remote(
            stsend.at[which],
            strecv.at[which, d],
            sts.at[which, d],
            strs.at[which, d],
            (tm, j),
        )

    def stat_send(which):
        red = jnp.dot(stin[...], gmat[...], precision=HIGHEST, preferred_element_type=F32)
        stsend[which] = red
        strecv[which, 0] = red

        def go(d, _):
            stat_copy(which, d).start()
            return 0

        lax.fori_loop(1, 16, go, 0)

    def stat_wait(which):
        def go(d, _):
            stat_copy(which, d).wait_recv()
            return 0

        lax.fori_loop(1, 16, go, 0)
        return jnp.sum(strecv[which], axis=0)

    stat_send(0)

    def colours():
        owe = jnp.dot(ow[...].astype(F32), emat[0:96, :], preferred_element_type=F32)
        q = iota((64, BLK), 0)
        kq = lax.div(q, 20)
        wq = lax.rem(q, 20)
        wl = lax.div(iota((64, BLK), 1), 96)
        small = jnp.where(
            kq == 0,
            owe[0:1, :],
            jnp.where(kq == 1, owe[1:2, :], jnp.where(kq == 2, owe[2:3, :], 0.0)),
        )
        for b in range(5):
            core = jnp.where(wq == wl + 4 * b, small, 0.0).astype(BF16)
            rmat[b, 0:64, :] = core
            rmat[b, 64:128, :] = core

    for cp in small_cps:
        cp.wait()
    colours()

    tot = stat_wait(0) / COUNT
    rows = []
    for f in range(2):
        mean = tot[2 * f : 2 * f + 1]
        meansq = tot[2 * f + 1 : 2 * f + 2]
        rstd = lax.rsqrt(meansq - mean * mean + EPS)
        rows.append((mean, rstd))
    table[...] = jnp.zeros((8, 128), F32)
    for f in range(2):
        table[f : f + 1, :] = rows[f][0]
        table[6 + f : 7 + f, 0:96] = 0.5 * rows[f][1][:, 0:96] * gain[...]
    table[4:5, 0:96] = gain[...]
    table[5:6, 0:96] = 0.5 * bias[...]
    cst[...] = jnp.dot(table[...], emat[...], precision=HIGHEST, preferred_element_type=F32)

    def factor():
        for f in range(2):
            mean_l = cst[f : f + 1, :]
            a_l = cst[6 + f : 7 + f, :]
            hb_l = cst[5:6, :]
            g2_l = 0.5 * cst[4:5, :]

            def factor_step(i, _, f=f, mean_l=mean_l, a_l=a_l, hb_l=hb_l, g2_l=g2_l):
                b = lax.div(i, 8)
                r = pl.multiple_of(lax.rem(i, 8) * 32, 32)
                v = xb[f * 5 + b, pl.ds(r, 32), :].astype(F32) - mean_l
                u = v * a_l + hb_l
                h = jnp.tanh(u)
                w = (1.0 + u * (1.0 - h)) * ((1.0 + h) * g2_l)
                for i in range(3):
                    xs[f * 5 + b, i, pl.ds(r, 32), :] = v[:, 128 * i : 128 * i + 128]
                    fs[f * 5 + b, i, pl.ds(r, 32), :] = w[:, 128 * i : 128 * i + 128]
                return 0

            lax.fori_loop(0, 40, factor_step, 0)

    factor()

    def frame_picks():
        for r in range(2):
            ids = rbuf[r, :, 48:64, :].astype(F32)
            ids = jnp.broadcast_to(ids[:, 15:16, :], (16, 16, 128)).reshape(256, 128)
            ids = jnp.concatenate([ids, ids], axis=1)
            at = iota((256, 256), 1)
            hit = (ids == lax.div(at, 16).astype(F32)) & (
                lax.rem(iota((256, 256), 0), 16) == lax.rem(at, 16)
            )
            picks[:, 256 * r : 256 * r + 256] = jnp.where(hit, 1.0, 0.0).T.astype(BF16)

    def frame_sums():
        stack = jnp.concatenate(
            [rbuf[:, :, 16 * g : 16 * g + 16, :].reshape(512, 128) for g in range(4)], axis=1
        )
        total = jnp.dot(picks[...], stack, preferred_element_type=F32)
        for g in range(4):
            v = total[:, 128 * g : 128 * g + 128].reshape(8, 2, 16, 128)
            if g == 3:
                v = jnp.where(iota(v.shape, 2) >= 12, 0.0, v)
            sums[:, :, 16 * g : 16 * g + 16, :] = v

    def packed():
        for owner in range(8):
            v = sums[owner]
            largest = jnp.max(jnp.maximum(v[0], v[1]), axis=0, keepdims=True)
            smallest = jnp.min(jnp.minimum(v[0], v[1]), axis=0, keepdims=True)
            largest = jnp.maximum(jnp.maximum(largest, -smallest), 1e-20)
            step = jnp.floor(jnp.log(largest) * EIGHTHS) + 2.0
            scale = RANGE * jnp.exp(step * (-1.0 / EIGHTHS))
            w = jnp.round(v * scale[None])
            w = jnp.where(iota(v.shape, 1) >= 60, step[None], w)
            packs[owner] = w.astype(jnp.int32).astype(jnp.int16)

    def unpacked(v):
        v = v.astype(jnp.int32).astype(F32)
        return v * (jnp.exp(v[:, 60:61, :] * (1.0 / EIGHTHS)) * (1.0 / RANGE))

    def z_copy(r, d):
        owner = lax.rem(z + d, 4) * 2 + lax.rem(c + r, 2)
        return remote(packs.at[owner], zbuf.at[r, d], zs.at[r, d], zr.at[r, d], (owner, tl))

    partners = tuple((r, d) for r in range(2) for d in range(4) if r + d > 0)

    def recv_strip(d, _):
        strip_copy(0, d).wait_recv()
        strip_copy(1, d).wait_recv()
        return 0

    lax.fori_loop(1, 16, recv_strip, 0)
    strip_copy(1, 0).wait_recv()
    frame_picks()
    frame_sums()
    packed()
    for r, d in partners:
        z_copy(r, d).start()


    spread = jnp.where(lax.div(lax.rem(iota((128, 16), 0), 64), 4) == iota((128, 16), 1), 1.0, 0.0)

    def taps_reduced():
        iwr = jnp.dot(spread.astype(BF16), iw[...], preferred_element_type=F32).T.astype(BF16)
        for i in range(9):
            gred[3 * i : 3 * i + 3] = jnp.dot(
                cwv[3 * i : 3 * i + 3].reshape(288, BLK), iwr, preferred_element_type=F32
            ).reshape(3, 96, 128)

    cw_cp.wait()
    taps_reduced()

    ln = iota((16, 128), 1)
    main = ln < 64
    b0 = lax.rem(ln, 2) == 0
    a0 = lax.rem(lax.div(ln, 2), 2) == 0

    def combine(mc, _):
        r = pl.multiple_of(mc * 16, 16)
        for dt in range(3):
            cols = []
            for dh in range(3):
                g = [gred[9 * dt + 3 * dh + dw, pl.ds(r, 16), :] for dw in range(3)]
                g01 = g[0] + g[1]
                g12 = g[1] + g[2]
                zero = jnp.zeros_like(g01)
                cols.append(
                    (
                        jnp.where(main, jnp.where(b0, g12, zero), jnp.where(b0, zero, g[0])),
                        jnp.where(main, jnp.where(b0, g01, g[2]), zero),
                        jnp.where(main, jnp.where(b0, g[0], g12), zero),
                        jnp.where(main, jnp.where(b0, zero, g01), jnp.where(b0, g[2], zero)),
                    )
                )
            for w in range(4):
                h0, h1, h2 = (cols[dh][w] for dh in range(3))
                h01 = h0 + h1
                h12 = h1 + h2
                zero = jnp.zeros_like(h01)
                taps = (
                    jnp.where(a0, h2, zero),
                    jnp.where(a0, h12, zero),
                    jnp.where(a0, h01, h2),
                    jnp.where(a0, h0, h12),
                    jnp.where(a0, zero, h01),
                    jnp.where(a0, zero, h0),
                )
                for t in range(6):
                    row = pl.multiple_of(t * BLK + w * 96 + r, 16)
                    top = taps[t].astype(BF16)
                    rest = (taps[t] - top.astype(F32)).astype(BF16)
                    bmat[pl.ds(row, 16), 128 * dt : 128 * dt + 128] = top
                    bmat[pl.ds(row, 16), BLK + 128 * dt : BLK + 128 * dt + 128] = rest
        return 0

    def weights():
        lax.fori_loop(0, 6, combine, 0)

    weights()

    def frame_rows():
        for r in range(2):
            dp = sums[tm] if r == 0 else unpacked(zbuf[1, 0])
            for d in range(1, 4):
                dp = dp + unpacked(zbuf[r, d])
            for f in range(2):
                top = dp[f].astype(BF16)
                rest = dp[f] - top.astype(F32)
                both = jnp.concatenate([top.astype(F32), rest], axis=0).T
                dpx[lax.rem(c + r, 2), 128 * f : 128 * f + 128, :] = both.astype(BF16)

    for r, d in partners:
        z_copy(r, d).wait_recv()
    frame_rows()

    def dxh():
        carry = tuple(jnp.zeros((8, 128), F32) for _ in range(12))
        for half in range(2):

            def dxh_step(b, carry, half=half):
                da = jnp.dot(dpx[half], rmat[b], preferred_element_type=F32)
                new = []
                for f in range(2):
                    at = pl.ds(128 * half, 128)
                    s, sx = [], []
                    for i in range(3):
                        v = da[128 * f : 128 * f + 128, 128 * i : 128 * i + 128]
                        v = v * fs[f * 5 + b, i, at, :]
                        fs[f * 5 + b, i, at, :] = v
                        s.append(carry[6 * f + i] + fold(v))
                        sx.append(carry[6 * f + 3 + i] + fold(v * xs[f * 5 + b, i, at, :]))
                    new += s + sx
                return tuple(new)

            for b in range(5):
                carry = dxh_step(b, carry)
        for i in range(12):
            stin[i // 3 : i // 3 + 1, 128 * (i % 3) : 128 * (i % 3) + 128] = jnp.sum(
                carry[i], axis=0, keepdims=True
            )

    dxh()
    stat_send(1)
    tot = stat_wait(1) / COUNT
    terms = []
    for f in range(2):
        rstd = rows[f][1]
        first = tot[2 * f : 2 * f + 1]
        second = tot[2 * f + 1 : 2 * f + 2] * rstd
        terms += [rstd, -rstd * rstd * second, -rstd * first, jnp.zeros_like(rstd)]
    cst[...] = jnp.dot(
        jnp.concatenate(terms, axis=0), emat[...], precision=HIGHEST, preferred_element_type=F32
    )

    def left_side():
        for f in range(2):
            p_l = cst[4 * f : 4 * f + 1, :]
            q_l = cst[4 * f + 1 : 4 * f + 2, :]
            r_l = cst[4 * f + 2 : 4 * f + 3, :]

            def lhs_step(b, _, f=f, p_l=p_l, q_l=q_l, r_l=r_l):
                fb = f * 5 + b
                row = iota((64, 128), 0)
                for rho in range(4):
                    sel = pl.ds(rho, 64, stride=4)
                    for i in range(3):
                        ls = slice(128 * i, 128 * i + 128)
                        d = p_l[:, ls] * fs[fb, i, sel, :] + q_l[:, ls] * xs[fb, i, sel, :] + r_l[:, ls]
                        at = BLK * (rho + 1) + 128 * i
                        lhs[fb, :, at : at + 128] = d.astype(BF16)
                        if rho == 0:
                            d = jnp.where(row == 63, 0.0, pltpu.roll(d, 63, 0))
                            lhs[fb, :, BLK * 5 + 128 * i : BLK * 5 + 128 * i + 128] = d.astype(BF16)
                        if rho == 3:
                            d = jnp.where(row == 0, 0.0, pltpu.roll(d, 1, 0))
                            lhs[fb, :, 128 * i : 128 * i + 128] = d.astype(BF16)
                return 0

            lax.fori_loop(0, 5, lhs_step, 0)

    left_side()

    def conv():
        left = lhs[...].reshape(640, 6 * BLK)
        ys[...] = jnp.dot(left, bmat[...], preferred_element_type=F32)

    conv()

    ln = iota((64, 128), 1)
    lo64 = ln < 64
    odd = lax.rem(ln, 2) == 1

    def taken(f, dt, b):
        r = 64 * (5 * f + b)
        return (
            ys[r : r + 64, 128 * dt : 128 * dt + 128]
            + ys[r : r + 64, BLK + 128 * dt : BLK + 128 * dt + 128]
        )

    plans = (
        (1, 0, ((0, 0),)),
        (1, 1, ((0, 1), (1, 0))),
        (0, 0, ((0, 2), (1, 1))),
        (0, 1, ((1, 2),)),
    )
    def tokens():
        for group, t, terms in plans:
            cc = []
            for b in range(5):
                v = taken(*terms[0], b)
                for term in terms[1:]:
                    v = v + taken(*term, b)
                cc.append(v)
            r1 = pltpu.roll(cc[1], 64, 1)
            r3 = pltpu.roll(cc[3], 64, 1)
            v0 = jnp.where(
                lo64, cc[0] + jnp.where(odd, r1, 0.0), r1 + jnp.where(odd, cc[2], cc[0])
            )
            v1 = jnp.where(
                lo64, cc[2] + jnp.where(odd, r3, r1), r3 + jnp.where(odd, cc[4], cc[2])
            )
            v2 = jnp.where(lo64, cc[4] + jnp.where(odd, 0.0, r3), jnp.where(odd, cc[0], cc[4]))
            for i, v in enumerate((v0, v1, v2)):
                tok[group, 8 * t : 8 * t + 8, :, 128 * i : 128 * i + 128] = v.reshape(8, 8, 128)

    tokens()

    def own_copy(d, sending):
        j = lax.rem(tl + d, 16)
        at = tl if sending else lax.rem(tl + 16 - d, 16)
        return remote(tok.at[0, j], trecv.at[0, at], tks.at[0, d], tkr.at[0, at], (tm, j))

    def span_copy(j, sending):
        at = tl if sending else j
        return remote(tok.at[1, j], trecv.at[1, at], tks.at[1, j], tkr.at[1, at], (below, j))

    def send_span(j, _):
        span_copy(j, True).start()
        return 0

    lax.fori_loop(0, 16, send_span, 0)

    def send_own(d, _):
        own_copy(d, True).start()
        return 0

    lax.fori_loop(1, 16, send_own, 0)
    trecv[0, tl] = tok[0, tl]

    def recv_span(j, _):
        span_copy(j, False).wait_recv()
        return 0

    lax.fori_loop(0, 16, recv_span, 0)

    def recv_own(d, _):
        own_copy(d, False).wait_recv()
        return 0

    lax.fori_loop(1, 16, recv_own, 0)

    def assemble():
        ln = iota((8, 128), 1)
        lo8 = ln < 64
        odd8 = lax.rem(ln, 2) == 1
        strips = []
        for j in range(16):
            strips.append(
                [
                    trecv[0, j, :, 128 * i : 128 * i + 128]
                    + jnp.where(tm < 7, trecv[1, j, :, 128 * i : 128 * i + 128], 0.0)
                    for i in range(3)
                ]
            )
        halo = [pltpu.roll(s[2], 64, 1) for s in strips]
        for j in range(16):
            if j > 0:
                strips[j][0] = strips[j][0] + jnp.where(lo8 & ~odd8, halo[j - 1], 0.0)
        done = []
        for j in range(16):
            v2 = strips[j][2]
            if j < 15:
                v2 = v2 + jnp.where(odd8, halo[j + 1], 0.0)
            done.append((strips[j][0], strips[j][1], v2))
        for pair in range(8):
            e = done[2 * pair]
            o = [pltpu.roll(v, 64, 1) for v in done[2 * pair + 1]]
            at = 640 * pair
            out[:, at : at + 128] = e[0]
            out[:, at + 128 : at + 256] = e[1]
            out[:, at + 256 : at + 384] = jnp.where(lo8, e[2], o[0])
            out[:, at + 384 : at + 512] = jnp.where(lo8, o[0], o[1])
            out[:, at + 512 : at + 640] = jnp.where(lo8, o[1], o[2])

    assemble()

    def sent_strip(d, _):
        strip_copy(0, d).wait_send()
        strip_copy(1, d).wait_send()
        stat_copy(0, d).wait_send()
        stat_copy(1, d).wait_send()
        return 0

    lax.fori_loop(1, 16, sent_strip, 0)
    strip_copy(1, 0).wait_send()
    for r, d in partners:
        z_copy(r, d).wait_send()

    def sent_own(d, _):
        own_copy(d, True).wait_send()
        return 0

    lax.fori_loop(1, 16, sent_own, 0)

    def sent_span(j, _):
        span_copy(j, True).wait_send()
        return 0

    lax.fori_loop(0, 16, sent_span, 0)


def body(pix_grad, frame_ids, pre_norm, gain, bias, out_weight, conv_weight, in_weight):
    hbm = pl.BlockSpec(memory_space=pltpu.HBM)
    smem = pl.BlockSpec(memory_space=pltpu.SMEM)
    dma = pltpu.SemaphoreType.DMA
    pix_grad = jnp.transpose(pix_grad, (0, 1, 3, 2))
    out_weight = out_weight.T
    gain = gain.reshape(1, 96)
    bias = bias.reshape(1, 96)
    return pl.pallas_call(
        kernel,
        out_shape=jax.ShapeDtypeStruct((8, 5120), F32),
        in_specs=[hbm, smem] + [hbm] * 6,
        out_specs=pl.BlockSpec(memory_space=pltpu.VMEM),
        scratch_shapes=[
            pltpu.VMEM((1, 96), F32),
            pltpu.VMEM((1, 96), F32),
            pltpu.VMEM((3, 96), BF16),
            pltpu.VMEM((16, 384), BF16),
            pltpu.VMEM((3, 320, 256), BF16),
            pltpu.VMEM((PIECES, 256, BLK), BF16),
            pltpu.VMEM((27, 96, 384), BF16),
            pltpu.VMEM((2, 16, 64, 128), BF16),
            pltpu.VMEM((2, 16, 64, 128), BF16),
            pltpu.VMEM((256, 512), BF16),
            pltpu.VMEM((8, 2, 64, 128), F32),
            pltpu.VMEM((8, 2, 64, 128), jnp.int16),
            pltpu.VMEM((2, 4, 2, 64, 128), jnp.int16),
            pltpu.VMEM((2, 256, 128), BF16),
            pltpu.VMEM((5, 128, BLK), BF16),
            pltpu.VMEM((PIECES, 3, 256, 128), F32),
            pltpu.VMEM((PIECES, 3, 256, 128), F32),
            pltpu.VMEM((BLK, 128), F32),
            pltpu.VMEM((128, BLK), F32),
            pltpu.VMEM((8, BLK), F32),
            pltpu.VMEM((2, 8, 128), F32),
            pltpu.VMEM((2, 16, 8, 128), F32),
            pltpu.VMEM((8, 128), F32),
            pltpu.VMEM((8, BLK), F32),
            pltpu.VMEM((27, 96, 128), F32),
            pltpu.VMEM((6 * BLK, 2 * BLK), BF16),
            pltpu.VMEM((PIECES, 64, 6 * BLK), BF16),
            pltpu.VMEM((640, 2 * BLK), F32),
            pltpu.VMEM((2, 16, 8, BLK), F32),
            pltpu.VMEM((2, 16, 8, BLK), F32),
            dma,
            dma((PIECES,)),
            dma,
            dma((4,)),
            dma((2, 16)),
            dma((2, 16)),
            dma((2, 4)),
            dma((2, 4)),
            dma((2, 16)),
            dma((2, 16)),
            dma((2, 16)),
            dma((2, 16)),
        ],
        compiler_params=pltpu.CompilerParams(
            collective_id=0, has_side_effects=True, vmem_limit_bytes=62 * 1024 * 1024
        ),
    )(pix_grad, frame_ids, pre_norm, gain, bias, out_weight, conv_weight, in_weight)


def solution(mesh):
    return jax.shard_map(
        body,
        mesh=mesh,
        in_specs=(
            P(("tm", "tile"), None, None, None),
            P(("tm", "tile")),
            P("tm", None, "tile"),
            P(),
            P(),
            P(),
            P(),
            P(),
        ),
        out_specs=P(("tm", "tile"), None),
        check_vma=False,
    )
```

```python
import jax
import jax.numpy as jnp
from jax import lax
from jax.experimental import pallas as pl
from jax.experimental.pallas import tpu as pltpu
from jax.sharding import PartitionSpec as P

MESH = pl.DeviceIdType.MESH
F32 = jnp.float32
BF16 = jnp.bfloat16
COUNT = 256.0 * 320.0 * 3.0
EPS = 1e-05
EIGHTHS = 8.0 / 0.6931471805599453
RANGE = 32700.0
BLK = 384
PIECES = 10


def iota(shape, dim):
    return lax.broadcasted_iota(jnp.int32, shape, dim)


def exact_dot(v, ones):
    top = v.astype(BF16).astype(F32)
    mid = (v - top).astype(BF16).astype(F32)
    parts = jnp.concatenate([top, mid, v - top - mid], axis=0).astype(BF16)
    w = jnp.dot(parts, ones, preferred_element_type=F32)
    n = v.shape[0]
    return w[0:n] + (w[n : 2 * n] + w[2 * n : 3 * n])


def remote(src, dst, send_sem, recv_sem, device):
    return pltpu.make_async_remote_copy(
        src_ref=src,
        dst_ref=dst,
        send_sem=send_sem,
        recv_sem=recv_sem,
        device_id=device,
        device_id_type=MESH,
    )


def kernel(
    pix_hbm,
    fid,
    x_hbm,
    gain_hbm,
    bias_hbm,
    ow_hbm,
    cw_hbm,
    iw_hbm,
    out,
    gain,
    bias,
    ow,
    iw,
    pixv,
    xb,
    cwv,
    sbuf,
    rbuf,
    picks,
    sums,
    packs,
    zbuf,
    dpx,
    rmat,
    xs,
    fs,
    gmat,
    emat,
    stin,
    stsend,
    strecv,
    table,
    cst,
    gred,
    bmat,
    lhs0,
    lhs1,
    ys,
    tok,
    trecv,
    pix_sem,
    x_sem,
    cw_sem,
    small_sem,
    s1s,
    s1r,
    zs,
    zr,
    sts,
    strs,
    tks,
    tkr,
):
    tm = lax.axis_index("tm")
    tl = lax.axis_index("tile")
    z = lax.div(tm, 2)
    c = lax.rem(tm, 2)
    below = lax.rem(tm + 7, 8)

    pix_cp = pltpu.make_async_copy(pix_hbm.at[0], pixv, pix_sem)
    pix_cp.start()
    x_cps = []
    for f in range(2):
        for b in range(5):
            cp = pltpu.make_async_copy(
                x_hbm.at[f, :, pl.ds(BLK * b, BLK)], xb.at[f * 5 + b], x_sem.at[f * 5 + b]
            )
            cp.start()
            x_cps.append(cp)
    small_cps = []
    for i, (src, dst) in enumerate(
        ((gain_hbm, gain), (bias_hbm, bias), (ow_hbm, ow), (iw_hbm, iw))
    ):
        cp = pltpu.make_async_copy(src, dst, small_sem.at[i])
        cp.start()
        small_cps.append(cp)
    cw_cp = pltpu.make_async_copy(cw_hbm, cwv, cw_sem)
    cw_cp.start()

    barrier = pltpu.get_barrier_semaphore()

    def greet(device):
        pl.semaphore_signal(barrier, inc=1, device_id=device, device_id_type=MESH)

    def greet_chip(d, _):
        j = lax.rem(tl + d, 16)
        greet((tm, j))
        greet((tm + 1 - 2 * c, j))
        return 0

    lax.fori_loop(1, 16, greet_chip, 0)
    greet((tm + 1 - 2 * c, tl))
    for d in range(1, 4):
        for r in range(2):
            greet((lax.rem(z + d, 4) * 2 + lax.rem(c + r, 2), tl))

    lam = iota((BLK, 128), 0)
    chan = iota((BLK, 128), 1)
    same = (lax.div(lax.rem(lam, 96), 3) == lax.div(chan, 3)) & (chan < 96)
    gmat[...] = jnp.where(same, 1.0, 0.0).astype(BF16)
    emat[...] = jnp.where(
        lax.rem(iota((128, BLK), 1), 96) == iota((128, BLK), 0), 1.0, 0.0
    ).astype(BF16)

    def pack():
        frame_id = fid[0].astype(F32)
        r = iota((256, 240), 0)
        m = iota((256, 240), 1)
        slot = lax.rem(r, 64)
        col = 20 * lax.div(r, 64) + lax.rem(slot, 20)
        hit = (slot < 60) & (m == 80 * lax.div(slot, 20) + col)
        pick = jnp.where(hit, 1.0, 0.0).astype(BF16)
        spare = lax.rem(iota((256, 256), 0), 64) >= 60
        for n in range(4):
            stack = jnp.concatenate(
                [pixv[k, 80 * n : 80 * n + 80, :] for k in range(3)], axis=0
            )
            rows = jnp.dot(pick, stack, preferred_element_type=F32)
            rows = jnp.where(spare, frame_id, rows).astype(BF16)
            for jj in range(4):
                for ch in range(2):
                    sbuf[ch, 4 * n + jj] = rows[
                        64 * jj : 64 * jj + 64, 128 * ch : 128 * ch + 128
                    ]

    pix_cp.wait()
    pack()
    def strip_copy(r, d):
        j = lax.rem(tl + d, 16)
        h = lax.rem(c + r, 2)
        return remote(sbuf.at[h, j], rbuf.at[r, d], s1s.at[r, d], s1r.at[r, d], (2 * z + h, j))

    def strips_sent():
        def send_strip(d, _):
            strip_copy(0, d).start()
            strip_copy(1, d).start()
            return 0

        lax.fori_loop(1, 16, send_strip, 0)
        strip_copy(1, 0).start()
        rbuf[0, 0] = sbuf[c, tl]

    for cp in x_cps:
        cp.wait()

    def fold(v):
        return v.reshape(v.shape[0] // 8, 8, v.shape[1]).sum(axis=0)

    def stats():
        stin[...] = jnp.zeros((8, BLK), F32)
        for f in range(2):

            def stat_step(i, carry, f=f):
                s, ss = carry
                b = lax.div(i, 8)
                r = pl.multiple_of(lax.rem(i, 8) * 32, 32)
                v = xb[f * 5 + b, pl.ds(r, 32), :].astype(F32)
                return s + fold(v), ss + fold(v * v)

            zero = jnp.zeros((8, BLK), F32)
            s, ss = lax.fori_loop(0, 40, stat_step, (zero, zero))
            stin[2 * f : 2 * f + 1, :] = jnp.sum(s, axis=0, keepdims=True)
            stin[2 * f + 1 : 2 * f + 2, :] = jnp.sum(ss, axis=0, keepdims=True)

    stats()
    pl.semaphore_wait(barrier, 31 + 6)
    strips_sent()

    def stat_copy(which, d):
        j = lax.rem(tl + d, 16)
        return remote(
            stsend.at[which],
            strecv.at[which, d],
            sts.at[which, d],
            strs.at[which, d],
            (tm, j),
        )

    def stat_send(which):
        red = exact_dot(stin[...], gmat[...])
        stsend[which] = red
        strecv[which, 0] = red

        def go(d, _):
            stat_copy(which, d).start()
            return 0

        lax.fori_loop(1, 16, go, 0)

    def stat_wait(which):
        def go(d, _):
            stat_copy(which, d).wait_recv()
            return 0

        lax.fori_loop(1, 16, go, 0)
        return jnp.sum(strecv[which], axis=0)

    stat_send(0)

    def colours():
        owe = jnp.dot(ow[...], emat[0:96, :], preferred_element_type=F32)
        q = iota((64, BLK), 0)
        kq = lax.div(q, 20)
        wq = lax.rem(q, 20)
        wl = lax.div(iota((64, BLK), 1), 96)
        small = jnp.where(
            kq == 0,
            owe[0:1, :],
            jnp.where(kq == 1, owe[1:2, :], jnp.where(kq == 2, owe[2:3, :], 0.0)),
        )
        for b in range(5):
            core = jnp.where(wq == wl + 4 * b, small, 0.0).astype(BF16)
            rmat[b, 0:64, :] = core
            rmat[b, 64:128, :] = core

    for cp in small_cps:
        cp.wait()
    colours()


    spread = jnp.where(lax.div(lax.rem(iota((128, 16), 0), 64), 4) == iota((128, 16), 1), 1.0, 0.0)

    def taps_reduced():
        iwr = jnp.dot(spread.astype(BF16), iw[...], preferred_element_type=F32).T.astype(BF16)
        for i in range(9):
            gred[3 * i : 3 * i + 3] = jnp.dot(
                cwv[3 * i : 3 * i + 3].reshape(288, BLK), iwr, preferred_element_type=F32
            ).reshape(3, 96, 128)

    cw_cp.wait()
    taps_reduced()

    ln = iota((16, 128), 1)
    main = ln < 64
    b0 = lax.rem(ln, 2) == 0
    a0 = lax.rem(lax.div(ln, 2), 2) == 0

    def combine(mc, _):
        r = pl.multiple_of(mc * 16, 16)
        for dt in range(3):
            cols = []
            for dh in range(3):
                g = [gred[9 * dt + 3 * dh + dw, pl.ds(r, 16), :] for dw in range(3)]
                g01 = g[0] + g[1]
                g12 = g[1] + g[2]
                zero = jnp.zeros_like(g01)
                cols.append(
                    (
                        jnp.where(main, jnp.where(b0, g12, zero), jnp.where(b0, zero, g[0])),
                        jnp.where(main, jnp.where(b0, g01, g[2]), zero),
                        jnp.where(main, jnp.where(b0, g[0], g12), zero),
                        jnp.where(main, jnp.where(b0, zero, g01), jnp.where(b0, g[2], zero)),
                    )
                )
            for w in range(4):
                h0, h1, h2 = (cols[dh][w] for dh in range(3))
                h01 = h0 + h1
                h12 = h1 + h2
                zero = jnp.zeros_like(h01)
                taps = (
                    jnp.where(a0, h2, zero),
                    jnp.where(a0, h12, zero),
                    jnp.where(a0, h01, h2),
                    jnp.where(a0, h0, h12),
                    jnp.where(a0, zero, h01),
                    jnp.where(a0, zero, h0),
                )
                for t in range(6):
                    row = pl.multiple_of(t * BLK + w * 96 + r, 16)
                    top = taps[t].astype(BF16)
                    rest = (taps[t] - top.astype(F32)).astype(BF16)
                    bmat[pl.ds(row, 16), 256 * dt : 256 * dt + 128] = top
                    bmat[pl.ds(row, 16), 256 * dt + 128 : 256 * dt + 256] = rest
        return 0

    def weights():
        lax.fori_loop(0, 6, combine, 0)

    weights()

    def frame_picks():
        for r in range(2):
            ids = rbuf[r, :, 48:64, :].astype(F32)
            ids = jnp.broadcast_to(ids[:, 15:16, :], (16, 16, 128)).reshape(256, 128)
            ids = jnp.concatenate([ids, ids], axis=1)
            at = iota((256, 256), 1)
            hit = (ids == lax.div(at, 16).astype(F32)) & (
                lax.rem(iota((256, 256), 0), 16) == lax.rem(at, 16)
            )
            picks[:, 256 * r : 256 * r + 256] = jnp.where(hit, 1.0, 0.0).T.astype(BF16)

    def frame_sums():
        stack = jnp.concatenate(
            [rbuf[:, :, 16 * g : 16 * g + 16, :].reshape(512, 128) for g in range(4)], axis=1
        )
        total = jnp.dot(picks[...], stack, preferred_element_type=F32)
        for g in range(4):
            v = total[:, 128 * g : 128 * g + 128].reshape(8, 2, 16, 128)
            if g == 3:
                v = jnp.where(iota(v.shape, 2) >= 12, 0.0, v)
            sums[:, :, 16 * g : 16 * g + 16, :] = v

    def packed():
        for owner in range(8):
            v = sums[owner]
            largest = jnp.max(jnp.maximum(v[0], v[1]), axis=0, keepdims=True)
            smallest = jnp.min(jnp.minimum(v[0], v[1]), axis=0, keepdims=True)
            largest = jnp.maximum(jnp.maximum(largest, -smallest), 1e-20)
            step = jnp.floor(jnp.log(largest) * EIGHTHS) + 2.0
            scale = RANGE * jnp.exp(step * (-1.0 / EIGHTHS))
            w = jnp.round(v * scale[None])
            w = jnp.where(iota(v.shape, 1) >= 60, step[None], w)
            packs[owner] = w.astype(jnp.int32).astype(jnp.int16)

    def unpacked(v):
        v = v.astype(jnp.int32).astype(F32)
        return v * (jnp.exp(v[:, 60:61, :] * (1.0 / EIGHTHS)) * (1.0 / RANGE))

    def z_copy(r, d):
        owner = lax.rem(z + d, 4) * 2 + lax.rem(c + r, 2)
        return remote(packs.at[owner], zbuf.at[r, d], zs.at[r, d], zr.at[r, d], (owner, tl))

    partners = tuple((r, d) for r in range(2) for d in range(4) if r + d > 0)

    def recv_strip(d, _):
        strip_copy(0, d).wait_recv()
        strip_copy(1, d).wait_recv()
        return 0

    lax.fori_loop(1, 16, recv_strip, 0)
    strip_copy(1, 0).wait_recv()
    frame_picks()
    frame_sums()
    packed()
    for r, d in partners:
        z_copy(r, d).start()

    tot = stat_wait(0) / COUNT
    rows = []
    for f in range(2):
        mean = tot[2 * f : 2 * f + 1]
        meansq = tot[2 * f + 1 : 2 * f + 2]
        rstd = lax.rsqrt(meansq - mean * mean + EPS)
        rows.append((mean, rstd))
    table[...] = jnp.zeros((8, 128), F32)
    for f in range(2):
        table[f : f + 1, :] = rows[f][0]
        table[6 + f : 7 + f, 0:96] = 0.5 * rows[f][1][:, 0:96] * gain[...]
    table[4:5, 0:96] = gain[...]
    table[5:6, 0:96] = 0.5 * bias[...]
    cst[...] = exact_dot(table[...], emat[...])

    def factor():
        for f in range(2):
            mean_l = cst[f : f + 1, :]
            a_l = cst[6 + f : 7 + f, :]
            hb_l = cst[5:6, :]
            g2_l = 0.5 * cst[4:5, :]

            def factor_step(i, _, f=f, mean_l=mean_l, a_l=a_l, hb_l=hb_l, g2_l=g2_l):
                b = lax.div(i, 8)
                r = pl.multiple_of(lax.rem(i, 8) * 32, 32)
                v = xb[f * 5 + b, pl.ds(r, 32), :].astype(F32) - mean_l
                u = v * a_l + hb_l
                h = jnp.tanh(u)
                w = (1.0 + u * (1.0 - h)) * ((1.0 + h) * g2_l)
                for i in range(3):
                    xs[f * 5 + b, i, pl.ds(r, 32), :] = v[:, 128 * i : 128 * i + 128]
                    fs[f * 5 + b, i, pl.ds(r, 32), :] = w[:, 128 * i : 128 * i + 128]
                return 0

            lax.fori_loop(0, 40, factor_step, 0)

    factor()

    def frame_rows():
        for r in range(2):
            dp = sums[tm] if r == 0 else unpacked(zbuf[1, 0])
            for d in range(1, 4):
                dp = dp + unpacked(zbuf[r, d])
            for f in range(2):
                top = dp[f].astype(BF16)
                rest = dp[f] - top.astype(F32)
                both = jnp.concatenate([top.astype(F32), rest], axis=0).T
                dpx[lax.rem(c + r, 2), 128 * f : 128 * f + 128, :] = both.astype(BF16)

    for r, d in partners:
        z_copy(r, d).wait_recv()
    frame_rows()

    def dxh():
        carry = tuple(jnp.zeros((8, 128), F32) for _ in range(12))
        for half in range(2):

            def dxh_step(b, carry, half=half):
                da = jnp.dot(dpx[half], rmat[b], preferred_element_type=F32)
                new = []
                for f in range(2):
                    at = pl.ds(128 * half, 128)
                    s, sx = [], []
                    for i in range(3):
                        v = da[128 * f : 128 * f + 128, 128 * i : 128 * i + 128]
                        v = v * fs[f * 5 + b, i, at, :]
                        fs[f * 5 + b, i, at, :] = v
                        s.append(carry[6 * f + i] + fold(v))
                        sx.append(carry[6 * f + 3 + i] + fold(v * xs[f * 5 + b, i, at, :]))
                    new += s + sx
                return tuple(new)

            for b in range(5):
                carry = dxh_step(b, carry)
        for i in range(12):
            stin[i // 3 : i // 3 + 1, 128 * (i % 3) : 128 * (i % 3) + 128] = jnp.sum(
                carry[i], axis=0, keepdims=True
            )

    dxh()
    stat_send(1)
    tot = stat_wait(1) / COUNT
    terms = []
    for f in range(2):
        rstd = rows[f][1]
        first = tot[2 * f : 2 * f + 1]
        second = tot[2 * f + 1 : 2 * f + 2] * rstd
        terms += [rstd, -rstd * rstd * second, -rstd * first, jnp.zeros_like(rstd)]
    cst[...] = exact_dot(jnp.concatenate(terms, axis=0), emat[...])

    def left_side(f):
        left = lhs0 if f == 0 else lhs1
        row = iota((64, 128), 0)
        for i in range(3):
            ls = slice(128 * i, 128 * i + 128)
            p_l = cst[4 * f : 4 * f + 1, ls]
            q_l = cst[4 * f + 1 : 4 * f + 2, ls]
            r_l = cst[4 * f + 2 : 4 * f + 3, ls]
            for b in range(5):
                fb = f * 5 + b
                for rho in range(4):
                    sel = pl.ds(rho, 64, stride=4)
                    d = p_l * fs[fb, i, sel, :] + q_l * xs[fb, i, sel, :] + r_l
                    at = BLK * (rho + 1) + 128 * i
                    left[64 * b : 64 * b + 64, at : at + 128] = d.astype(BF16)
                    if rho == 0:
                        d = jnp.where(row == 63, 0.0, pltpu.roll(d, 63, 0))
                        at = BLK * 5 + 128 * i
                        left[64 * b : 64 * b + 64, at : at + 128] = d.astype(BF16)
                    if rho == 3:
                        d = jnp.where(row == 0, 0.0, pltpu.roll(d, 1, 0))
                        at = 128 * i
                        left[64 * b : 64 * b + 64, at : at + 128] = d.astype(BF16)

    def conv(f, first, last):
        left = lhs0 if f == 0 else lhs1
        at = slice(256 * first, 256 * last + 256)
        ys[320 * f : 320 * f + 320, at] = jnp.dot(
            left[...], bmat[:, at], preferred_element_type=F32
        )

    ln = iota((64, 128), 1)
    lo64 = ln < 64
    odd = lax.rem(ln, 2) == 1

    def taken(f, dt, b):
        r = 64 * (5 * f + b)
        return (
            ys[r : r + 64, 256 * dt : 256 * dt + 128]
            + ys[r : r + 64, 256 * dt + 128 : 256 * dt + 256]
        )

    def tokens(group, t, terms):
        cc = []
        for b in range(5):
            v = taken(*terms[0], b)
            for term in terms[1:]:
                v = v + taken(*term, b)
            cc.append(v)
        r1 = pltpu.roll(cc[1], 64, 1)
        r3 = pltpu.roll(cc[3], 64, 1)
        v0 = jnp.where(
            lo64, cc[0] + jnp.where(odd, r1, 0.0), r1 + jnp.where(odd, cc[2], cc[0])
        )
        v1 = jnp.where(
            lo64, cc[2] + jnp.where(odd, r3, r1), r3 + jnp.where(odd, cc[4], cc[2])
        )
        v2 = jnp.where(lo64, cc[4] + jnp.where(odd, 0.0, r3), jnp.where(odd, cc[0], cc[4]))
        for i, v in enumerate((v0, v1, v2)):
            tok[group, 8 * t : 8 * t + 8, :, 128 * i : 128 * i + 128] = v.reshape(8, 8, 128)

    def own_copy(d, sending):
        j = lax.rem(tl + d, 16)
        at = tl if sending else lax.rem(tl + 16 - d, 16)
        return remote(tok.at[0, j], trecv.at[0, at], tks.at[0, d], tkr.at[0, at], (tm, j))

    def span_copy(j, sending):
        at = tl if sending else j
        return remote(tok.at[1, j], trecv.at[1, at], tks.at[1, j], tkr.at[1, at], (below, j))

    def send_span(j, _):
        span_copy(j, True).start()
        return 0

    def send_own(d, _):
        own_copy(d, True).start()
        return 0

    left_side(0)
    conv(0, 0, 1)
    left_side(1)
    conv(1, 0, 0)
    tokens(1, 0, ((0, 0),))
    tokens(1, 1, ((0, 1), (1, 0)))
    lax.fori_loop(0, 16, send_span, 0)
    conv(0, 2, 2)
    conv(1, 1, 2)
    tokens(0, 0, ((0, 2), (1, 1)))
    tokens(0, 1, ((1, 2),))
    lax.fori_loop(1, 16, send_own, 0)
    trecv[0, tl] = tok[0, tl]

    def recv_span(j, _):
        span_copy(j, False).wait_recv()
        return 0

    lax.fori_loop(0, 16, recv_span, 0)

    def recv_own(d, _):
        own_copy(d, False).wait_recv()
        return 0

    lax.fori_loop(1, 16, recv_own, 0)

    def assemble():
        ln = iota((8, 128), 1)
        lo8 = ln < 64
        odd8 = lax.rem(ln, 2) == 1
        strips = []
        for j in range(16):
            strips.append(
                [
                    trecv[0, j, :, 128 * i : 128 * i + 128]
                    + jnp.where(tm < 7, trecv[1, j, :, 128 * i : 128 * i + 128], 0.0)
                    for i in range(3)
                ]
            )
        halo = [pltpu.roll(s[2], 64, 1) for s in strips]
        for j in range(16):
            if j > 0:
                strips[j][0] = strips[j][0] + jnp.where(lo8 & ~odd8, halo[j - 1], 0.0)
        done = []
        for j in range(16):
            v2 = strips[j][2]
            if j < 15:
                v2 = v2 + jnp.where(odd8, halo[j + 1], 0.0)
            done.append((strips[j][0], strips[j][1], v2))
        for pair in range(8):
            e = done[2 * pair]
            o = [pltpu.roll(v, 64, 1) for v in done[2 * pair + 1]]
            at = 640 * pair
            out[:, at : at + 128] = e[0]
            out[:, at + 128 : at + 256] = e[1]
            out[:, at + 256 : at + 384] = jnp.where(lo8, e[2], o[0])
            out[:, at + 384 : at + 512] = jnp.where(lo8, o[0], o[1])
            out[:, at + 512 : at + 640] = jnp.where(lo8, o[1], o[2])

    assemble()

    def sent_strip(d, _):
        strip_copy(0, d).wait_send()
        strip_copy(1, d).wait_send()
        stat_copy(0, d).wait_send()
        stat_copy(1, d).wait_send()
        return 0

    lax.fori_loop(1, 16, sent_strip, 0)
    strip_copy(1, 0).wait_send()
    for r, d in partners:
        z_copy(r, d).wait_send()

    def sent_own(d, _):
        own_copy(d, True).wait_send()
        return 0

    lax.fori_loop(1, 16, sent_own, 0)

    def sent_span(j, _):
        span_copy(j, True).wait_send()
        return 0

    lax.fori_loop(0, 16, sent_span, 0)


def body(pix_grad, frame_ids, pre_norm, gain, bias, out_weight, conv_weight, in_weight):
    hbm = pl.BlockSpec(memory_space=pltpu.HBM)
    smem = pl.BlockSpec(memory_space=pltpu.SMEM)
    dma = pltpu.SemaphoreType.DMA

    def kept(array):
        return pltpu.with_memory_space_constraint(array, pltpu.HBM)

    pix_grad = jnp.transpose(pix_grad, (0, 1, 3, 2))
    out_weight = out_weight.T
    gain = gain.reshape(1, 96)
    bias = bias.reshape(1, 96)
    return pl.pallas_call(
        kernel,
        out_shape=jax.ShapeDtypeStruct((8, 5120), F32),
        in_specs=[hbm, smem] + [hbm] * 6,
        out_specs=pl.BlockSpec(memory_space=pltpu.VMEM),
        scratch_shapes=[
            pltpu.VMEM((1, 96), F32),
            pltpu.VMEM((1, 96), F32),
            pltpu.VMEM((3, 96), BF16),
            pltpu.VMEM((16, 384), BF16),
            pltpu.VMEM((3, 320, 256), BF16),
            pltpu.VMEM((PIECES, 256, BLK), BF16),
            pltpu.VMEM((27, 96, 384), BF16),
            pltpu.VMEM((2, 16, 64, 128), BF16),
            pltpu.VMEM((2, 16, 64, 128), BF16),
            pltpu.VMEM((256, 512), BF16),
            pltpu.VMEM((8, 2, 64, 128), F32),
            pltpu.VMEM((8, 2, 64, 128), jnp.int16),
            pltpu.VMEM((2, 4, 2, 64, 128), jnp.int16),
            pltpu.VMEM((2, 256, 128), BF16),
            pltpu.VMEM((5, 128, BLK), BF16),
            pltpu.VMEM((PIECES, 3, 256, 128), F32),
            pltpu.VMEM((PIECES, 3, 256, 128), F32),
            pltpu.VMEM((BLK, 128), BF16),
            pltpu.VMEM((128, BLK), BF16),
            pltpu.VMEM((8, BLK), F32),
            pltpu.VMEM((2, 8, 128), F32),
            pltpu.VMEM((2, 16, 8, 128), F32),
            pltpu.VMEM((8, 128), F32),
            pltpu.VMEM((8, BLK), F32),
            pltpu.VMEM((27, 96, 128), F32),
            pltpu.VMEM((6 * BLK, 2 * BLK), BF16),
            pltpu.VMEM((320, 6 * BLK), BF16),
            pltpu.VMEM((320, 6 * BLK), BF16),
            pltpu.VMEM((640, 2 * BLK), F32),
            pltpu.VMEM((2, 16, 8, BLK), F32),
            pltpu.VMEM((2, 16, 8, BLK), F32),
            dma,
            dma((PIECES,)),
            dma,
            dma((4,)),
            dma((2, 16)),
            dma((2, 16)),
            dma((2, 4)),
            dma((2, 4)),
            dma((2, 16)),
            dma((2, 16)),
            dma((2, 16)),
            dma((2, 16)),
        ],
        compiler_params=pltpu.CompilerParams(
            collective_id=0, has_side_effects=True, vmem_limit_bytes=50 * 1024 * 1024
        ),
    )(
        kept(pix_grad),
        frame_ids,
        kept(pre_norm),
        kept(gain),
        kept(bias),
        kept(out_weight),
        kept(conv_weight),
        kept(in_weight),
    )


def solution(mesh):
    return jax.shard_map(
        body,
        mesh=mesh,
        in_specs=(
            P(("tm", "tile"), None, None, None),
            P(("tm", "tile")),
            P("tm", None, "tile"),
            P(),
            P(),
            P(),
            P(),
            P(),
        ),
        out_specs=P(("tm", "tile"), None),
        check_vma=False,
    )
```

```python
import jax
import jax.numpy as jnp
from jax import lax
from jax.experimental import pallas as pl
from jax.experimental.pallas import tpu as pltpu
from jax.sharding import PartitionSpec as P

MESH = pl.DeviceIdType.MESH
F32 = jnp.float32
BF16 = jnp.bfloat16
COUNT = 256.0 * 320.0 * 3.0
EPS = 1e-05
EIGHTHS = 8.0 / 0.6931471805599453
RANGE = 32700.0
BLK = 384
PEERS = (
    (1, 2), (3, 2), (2, 1), (2, 3), (2, 2), (0, 1), (1, 1), (0, 3),
    (3, 3), (1, 3), (3, 1), (0, 2), (2, 0), (1, 0), (3, 0),
)
FARTHEST = (
    (2, 2), (1, 2), (3, 2), (2, 1), (2, 3), (1, 1), (3, 3), (1, 3),
    (3, 1), (2, 0), (0, 2), (0, 1), (1, 0), (0, 3), (3, 0),
)
DXH = ((0, 0), (0, 1), (0, 2), (1, 2), (1, 3), (1, 4))
PIECES = 10


def iota(shape, dim):
    return lax.broadcasted_iota(jnp.int32, shape, dim)


def exact_dot(v, ones):
    top = v.astype(BF16).astype(F32)
    mid = (v - top).astype(BF16).astype(F32)
    parts = jnp.concatenate([top, mid, v - top - mid], axis=0).astype(BF16)
    w = jnp.dot(parts, ones, preferred_element_type=F32)
    n = v.shape[0]
    return w[0:n] + (w[n : 2 * n] + w[2 * n : 3 * n])


def remote(src, dst, send_sem, recv_sem, device):
    return pltpu.make_async_remote_copy(
        src_ref=src,
        dst_ref=dst,
        send_sem=send_sem,
        recv_sem=recv_sem,
        device_id=device,
        device_id_type=MESH,
    )


def kernel(
    pix_hbm,
    fid,
    x_hbm,
    gain_hbm,
    bias_hbm,
    ow_hbm,
    cw_hbm,
    iw_hbm,
    out,
    gain,
    bias,
    ow,
    iw,
    pixv,
    xb,
    cwv,
    sbuf,
    rbuf,
    picks,
    sums,
    packs,
    zbuf,
    dpx,
    rmat,
    xs,
    fs,
    gmat,
    emat,
    stin,
    stsend,
    strecv,
    table,
    cst,
    gred,
    bmat,
    lhs0,
    lhs1,
    ys,
    tok,
    trecv,
    pix_sem,
    x_sem,
    cw_sem,
    small_sem,
    s1s,
    s1r,
    zs,
    zr,
    sts,
    strs,
    tks,
    tkr,
):
    tm = lax.axis_index("tm")
    tl = lax.axis_index("tile")
    z = lax.div(tm, 2)
    c = lax.rem(tm, 2)
    below = lax.rem(tm + 7, 8)
    x = lax.div(tl, 4)
    y = lax.rem(tl, 4)

    def tile_at(place):
        return lax.rem(x + place[0], 4) * 4 + lax.rem(y + place[1], 4)


    pix_cp = pltpu.make_async_copy(pix_hbm.at[0], pixv, pix_sem)
    pix_cp.start()
    x_cps = []
    for f in range(2):
        for b in range(5):
            cp = pltpu.make_async_copy(
                x_hbm.at[f, :, pl.ds(BLK * b, BLK)], xb.at[f * 5 + b], x_sem.at[f * 5 + b]
            )
            cp.start()
            x_cps.append(cp)
    small_cps = []
    for i, (src, dst) in enumerate(
        ((gain_hbm, gain), (bias_hbm, bias), (ow_hbm, ow), (iw_hbm, iw))
    ):
        cp = pltpu.make_async_copy(src, dst, small_sem.at[i])
        cp.start()
        small_cps.append(cp)
    cw_cp = pltpu.make_async_copy(cw_hbm, cwv, cw_sem)
    cw_cp.start()

    barrier = pltpu.get_barrier_semaphore()

    def greet(device):
        pl.semaphore_signal(barrier, inc=1, device_id=device, device_id_type=MESH)

    def greet_chip(d, _):
        j = lax.rem(tl + d, 16)
        greet((tm, j))
        greet((tm + 1 - 2 * c, j))
        return 0

    lax.fori_loop(1, 16, greet_chip, 0)
    greet((tm + 1 - 2 * c, tl))
    for d in range(1, 4):
        for r in range(2):
            greet((lax.rem(z + d, 4) * 2 + lax.rem(c + r, 2), tl))

    lam = iota((BLK, 128), 0)
    chan = iota((BLK, 128), 1)
    same = (lax.div(lax.rem(lam, 96), 3) == lax.div(chan, 3)) & (chan < 96)
    gmat[...] = jnp.where(same, 1.0, 0.0).astype(BF16)
    emat[...] = jnp.where(
        lax.rem(iota((128, BLK), 1), 96) == iota((128, BLK), 0), 1.0, 0.0
    ).astype(BF16)

    def pack():
        frame_id = fid[0].astype(F32)
        r = iota((256, 240), 0)
        m = iota((256, 240), 1)
        slot = lax.rem(r, 32)
        col = 20 * lax.div(r, 64) + 10 * lax.div(lax.rem(r, 64), 32) + lax.rem(slot, 10)
        hit = (slot < 30) & (m == 80 * lax.div(slot, 10) + col)
        pick = jnp.where(hit, 1.0, 0.0).astype(BF16)
        spare = lax.rem(iota((256, 256), 0), 32) >= 30
        for n in range(4):
            stack = jnp.concatenate(
                [pixv[k, 80 * n : 80 * n + 80, :] for k in range(3)], axis=0
            )
            rows = jnp.dot(pick, stack, preferred_element_type=F32)
            rows = jnp.where(spare, frame_id, rows).astype(BF16)
            for jj in range(4):
                for ch in range(2):
                    sbuf[ch, 4 * n + jj] = rows[
                        64 * jj : 64 * jj + 64, 128 * ch : 128 * ch + 128
                    ]

    pix_cp.wait()
    pack()
    def strip_copy(half, r, d):
        j = tl if d == 0 else tile_at(PEERS[d - 1])
        h = lax.rem(c + r, 2)
        rows = pl.ds(32 * half, 32)
        return remote(
            sbuf.at[h, j, rows],
            rbuf.at[r, d, rows],
            s1s.at[half, r, d],
            s1r.at[half, r, d],
            (2 * z + h, j),
        )

    strips = tuple((r, d) for d in range(1, 16) for r in range(2)) + ((1, 0),)

    def strips_sent():
        for half in range(2):
            for r, d in strips:
                strip_copy(half, r, d).start()
        rbuf[0, 0] = sbuf[c, tl]

    for cp in x_cps:
        cp.wait()

    def fold(v):
        return v.reshape(v.shape[0] // 8, 8, v.shape[1]).sum(axis=0)

    def stats():
        stin[...] = jnp.zeros((8, BLK), F32)
        for f in range(2):

            def stat_step(i, carry, f=f):
                s, ss = carry
                b = lax.div(i, 8)
                r = pl.multiple_of(lax.rem(i, 8) * 32, 32)
                v = xb[f * 5 + b, pl.ds(r, 32), :].astype(F32)
                return s + fold(v), ss + fold(v * v)

            zero = jnp.zeros((8, BLK), F32)
            s, ss = lax.fori_loop(0, 40, stat_step, (zero, zero))
            stin[2 * f : 2 * f + 1, :] = jnp.sum(s, axis=0, keepdims=True)
            stin[2 * f + 1 : 2 * f + 2, :] = jnp.sum(ss, axis=0, keepdims=True)

    stats()
    pl.semaphore_wait(barrier, 31 + 6)
    strips_sent()

    def stat_copy(which, d):
        return remote(
            stsend.at[which],
            strecv.at[which, d],
            sts.at[which, d],
            strs.at[which, d],
            (tm, tile_at(FARTHEST[d - 1])),
        )

    def stat_send(which):
        red = exact_dot(stin[...], gmat[...])
        stsend[which] = red
        strecv[which, 0] = red
        for d in range(1, 16):
            stat_copy(which, d).start()

    def stat_wait(which):
        for d in range(1, 16):
            stat_copy(which, d).wait_recv()
        return jnp.sum(strecv[which], axis=0)

    stat_send(0)

    def colours():
        owe = jnp.dot(ow[...], emat[0:96, :], preferred_element_type=F32)
        q = iota((32, BLK), 0)
        kq = lax.div(q, 10)
        wq = lax.rem(q, 10)
        wl = lax.div(iota((32, BLK), 1), 96)
        small = jnp.where(
            kq == 0,
            owe[0:1, :],
            jnp.where(kq == 1, owe[1:2, :], jnp.where(kq == 2, owe[2:3, :], 0.0)),
        )
        for half, b in DXH:
            core = jnp.where(wq + 10 * half == wl + 4 * b, small, 0.0).astype(BF16)
            for part in range(3):
                rmat[half, b, 32 * part : 32 * part + 32, :] = core
            rmat[half, b, 96:128, :] = jnp.zeros((32, BLK), BF16)

    for cp in small_cps:
        cp.wait()
    colours()


    spread = jnp.where(lax.div(lax.rem(iota((128, 16), 0), 64), 4) == iota((128, 16), 1), 1.0, 0.0)

    def taps_reduced():
        iwr = jnp.dot(spread.astype(BF16), iw[...], preferred_element_type=F32).T.astype(BF16)
        for i in range(9):
            gred[3 * i : 3 * i + 3] = jnp.dot(
                cwv[3 * i : 3 * i + 3].reshape(288, BLK), iwr, preferred_element_type=F32
            ).reshape(3, 96, 128)

    cw_cp.wait()
    taps_reduced()

    ln = iota((16, 128), 1)
    main = ln < 64
    b0 = lax.rem(ln, 2) == 0
    a0 = lax.rem(lax.div(ln, 2), 2) == 0

    def combine(mc, _):
        r = pl.multiple_of(mc * 16, 16)
        for dt in range(3):
            cols = []
            for dh in range(3):
                g = [gred[9 * dt + 3 * dh + dw, pl.ds(r, 16), :] for dw in range(3)]
                g01 = g[0] + g[1]
                g12 = g[1] + g[2]
                zero = jnp.zeros_like(g01)
                cols.append(
                    (
                        jnp.where(main, jnp.where(b0, g12, zero), jnp.where(b0, zero, g[0])),
                        jnp.where(main, jnp.where(b0, g01, g[2]), zero),
                        jnp.where(main, jnp.where(b0, g[0], g12), zero),
                        jnp.where(main, jnp.where(b0, zero, g01), jnp.where(b0, g[2], zero)),
                    )
                )
            for w in range(4):
                h0, h1, h2 = (cols[dh][w] for dh in range(3))
                h01 = h0 + h1
                h12 = h1 + h2
                zero = jnp.zeros_like(h01)
                taps = (
                    jnp.where(a0, h2, zero),
                    jnp.where(a0, h12, zero),
                    jnp.where(a0, h01, h2),
                    jnp.where(a0, h0, h12),
                    jnp.where(a0, zero, h01),
                    jnp.where(a0, zero, h0),
                )
                for t in range(6):
                    row = pl.multiple_of(t * BLK + w * 96 + r, 16)
                    top = taps[t].astype(BF16)
                    rest = (taps[t] - top.astype(F32)).astype(BF16)
                    bmat[pl.ds(row, 16), 256 * dt : 256 * dt + 128] = top
                    bmat[pl.ds(row, 16), 256 * dt + 128 : 256 * dt + 256] = rest
        return 0

    def weights():
        lax.fori_loop(0, 6, combine, 0)

    weights()

    def frame_picks():
        for r in range(2):
            ids = rbuf[r, :, 16:32, :].astype(F32)
            ids = jnp.broadcast_to(ids[:, 15:16, :], (16, 16, 128)).reshape(256, 128)
            ids = jnp.concatenate([ids, ids], axis=1)
            at = iota((256, 256), 1)
            hit = (ids == lax.div(at, 16).astype(F32)) & (
                lax.rem(iota((256, 256), 0), 16) == lax.rem(at, 16)
            )
            picks[:, 256 * r : 256 * r + 256] = jnp.where(hit, 1.0, 0.0).T.astype(BF16)

    def frame_sums(half):
        stack = jnp.concatenate(
            [rbuf[:, :, 16 * g : 16 * g + 16, :].reshape(512, 128) for g in (2 * half, 2 * half + 1)],
            axis=1,
        )
        total = jnp.dot(picks[...], stack, preferred_element_type=F32)
        for g in range(2):
            v = total[:, 128 * g : 128 * g + 128].reshape(8, 2, 16, 128)
            if g == 1:
                v = jnp.where(iota(v.shape, 2) >= 14, 0.0, v)
            sums[half, :, :, 16 * g : 16 * g + 16, :] = v

    def packed(half):
        for owner in range(8):
            v = sums[half, owner]
            largest = jnp.max(jnp.maximum(v[0], v[1]), axis=0, keepdims=True)
            smallest = jnp.min(jnp.minimum(v[0], v[1]), axis=0, keepdims=True)
            largest = jnp.maximum(jnp.maximum(largest, -smallest), 1e-20)
            step = jnp.floor(jnp.log(largest) * EIGHTHS) + 2.0
            scale = RANGE * jnp.exp(step * (-1.0 / EIGHTHS))
            w = jnp.round(v * scale[None])
            w = jnp.where(iota(v.shape, 1) >= 30, step[None], w)
            packs[half, owner] = w.astype(jnp.int32).astype(jnp.int16)

    def unpacked(v):
        v = v.astype(jnp.int32).astype(F32)
        return v * (jnp.exp(v[:, 30:31, :] * (1.0 / EIGHTHS)) * (1.0 / RANGE))

    def z_copy(half, r, d):
        owner = lax.rem(z + d, 4) * 2 + lax.rem(c + r, 2)
        return remote(
            packs.at[half, owner],
            zbuf.at[half, r, d],
            zs.at[half, r, d],
            zr.at[half, r, d],
            (owner, tl),
        )

    partners = tuple((r, d) for d in (2, 1, 3, 0) for r in (1, 0) if r + d > 0)

    for half in range(2):
        for r, d in strips:
            strip_copy(half, r, d).wait_recv()
        if half == 0:
            frame_picks()
        frame_sums(half)
        packed(half)
        for r, d in partners:
            z_copy(half, r, d).start()

    tot = stat_wait(0) / COUNT
    rows = []
    for f in range(2):
        mean = tot[2 * f : 2 * f + 1]
        meansq = tot[2 * f + 1 : 2 * f + 2]
        rstd = lax.rsqrt(meansq - mean * mean + EPS)
        rows.append((mean, rstd))
    table[...] = jnp.zeros((8, 128), F32)
    for f in range(2):
        table[f : f + 1, :] = rows[f][0]
        table[6 + f : 7 + f, 0:96] = 0.5 * rows[f][1][:, 0:96] * gain[...]
    table[4:5, 0:96] = gain[...]
    table[5:6, 0:96] = 0.5 * bias[...]
    cst[...] = exact_dot(table[...], emat[...])

    def factor():
        for f in range(2):
            mean_l = cst[f : f + 1, :]
            a_l = cst[6 + f : 7 + f, :]
            hb_l = cst[5:6, :]
            g2_l = 0.5 * cst[4:5, :]

            def factor_step(i, _, f=f, mean_l=mean_l, a_l=a_l, hb_l=hb_l, g2_l=g2_l):
                b = lax.div(i, 8)
                r = pl.multiple_of(lax.rem(i, 8) * 32, 32)
                v = xb[f * 5 + b, pl.ds(r, 32), :].astype(F32) - mean_l
                u = v * a_l + hb_l
                h = jnp.tanh(u)
                w = (1.0 + u * (1.0 - h)) * ((1.0 + h) * g2_l)
                for i in range(3):
                    xs[f * 5 + b, i, pl.ds(r, 32), :] = v[:, 128 * i : 128 * i + 128]
                    fs[f * 5 + b, i, pl.ds(r, 32), :] = w[:, 128 * i : 128 * i + 128]
                return 0

            lax.fori_loop(0, 40, factor_step, 0)

    factor()

    def frame_rows(half):
        for r in range(2):
            dp = sums[half, tm] if r == 0 else unpacked(zbuf[half, 1, 0])
            for d in range(1, 4):
                dp = dp + unpacked(zbuf[half, r, d])
            for f in range(2):
                top = dp[f].astype(BF16).astype(F32)
                mid = (dp[f] - top).astype(BF16).astype(F32)
                rest = dp[f] - top - mid
                parts = jnp.concatenate([top, mid, rest, jnp.zeros_like(rest)], axis=0).T
                dpx[half, lax.rem(c + r, 2), 128 * f : 128 * f + 128, :] = parts.astype(BF16)

    def dxh(blocks, carry):
        for b in blocks:
            for rows_at in range(2):
                da = None
                for half in range(2):
                    if (half, b) in DXH:
                        v = jnp.dot(
                            dpx[half, rows_at], rmat[half, b], preferred_element_type=F32
                        )
                        da = v if da is None else da + v
                new = []
                for f in range(2):
                    at = pl.ds(128 * rows_at, 128)
                    s, sx = [], []
                    for i in range(3):
                        v = da[128 * f : 128 * f + 128, 128 * i : 128 * i + 128]
                        v = v * fs[f * 5 + b, i, at, :]
                        fs[f * 5 + b, i, at, :] = v
                        s.append(carry[6 * f + i] + fold(v))
                        sx.append(carry[6 * f + 3 + i] + fold(v * xs[f * 5 + b, i, at, :]))
                    new += s + sx
                carry = tuple(new)
        return carry

    carry = tuple(jnp.zeros((8, 128), F32) for _ in range(12))
    for half in range(2):
        for r, d in partners:
            z_copy(half, r, d).wait_recv()
        frame_rows(half)
        carry = dxh((0, 1) if half == 0 else (2, 3, 4), carry)

    def dxh_sums():
        for i in range(12):
            stin[i // 3 : i // 3 + 1, 128 * (i % 3) : 128 * (i % 3) + 128] = jnp.sum(
                carry[i], axis=0, keepdims=True
            )

    dxh_sums()
    stat_send(1)
    tot = stat_wait(1) / COUNT
    terms = []
    for f in range(2):
        rstd = rows[f][1]
        first = tot[2 * f : 2 * f + 1]
        second = tot[2 * f + 1 : 2 * f + 2] * rstd
        terms += [rstd, -rstd * rstd * second, -rstd * first, jnp.zeros_like(rstd)]
    cst[...] = exact_dot(jnp.concatenate(terms, axis=0), emat[...])

    def left_side(f):
        left = lhs0 if f == 0 else lhs1
        row = iota((64, 128), 0)
        for i in range(3):
            ls = slice(128 * i, 128 * i + 128)
            p_l = cst[4 * f : 4 * f + 1, ls]
            q_l = cst[4 * f + 1 : 4 * f + 2, ls]
            r_l = cst[4 * f + 2 : 4 * f + 3, ls]
            for b in range(5):
                fb = f * 5 + b
                for rho in range(4):
                    sel = pl.ds(rho, 64, stride=4)
                    d = p_l * fs[fb, i, sel, :] + q_l * xs[fb, i, sel, :] + r_l
                    at = BLK * (rho + 1) + 128 * i
                    left[64 * b : 64 * b + 64, at : at + 128] = d.astype(BF16)
                    if rho == 0:
                        d = jnp.where(row == 63, 0.0, pltpu.roll(d, 63, 0))
                        at = BLK * 5 + 128 * i
                        left[64 * b : 64 * b + 64, at : at + 128] = d.astype(BF16)
                    if rho == 3:
                        d = jnp.where(row == 0, 0.0, pltpu.roll(d, 1, 0))
                        at = 128 * i
                        left[64 * b : 64 * b + 64, at : at + 128] = d.astype(BF16)

    def conv(f, first, last):
        left = lhs0 if f == 0 else lhs1
        at = slice(256 * first, 256 * last + 256)
        ys[320 * f : 320 * f + 320, at] = jnp.dot(
            left[...], bmat[:, at], preferred_element_type=F32
        )

    ln = iota((64, 128), 1)
    lo64 = ln < 64
    odd = lax.rem(ln, 2) == 1

    def taken(f, dt, b):
        r = 64 * (5 * f + b)
        return (
            ys[r : r + 64, 256 * dt : 256 * dt + 128]
            + ys[r : r + 64, 256 * dt + 128 : 256 * dt + 256]
        )

    def tokens(group, t, terms):
        cc = []
        for b in range(5):
            v = taken(*terms[0], b)
            for term in terms[1:]:
                v = v + taken(*term, b)
            cc.append(v)
        r1 = pltpu.roll(cc[1], 64, 1)
        r3 = pltpu.roll(cc[3], 64, 1)
        v0 = jnp.where(
            lo64, cc[0] + jnp.where(odd, r1, 0.0), r1 + jnp.where(odd, cc[2], cc[0])
        )
        v1 = jnp.where(
            lo64, cc[2] + jnp.where(odd, r3, r1), r3 + jnp.where(odd, cc[4], cc[2])
        )
        v2 = jnp.where(lo64, cc[4] + jnp.where(odd, 0.0, r3), jnp.where(odd, cc[0], cc[4]))
        for i, v in enumerate((v0, v1, v2)):
            tok[group, 8 * t : 8 * t + 8, :, 128 * i : 128 * i + 128] = v.reshape(8, 8, 128)

    def own_copy(d, sending):
        a, b = FARTHEST[d - 1]
        j = tile_at((a, b))
        at = tl if sending else tile_at((4 - a, 4 - b))
        return remote(tok.at[0, j], trecv.at[0, at], tks.at[0, d], tkr.at[0, at], (tm, j))

    def span_copy(d, sending):
        a, b = ((FARTHEST + ((0, 0),)))[d]
        j = tile_at((a, b))
        at = tl if sending else tile_at((4 - a, 4 - b))
        return remote(tok.at[1, j], trecv.at[1, at], tks.at[1, d], tkr.at[1, at], (below, j))

    left_side(0)
    conv(0, 0, 1)
    left_side(1)
    conv(1, 0, 0)
    tokens(1, 0, ((0, 0),))
    tokens(1, 1, ((0, 1), (1, 0)))
    for d in range(16):
        span_copy(d, True).start()
    conv(0, 2, 2)
    conv(1, 1, 2)
    tokens(0, 0, ((0, 2), (1, 1)))
    tokens(0, 1, ((1, 2),))
    for d in range(1, 16):
        own_copy(d, True).start()
    trecv[0, tl] = tok[0, tl]

    for d in range(16):
        span_copy(d, False).wait_recv()
    for d in range(1, 16):
        own_copy(d, False).wait_recv()

    def assemble():
        ln = iota((8, 128), 1)
        lo8 = ln < 64
        odd8 = lax.rem(ln, 2) == 1
        strips = []
        for j in range(16):
            strips.append(
                [
                    trecv[0, j, :, 128 * i : 128 * i + 128]
                    + jnp.where(tm < 7, trecv[1, j, :, 128 * i : 128 * i + 128], 0.0)
                    for i in range(3)
                ]
            )
        halo = [pltpu.roll(s[2], 64, 1) for s in strips]
        for j in range(16):
            if j > 0:
                strips[j][0] = strips[j][0] + jnp.where(lo8 & ~odd8, halo[j - 1], 0.0)
        done = []
        for j in range(16):
            v2 = strips[j][2]
            if j < 15:
                v2 = v2 + jnp.where(odd8, halo[j + 1], 0.0)
            done.append((strips[j][0], strips[j][1], v2))
        for pair in range(8):
            e = done[2 * pair]
            o = [pltpu.roll(v, 64, 1) for v in done[2 * pair + 1]]
            at = 640 * pair
            out[:, at : at + 128] = e[0]
            out[:, at + 128 : at + 256] = e[1]
            out[:, at + 256 : at + 384] = jnp.where(lo8, e[2], o[0])
            out[:, at + 384 : at + 512] = jnp.where(lo8, o[0], o[1])
            out[:, at + 512 : at + 640] = jnp.where(lo8, o[1], o[2])

    assemble()

    for half in range(2):
        for r, d in strips:
            strip_copy(half, r, d).wait_send()
        for r, d in partners:
            z_copy(half, r, d).wait_send()
        for d in range(1, 16):
            stat_copy(half, d).wait_send()
    for d in range(1, 16):
        own_copy(d, True).wait_send()
    for d in range(16):
        span_copy(d, True).wait_send()


def body(pix_grad, frame_ids, pre_norm, gain, bias, out_weight, conv_weight, in_weight):
    hbm = pl.BlockSpec(memory_space=pltpu.HBM)
    smem = pl.BlockSpec(memory_space=pltpu.SMEM)
    dma = pltpu.SemaphoreType.DMA

    def kept(array):
        return pltpu.with_memory_space_constraint(array, pltpu.HBM)

    pix_grad = jnp.transpose(pix_grad, (0, 1, 3, 2))
    out_weight = out_weight.T
    gain = gain.reshape(1, 96)
    bias = bias.reshape(1, 96)
    return pl.pallas_call(
        kernel,
        out_shape=jax.ShapeDtypeStruct((8, 5120), F32),
        in_specs=[hbm, smem] + [hbm] * 6,
        out_specs=pl.BlockSpec(memory_space=pltpu.VMEM),
        scratch_shapes=[
            pltpu.VMEM((1, 96), F32),
            pltpu.VMEM((1, 96), F32),
            pltpu.VMEM((3, 96), BF16),
            pltpu.VMEM((16, 384), BF16),
            pltpu.VMEM((3, 320, 256), BF16),
            pltpu.VMEM((PIECES, 256, BLK), BF16),
            pltpu.VMEM((27, 96, 384), BF16),
            pltpu.VMEM((2, 16, 64, 128), BF16),
            pltpu.VMEM((2, 16, 64, 128), BF16),
            pltpu.VMEM((256, 512), BF16),
            pltpu.VMEM((2, 8, 2, 32, 128), F32),
            pltpu.VMEM((2, 8, 2, 32, 128), jnp.int16),
            pltpu.VMEM((2, 2, 4, 2, 32, 128), jnp.int16),
            pltpu.VMEM((2, 2, 256, 128), BF16),
            pltpu.VMEM((2, 5, 128, BLK), BF16),
            pltpu.VMEM((PIECES, 3, 256, 128), F32),
            pltpu.VMEM((PIECES, 3, 256, 128), F32),
            pltpu.VMEM((BLK, 128), BF16),
            pltpu.VMEM((128, BLK), BF16),
            pltpu.VMEM((8, BLK), F32),
            pltpu.VMEM((2, 8, 128), F32),
            pltpu.VMEM((2, 16, 8, 128), F32),
            pltpu.VMEM((8, 128), F32),
            pltpu.VMEM((8, BLK), F32),
            pltpu.VMEM((27, 96, 128), F32),
            pltpu.VMEM((6 * BLK, 2 * BLK), BF16),
            pltpu.VMEM((320, 6 * BLK), BF16),
            pltpu.VMEM((320, 6 * BLK), BF16),
            pltpu.VMEM((640, 2 * BLK), F32),
            pltpu.VMEM((2, 16, 8, BLK), F32),
            pltpu.VMEM((2, 16, 8, BLK), F32),
            dma,
            dma((PIECES,)),
            dma,
            dma((4,)),
            dma((2, 2, 16)),
            dma((2, 2, 16)),
            dma((2, 2, 4)),
            dma((2, 2, 4)),
            dma((2, 16)),
            dma((2, 16)),
            dma((2, 16)),
            dma((2, 16)),
        ],
        compiler_params=pltpu.CompilerParams(
            collective_id=0, has_side_effects=True, vmem_limit_bytes=50 * 1024 * 1024
        ),
    )(
        kept(pix_grad),
        frame_ids,
        kept(pre_norm),
        kept(gain),
        kept(bias),
        kept(out_weight),
        kept(conv_weight),
        kept(in_weight),
    )


def solution(mesh):
    return jax.shard_map(
        body,
        mesh=mesh,
        in_specs=(
            P(("tm", "tile"), None, None, None),
            P(("tm", "tile")),
            P("tm", None, "tile"),
            P(),
            P(),
            P(),
            P(),
            P(),
        ),
        out_specs=P(("tm", "tile"), None),
        check_vma=False,
    )
```

```python
import jax
import jax.numpy as jnp
from jax import lax
from jax.experimental import pallas as pl
from jax.experimental.pallas import tpu as pltpu
from jax.sharding import PartitionSpec as P

MESH = pl.DeviceIdType.MESH
F32 = jnp.float32
BF16 = jnp.bfloat16
COUNT = 256.0 * 320.0 * 3.0
EPS = 1e-05
EIGHTHS = 8.0 / 0.6931471805599453
RANGE = 32700.0
BLK = 384
NEAR = ((2, 0), (0, 2), (1, 0), (0, 1), (3, 0), (0, 3))
PEERS = NEAR + ((1, 2), (3, 2), (2, 1), (2, 3), (2, 2), (1, 1), (3, 3), (1, 3), (3, 1))
FARTHEST = (
    (2, 2), (1, 2), (3, 2), (2, 1), (2, 3), (1, 1), (3, 3), (1, 3),
    (3, 1), (2, 0), (0, 2), (0, 1), (1, 0), (0, 3), (3, 0),
)
DXH = ((0, 0), (0, 1), (0, 2), (1, 2), (1, 3), (1, 4))
PIECES = 10


def iota(shape, dim):
    return lax.broadcasted_iota(jnp.int32, shape, dim)


def exact_dot(v, ones):
    top = v.astype(BF16).astype(F32)
    mid = (v - top).astype(BF16).astype(F32)
    parts = jnp.concatenate([top, mid, v - top - mid], axis=0).astype(BF16)
    w = jnp.dot(parts, ones, preferred_element_type=F32)
    n = v.shape[0]
    return w[0:n] + (w[n : 2 * n] + w[2 * n : 3 * n])


def remote(src, dst, send_sem, recv_sem, device):
    return pltpu.make_async_remote_copy(
        src_ref=src,
        dst_ref=dst,
        send_sem=send_sem,
        recv_sem=recv_sem,
        device_id=device,
        device_id_type=MESH,
    )


def kernel(
    pix_hbm,
    fid,
    x_hbm,
    gain_hbm,
    bias_hbm,
    ow_hbm,
    cw_hbm,
    iw_hbm,
    out,
    gain,
    bias,
    ow,
    iw,
    pixv,
    xb,
    cwv,
    sbuf,
    rbuf,
    picks,
    sums,
    packs,
    zbuf,
    dpx,
    rmat,
    xs,
    fs,
    gmat,
    emat,
    stin,
    stsend,
    strecv,
    table,
    cst,
    gred,
    bupper,
    bmiddle,
    blower,
    lupper,
    lmiddle,
    llower,
    yupper,
    ymiddle,
    ylower,
    tok,
    trecv,
    ready_sem,
    pix_sem,
    x_sem,
    cw_sem,
    small_sem,
    s1s,
    s1r,
    zs,
    zr,
    sts,
    strs,
    tks,
    tkr,
):
    tm = lax.axis_index("tm")
    tl = lax.axis_index("tile")
    z = lax.div(tm, 2)
    c = lax.rem(tm, 2)
    below = lax.rem(tm + 7, 8)
    x = lax.div(tl, 4)
    y = lax.rem(tl, 4)

    def tile_at(place):
        return lax.rem(x + place[0], 4) * 4 + lax.rem(y + place[1], 4)


    barrier = pltpu.get_barrier_semaphore()

    def greet(device):
        pl.semaphore_signal(barrier, inc=1, device_id=device, device_id_type=MESH)

    for place in NEAR:
        greet((tm, tile_at(place)))
        greet((tm + 1 - 2 * c, tile_at(place)))
    for d in (2, 1, 3):
        for r in range(2):
            greet((lax.rem(z + d, 4) * 2 + lax.rem(c + r, 2), tl))
    greet((tm + 1 - 2 * c, tl))

    pix_cp = pltpu.make_async_copy(pix_hbm.at[0], pixv, pix_sem)
    pix_cp.start()
    x_cps = []
    for f in range(2):
        for b in range(5):
            cp = pltpu.make_async_copy(
                x_hbm.at[f, :, pl.ds(BLK * b, BLK)], xb.at[f * 5 + b], x_sem.at[f * 5 + b]
            )
            cp.start()
            x_cps.append(cp)
    small_cps = []
    for i, (src, dst) in enumerate(
        ((gain_hbm, gain), (bias_hbm, bias), (ow_hbm, ow), (iw_hbm, iw))
    ):
        cp = pltpu.make_async_copy(src, dst, small_sem.at[i])
        cp.start()
        small_cps.append(cp)
    cw_cp = pltpu.make_async_copy(cw_hbm, cwv, cw_sem)
    cw_cp.start()

    def pack():
        frame_id = fid[0].astype(F32)
        r = iota((256, 240), 0)
        m = iota((256, 240), 1)
        slot = lax.rem(r, 32)
        col = 20 * lax.div(r, 64) + 10 * lax.div(lax.rem(r, 64), 32) + lax.rem(slot, 10)
        hit = (slot < 30) & (m == 80 * lax.div(slot, 10) + col)
        pick = jnp.where(hit, 1.0, 0.0).astype(BF16)
        spare = lax.rem(iota((256, 256), 0), 32) >= 30
        for n in range(4):
            stack = jnp.concatenate(
                [pixv[k, 80 * n : 80 * n + 80, :] for k in range(3)], axis=0
            )
            rows = jnp.dot(pick, stack, preferred_element_type=F32)
            rows = jnp.where(spare, frame_id, rows).astype(BF16)
            for jj in range(4):
                for ch in range(2):
                    sbuf[ch, 4 * n + jj] = rows[
                        64 * jj : 64 * jj + 64, 128 * ch : 128 * ch + 128
                    ]

    pix_cp.wait()
    pack()
    def strip_copy(half, r, d):
        j = tl if d == 0 else tile_at(PEERS[d - 1])
        h = lax.rem(c + r, 2)
        rows = pl.ds(32 * half, 32)
        return remote(
            sbuf.at[h, j, rows],
            rbuf.at[r, d, rows],
            s1s.at[half, r, d],
            s1r.at[half, r, d],
            (2 * z + h, j),
        )

    strips = tuple((r, d) for d in range(1, 16) for r in range(2)) + ((1, 0),)

    def strips_sent(some):
        for half in range(2):
            for r, d in some:
                strip_copy(half, r, d).start()

    pl.semaphore_wait(barrier, 12 + 6 + 1)
    for place in ((2, 0), (1, 0), (3, 0)):
        pl.semaphore_signal(
            ready_sem, inc=1, device_id=(tm, tile_at(place)), device_id_type=MESH
        )
    strips_sent(strips[0:12] + strips[-1:])
    rbuf[0, 0] = sbuf[c, tl]

    pl.semaphore_wait(ready_sem, 3)
    strips_sent(strips[12:30])

    lam = iota((BLK, 128), 0)
    chan = iota((BLK, 128), 1)
    same = (lax.div(lax.rem(lam, 96), 3) == lax.div(chan, 3)) & (chan < 96)
    gmat[...] = jnp.where(same, 1.0, 0.0).astype(BF16)
    emat[...] = jnp.where(
        lax.rem(iota((128, BLK), 1), 96) == iota((128, BLK), 0), 1.0, 0.0
    ).astype(BF16)

    for cp in x_cps:
        cp.wait()

    def fold(v):
        return v.reshape(v.shape[0] // 8, 8, v.shape[1]).sum(axis=0)

    def stats():
        stin[...] = jnp.zeros((8, BLK), F32)
        for f in range(2):

            def stat_step(i, carry, f=f):
                s, ss = carry
                b = lax.div(i, 8)
                r = pl.multiple_of(lax.rem(i, 8) * 32, 32)
                v = xb[f * 5 + b, pl.ds(r, 32), :].astype(F32)
                return s + fold(v), ss + fold(v * v)

            zero = jnp.zeros((8, BLK), F32)
            s, ss = lax.fori_loop(0, 40, stat_step, (zero, zero))
            stin[2 * f : 2 * f + 1, :] = jnp.sum(s, axis=0, keepdims=True)
            stin[2 * f + 1 : 2 * f + 2, :] = jnp.sum(ss, axis=0, keepdims=True)

    stats()

    def stat_copy(which, d):
        return remote(
            stsend.at[which],
            strecv.at[which, d],
            sts.at[which, d],
            strs.at[which, d],
            (tm, tile_at(FARTHEST[d - 1])),
        )

    def stat_send(which):
        red = exact_dot(stin[...], gmat[...])
        stsend[which] = red
        strecv[which, 0] = red
        for d in range(1, 16):
            stat_copy(which, d).start()

    def stat_wait(which):
        for d in range(1, 16):
            stat_copy(which, d).wait_recv()
        return jnp.sum(strecv[which], axis=0)

    stat_send(0)

    def colours():
        owe = jnp.dot(ow[...], emat[0:96, :], preferred_element_type=F32)
        q = iota((32, BLK), 0)
        kq = lax.div(q, 10)
        wq = lax.rem(q, 10)
        wl = lax.div(iota((32, BLK), 1), 96)
        small = jnp.where(
            kq == 0,
            owe[0:1, :],
            jnp.where(kq == 1, owe[1:2, :], jnp.where(kq == 2, owe[2:3, :], 0.0)),
        )
        for half, b in DXH:
            core = jnp.where(wq + 10 * half == wl + 4 * b, small, 0.0).astype(BF16)
            for part in range(3):
                rmat[half, b, 32 * part : 32 * part + 32, :] = core
            rmat[half, b, 96:128, :] = jnp.zeros((32, BLK), BF16)

    for cp in small_cps:
        cp.wait()
    colours()


    spread = jnp.where(lax.div(lax.rem(iota((128, 16), 0), 64), 4) == iota((128, 16), 1), 1.0, 0.0)

    def taps_reduced():
        iwr = jnp.dot(spread.astype(BF16), iw[...], preferred_element_type=F32).T.astype(BF16)
        for i in range(9):
            gred[3 * i : 3 * i + 3] = jnp.dot(
                cwv[3 * i : 3 * i + 3].reshape(288, BLK), iwr, preferred_element_type=F32
            ).reshape(3, 96, 128)

    cw_cp.wait()
    taps_reduced()

    ln = iota((16, 128), 1)
    main = ln < 64
    b0 = lax.rem(ln, 2) == 0
    a0 = lax.rem(lax.div(ln, 2), 2) == 0

    def combine(mc, _):
        r = pl.multiple_of(mc * 16, 16)
        for dt in range(3):
            cols = []
            for dh in range(3):
                g = [gred[9 * dt + 3 * dh + dw, pl.ds(r, 16), :] for dw in range(3)]
                g01 = g[0] + g[1]
                g12 = g[1] + g[2]
                zero = jnp.zeros_like(g01)
                cols.append(
                    (
                        jnp.where(main, jnp.where(b0, g12, zero), jnp.where(b0, zero, g[0])),
                        jnp.where(main, jnp.where(b0, g01, g[2]), zero),
                        jnp.where(main, jnp.where(b0, g[0], g12), zero),
                        jnp.where(main, jnp.where(b0, zero, g01), jnp.where(b0, g[2], zero)),
                    )
                )
            for w in range(4):
                h0, h1, h2 = (cols[dh][w] for dh in range(3))
                h01 = h0 + h1
                h12 = h1 + h2
                for value, ref, t, at in (
                    (h2, bupper, 0, 128 * dt),
                    (h12, bupper, 1, 128 * dt),
                    (h01, bmiddle, 0, 256 * dt),
                    (h0, bmiddle, 1, 256 * dt),
                    (h2, bmiddle, 0, 256 * dt + 128),
                    (h12, bmiddle, 1, 256 * dt + 128),
                    (h01, blower, 0, 128 * dt),
                    (h0, blower, 1, 128 * dt),
                ):
                    row = pl.multiple_of(t * BLK + w * 96 + r, 16)
                    top = value.astype(BF16).astype(F32)
                    rest = value - top
                    first = a0 if at % 256 == 0 and ref is bmiddle or ref is bupper else ~a0
                    ref[pl.ds(row, 16), at : at + 128] = jnp.where(first, top, rest).astype(BF16)
        return 0

    def weights():
        lax.fori_loop(0, 6, combine, 0)

    weights()

    def frame_picks():
        for r in range(2):
            ids = rbuf[r, :, 16:32, :].astype(F32)
            ids = jnp.broadcast_to(ids[:, 15:16, :], (16, 16, 128)).reshape(256, 128)
            ids = jnp.concatenate([ids, ids], axis=1)
            at = iota((256, 256), 1)
            hit = (ids == lax.div(at, 16).astype(F32)) & (
                lax.rem(iota((256, 256), 0), 16) == lax.rem(at, 16)
            )
            picks[:, 256 * r : 256 * r + 256] = jnp.where(hit, 1.0, 0.0).T.astype(BF16)

    def frame_sums(half):
        stack = jnp.concatenate(
            [rbuf[:, :, 16 * g : 16 * g + 16, :].reshape(512, 128) for g in (2 * half, 2 * half + 1)],
            axis=1,
        )
        total = jnp.dot(picks[...], stack, preferred_element_type=F32)
        for g in range(2):
            v = total[:, 128 * g : 128 * g + 128].reshape(8, 2, 16, 128)
            if g == 1:
                v = jnp.where(iota(v.shape, 2) >= 14, 0.0, v)
            sums[half, :, :, 16 * g : 16 * g + 16, :] = v

    def packed(half):
        for owner in range(8):
            v = sums[half, owner]
            largest = jnp.max(jnp.maximum(v[0], v[1]), axis=0, keepdims=True)
            smallest = jnp.min(jnp.minimum(v[0], v[1]), axis=0, keepdims=True)
            largest = jnp.maximum(jnp.maximum(largest, -smallest), 1e-20)
            step = jnp.floor(jnp.log(largest) * EIGHTHS) + 2.0
            scale = RANGE * jnp.exp(step * (-1.0 / EIGHTHS))
            w = jnp.round(v * scale[None])
            w = jnp.where(iota(v.shape, 1) >= 30, step[None], w)
            packs[half, owner] = w.astype(jnp.int32).astype(jnp.int16)

    def unpacked(v):
        v = v.astype(jnp.int32).astype(F32)
        return v * (jnp.exp(v[:, 30:31, :] * (1.0 / EIGHTHS)) * (1.0 / RANGE))

    def z_copy(half, r, d):
        owner = lax.rem(z + d, 4) * 2 + lax.rem(c + r, 2)
        return remote(
            packs.at[half, owner],
            zbuf.at[half, r, d],
            zs.at[half, r, d],
            zr.at[half, r, d],
            (owner, tl),
        )

    partners = tuple((r, d) for d in (2, 1, 3, 0) for r in (1, 0) if r + d > 0)

    for half in range(2):
        for r, d in strips:
            strip_copy(half, r, d).wait_recv()
        if half == 0:
            frame_picks()
        frame_sums(half)
        packed(half)
        for r, d in partners:
            z_copy(half, r, d).start()

    tot = stat_wait(0) / COUNT
    rows = []
    for f in range(2):
        mean = tot[2 * f : 2 * f + 1]
        meansq = tot[2 * f + 1 : 2 * f + 2]
        rstd = lax.rsqrt(meansq - mean * mean + EPS)
        rows.append((mean, rstd))
    table[...] = jnp.zeros((8, 128), F32)
    for f in range(2):
        table[f : f + 1, :] = rows[f][0]
        table[6 + f : 7 + f, 0:96] = 0.5 * rows[f][1][:, 0:96] * gain[...]
    table[4:5, 0:96] = gain[...]
    table[5:6, 0:96] = 0.5 * bias[...]
    cst[...] = exact_dot(table[...], emat[...])

    def factor():
        for f in range(2):
            mean_l = cst[f : f + 1, :]
            a_l = cst[6 + f : 7 + f, :]
            hb_l = cst[5:6, :]
            g2_l = 0.5 * cst[4:5, :]

            def factor_step(i, _, f=f, mean_l=mean_l, a_l=a_l, hb_l=hb_l, g2_l=g2_l):
                b = lax.div(i, 8)
                r = pl.multiple_of(lax.rem(i, 8) * 32, 32)
                v = xb[f * 5 + b, pl.ds(r, 32), :].astype(F32) - mean_l
                u = v * a_l + hb_l
                h = jnp.tanh(u)
                w = (1.0 + u * (1.0 - h)) * ((1.0 + h) * g2_l)
                for i in range(3):
                    xs[f * 5 + b, i, pl.ds(r, 32), :] = v[:, 128 * i : 128 * i + 128]
                    fs[f * 5 + b, i, pl.ds(r, 32), :] = w[:, 128 * i : 128 * i + 128]
                return 0

            lax.fori_loop(0, 40, factor_step, 0)

    factor()

    def frame_rows(half):
        for r in range(2):
            dp = sums[half, tm] if r == 0 else unpacked(zbuf[half, 1, 0])
            for d in range(1, 4):
                dp = dp + unpacked(zbuf[half, r, d])
            for f in range(2):
                top = dp[f].astype(BF16).astype(F32)
                mid = (dp[f] - top).astype(BF16).astype(F32)
                rest = dp[f] - top - mid
                parts = jnp.concatenate([top, mid, rest, jnp.zeros_like(rest)], axis=0).T
                dpx[half, lax.rem(c + r, 2), 128 * f : 128 * f + 128, :] = parts.astype(BF16)

    def dxh(blocks, carry):
        for b in blocks:
            for rows_at in range(2):
                da = None
                for half in range(2):
                    if (half, b) in DXH:
                        v = jnp.dot(
                            dpx[half, rows_at], rmat[half, b], preferred_element_type=F32
                        )
                        da = v if da is None else da + v
                new = []
                for f in range(2):
                    at = pl.ds(128 * rows_at, 128)
                    s, sx = [], []
                    for i in range(3):
                        v = da[128 * f : 128 * f + 128, 128 * i : 128 * i + 128]
                        v = v * fs[f * 5 + b, i, at, :]
                        fs[f * 5 + b, i, at, :] = v
                        s.append(carry[6 * f + i] + fold(v))
                        sx.append(carry[6 * f + 3 + i] + fold(v * xs[f * 5 + b, i, at, :]))
                    new += s + sx
                carry = tuple(new)
        return carry

    carry = tuple(jnp.zeros((8, 128), F32) for _ in range(12))
    for half in range(2):
        for r, d in partners:
            z_copy(half, r, d).wait_recv()
        frame_rows(half)
        carry = dxh((0, 1) if half == 0 else (2, 3, 4), carry)

    def dxh_sums():
        for i in range(12):
            stin[i // 3 : i // 3 + 1, 128 * (i % 3) : 128 * (i % 3) + 128] = jnp.sum(
                carry[i], axis=0, keepdims=True
            )

    dxh_sums()
    stat_send(1)
    tot = stat_wait(1) / COUNT
    terms = []
    for f in range(2):
        rstd = rows[f][1]
        first = tot[2 * f : 2 * f + 1]
        second = tot[2 * f + 1 : 2 * f + 2] * rstd
        terms += [rstd, -rstd * rstd * second, -rstd * first, jnp.zeros_like(rstd)]
    cst[...] = exact_dot(jnp.concatenate(terms, axis=0), emat[...])

    def placed(left, f, b, tap, i, d):
        at = BLK * tap + 128 * i
        left[f, 64 * b : 64 * b + 64, at : at + 128] = d.astype(BF16)

    def left_side(f, rows):
        row = iota((64, 128), 0)
        for i in range(3):
            ls = slice(128 * i, 128 * i + 128)
            p_l = cst[4 * f : 4 * f + 1, ls]
            q_l = cst[4 * f + 1 : 4 * f + 2, ls]
            r_l = cst[4 * f + 2 : 4 * f + 3, ls]
            for b in range(5):
                fb = f * 5 + b
                for rho in rows:
                    sel = pl.ds(rho, 64, stride=4)
                    d = p_l * fs[fb, i, sel, :] + q_l * xs[fb, i, sel, :] + r_l
                    if rho == 0:
                        placed(lupper, f, b, 1, i, d)
                        d = jnp.where(row == 63, 0.0, pltpu.roll(d, 63, 0))
                        placed(llower, f, b, 1, i, d)
                    elif rho == 3:
                        placed(llower, f, b, 0, i, d)
                        d = jnp.where(row == 0, 0.0, pltpu.roll(d, 1, 0))
                        placed(lupper, f, b, 0, i, d)
                    else:
                        placed(lmiddle, f, b, rho - 1, i, d)

    def conv(f, first, last, left, weight, result):
        width = weight.shape[1] // 3
        at = slice(width * first, width * last + width)
        result[320 * f : 320 * f + 320, at] = jnp.dot(
            left[f], weight[:, at], preferred_element_type=F32
        )

    def conv_middle(f, first, last):
        conv(f, first, last, lmiddle, bmiddle, ymiddle)

    def conv_ends(f, first, last):
        conv(f, first, last, lupper, bupper, yupper)
        conv(f, first, last, llower, blower, ylower)

    ln = iota((64, 128), 1)
    lo64 = ln < 64
    odd = lax.rem(ln, 2) == 1
    upper = lax.rem(lax.div(ln, 2), 2) == 0

    def taken(f, dt, b):
        r = slice(64 * (5 * f + b), 64 * (5 * f + b) + 64)
        narrow = slice(128 * dt, 128 * dt + 128)
        return (
            yupper[r, narrow] + ymiddle[r, 256 * dt : 256 * dt + 128],
            ylower[r, narrow] + ymiddle[r, 256 * dt + 128 : 256 * dt + 256],
        )

    def tokens(group, t, terms):
        cc = []
        for b in range(5):
            u, v = taken(*terms[0], b)
            for term in terms[1:]:
                more = taken(*term, b)
                u, v = u + more[0], v + more[1]
            cc.append(jnp.where(upper, u + pltpu.roll(u, 126, 1), v + pltpu.roll(v, 2, 1)))
        r1 = pltpu.roll(cc[1], 64, 1)
        r3 = pltpu.roll(cc[3], 64, 1)
        v0 = jnp.where(
            lo64, cc[0] + jnp.where(odd, r1, 0.0), r1 + jnp.where(odd, cc[2], cc[0])
        )
        v1 = jnp.where(
            lo64, cc[2] + jnp.where(odd, r3, r1), r3 + jnp.where(odd, cc[4], cc[2])
        )
        v2 = jnp.where(lo64, cc[4] + jnp.where(odd, 0.0, r3), jnp.where(odd, cc[0], cc[4]))
        for i, v in enumerate((v0, v1, v2)):
            tok[group, 8 * t : 8 * t + 8, :, 128 * i : 128 * i + 128] = v.reshape(8, 8, 128)

    def own_copy(j, at):
        return remote(tok.at[0, j], trecv.at[0, at], tks.at[0, j], tkr.at[0, at], (tm, j))

    def span_copy(j, at):
        return remote(tok.at[1, j], trecv.at[1, at], tks.at[1, j], tkr.at[1, at], (below, j))

    def owners(t):
        return tuple(
            8 * t + 4 * lax.rem(x + a, 2) + lax.rem(y + b, 4) for b in (2, 1, 3, 0) for a in (1, 0)
        )

    def send_span(t):
        for j in owners(t):
            span_copy(j, tl).start()

    def send_own(t):
        for j in owners(t):

            @pl.when(j != tl)
            def _(j=j):
                own_copy(j, tl).start()

    left_side(0, (1, 2))
    conv_middle(0, 0, 1)
    left_side(0, (0, 3))
    conv_ends(0, 0, 1)
    left_side(1, (1, 2))
    conv_middle(1, 0, 0)
    left_side(1, (0, 3))
    tokens(1, 0, ((0, 0),))
    send_span(0)
    conv_ends(1, 0, 0)
    tokens(1, 1, ((0, 1), (1, 0)))
    send_span(1)
    conv_middle(0, 2, 2)
    conv_ends(0, 2, 2)
    conv_middle(1, 1, 2)
    conv_ends(1, 1, 2)
    tokens(0, 0, ((0, 2), (1, 1)))
    tokens(0, 1, ((1, 2),))
    send_own(0)
    send_own(1)
    trecv[0, tl] = tok[0, tl]

    for place in FARTHEST + ((0, 0),):
        j = tile_at(place)
        span_copy(j, j).wait_recv()
    for place in FARTHEST:
        j = tile_at(place)
        own_copy(j, j).wait_recv()

    def assemble():
        ln = iota((8, 128), 1)
        lo8 = ln < 64
        odd8 = lax.rem(ln, 2) == 1
        strips = []
        for j in range(16):
            strips.append(
                [
                    trecv[0, j, :, 128 * i : 128 * i + 128]
                    + jnp.where(tm < 7, trecv[1, j, :, 128 * i : 128 * i + 128], 0.0)
                    for i in range(3)
                ]
            )
        halo = [pltpu.roll(s[2], 64, 1) for s in strips]
        for j in range(16):
            if j > 0:
                strips[j][0] = strips[j][0] + jnp.where(lo8 & ~odd8, halo[j - 1], 0.0)
        done = []
        for j in range(16):
            v2 = strips[j][2]
            if j < 15:
                v2 = v2 + jnp.where(odd8, halo[j + 1], 0.0)
            done.append((strips[j][0], strips[j][1], v2))
        for pair in range(8):
            e = done[2 * pair]
            o = [pltpu.roll(v, 64, 1) for v in done[2 * pair + 1]]
            at = 640 * pair
            out[:, at : at + 128] = e[0]
            out[:, at + 128 : at + 256] = e[1]
            out[:, at + 256 : at + 384] = jnp.where(lo8, e[2], o[0])
            out[:, at + 384 : at + 512] = jnp.where(lo8, o[0], o[1])
            out[:, at + 512 : at + 640] = jnp.where(lo8, o[1], o[2])

    assemble()

    for half in range(2):
        for r, d in strips:
            strip_copy(half, r, d).wait_send()
        for r, d in partners:
            z_copy(half, r, d).wait_send()
        for d in range(1, 16):
            stat_copy(half, d).wait_send()
    for place in FARTHEST:
        own_copy(tile_at(place), tl).wait_send()
    for place in FARTHEST + ((0, 0),):
        span_copy(tile_at(place), tl).wait_send()


def body(pix_grad, frame_ids, pre_norm, gain, bias, out_weight, conv_weight, in_weight):
    hbm = pl.BlockSpec(memory_space=pltpu.HBM)
    smem = pl.BlockSpec(memory_space=pltpu.SMEM)
    dma = pltpu.SemaphoreType.DMA

    def kept(array):
        return pltpu.with_memory_space_constraint(array, pltpu.HBM)

    pix_grad = jnp.transpose(pix_grad, (0, 1, 3, 2))
    out_weight = out_weight.T
    gain = gain.reshape(1, 96)
    bias = bias.reshape(1, 96)
    return pl.pallas_call(
        kernel,
        out_shape=jax.ShapeDtypeStruct((8, 5120), F32),
        in_specs=[hbm, smem] + [hbm] * 6,
        out_specs=pl.BlockSpec(memory_space=pltpu.VMEM),
        scratch_shapes=[
            pltpu.VMEM((1, 96), F32),
            pltpu.VMEM((1, 96), F32),
            pltpu.VMEM((3, 96), BF16),
            pltpu.VMEM((16, 384), BF16),
            pltpu.VMEM((3, 320, 256), BF16),
            pltpu.VMEM((PIECES, 256, BLK), BF16),
            pltpu.VMEM((27, 96, 384), BF16),
            pltpu.VMEM((2, 16, 64, 128), BF16),
            pltpu.VMEM((2, 16, 64, 128), BF16),
            pltpu.VMEM((256, 512), BF16),
            pltpu.VMEM((2, 8, 2, 32, 128), F32),
            pltpu.VMEM((2, 8, 2, 32, 128), jnp.int16),
            pltpu.VMEM((2, 2, 4, 2, 32, 128), jnp.int16),
            pltpu.VMEM((2, 2, 256, 128), BF16),
            pltpu.VMEM((2, 5, 128, BLK), BF16),
            pltpu.VMEM((PIECES, 3, 256, 128), F32),
            pltpu.VMEM((PIECES, 3, 256, 128), F32),
            pltpu.VMEM((BLK, 128), BF16),
            pltpu.VMEM((128, BLK), BF16),
            pltpu.VMEM((8, BLK), F32),
            pltpu.VMEM((2, 8, 128), F32),
            pltpu.VMEM((2, 16, 8, 128), F32),
            pltpu.VMEM((8, 128), F32),
            pltpu.VMEM((8, BLK), F32),
            pltpu.VMEM((27, 96, 128), F32),
            pltpu.VMEM((2 * BLK, BLK), BF16),
            pltpu.VMEM((2 * BLK, 2 * BLK), BF16),
            pltpu.VMEM((2 * BLK, BLK), BF16),
            pltpu.VMEM((2, 320, 2 * BLK), BF16),
            pltpu.VMEM((2, 320, 2 * BLK), BF16),
            pltpu.VMEM((2, 320, 2 * BLK), BF16),
            pltpu.VMEM((640, BLK), F32),
            pltpu.VMEM((640, 2 * BLK), F32),
            pltpu.VMEM((640, BLK), F32),
            pltpu.VMEM((2, 16, 8, BLK), F32),
            pltpu.VMEM((2, 16, 8, BLK), F32),
            pltpu.SemaphoreType.REGULAR,
            dma,
            dma((PIECES,)),
            dma,
            dma((4,)),
            dma((2, 2, 16)),
            dma((2, 2, 16)),
            dma((2, 2, 4)),
            dma((2, 2, 4)),
            dma((2, 16)),
            dma((2, 16)),
            dma((2, 16)),
            dma((2, 16)),
        ],
        compiler_params=pltpu.CompilerParams(
            collective_id=0, has_side_effects=True, vmem_limit_bytes=50 * 1024 * 1024
        ),
    )(
        kept(pix_grad),
        frame_ids,
        kept(pre_norm),
        kept(gain),
        kept(bias),
        kept(out_weight),
        kept(conv_weight),
        kept(in_weight),
    )


def solution(mesh):
    return jax.shard_map(
        body,
        mesh=mesh,
        in_specs=(
            P(("tm", "tile"), None, None, None),
            P(("tm", "tile")),
            P("tm", None, "tile"),
            P(),
            P(),
            P(),
            P(),
            P(),
        ),
        out_specs=P(("tm", "tile"), None),
        check_vma=False,
    )
```

```python
import jax
import jax.numpy as jnp
from jax import lax
from jax.experimental import pallas as pl
from jax.experimental.pallas import tpu as pltpu
from jax.sharding import PartitionSpec as P

MESH = pl.DeviceIdType.MESH
F32 = jnp.float32
BF16 = jnp.bfloat16
COUNT = 256.0 * 320.0 * 3.0
EPS = 1e-05
EIGHTHS = 8.0 / 0.6931471805599453
RANGE = 32700.0
BLK = 384
NEAR = ((2, 0), (0, 2), (1, 0), (0, 1), (3, 0), (0, 3))
PEERS = NEAR + ((1, 2), (3, 2), (2, 1), (2, 3), (2, 2), (1, 1), (3, 3), (1, 3), (3, 1))
FARTHEST = (
    (2, 2), (1, 2), (3, 2), (2, 1), (2, 3), (1, 1), (3, 3), (1, 3),
    (3, 1), (2, 0), (0, 2), (0, 1), (1, 0), (0, 3), (3, 0),
)
DXH = ((0, 0), (0, 1), (0, 2), (1, 2), (1, 3), (1, 4))
PIECES = 10


def iota(shape, dim):
    return lax.broadcasted_iota(jnp.int32, shape, dim)


def exact_dot(v, ones):
    top = v.astype(BF16).astype(F32)
    mid = (v - top).astype(BF16).astype(F32)
    parts = jnp.concatenate([top, mid, v - top - mid], axis=0).astype(BF16)
    w = jnp.dot(parts, ones, preferred_element_type=F32)
    n = v.shape[0]
    return w[0:n] + (w[n : 2 * n] + w[2 * n : 3 * n])


def remote(src, dst, send_sem, recv_sem, device):
    return pltpu.make_async_remote_copy(
        src_ref=src,
        dst_ref=dst,
        send_sem=send_sem,
        recv_sem=recv_sem,
        device_id=device,
        device_id_type=MESH,
    )


def kernel(
    pix_hbm,
    fid,
    x_hbm,
    gain_hbm,
    bias_hbm,
    ow_hbm,
    cw_hbm,
    iw_hbm,
    out,
    gain,
    bias,
    ow,
    iw,
    pixv,
    xb,
    cwv,
    sbuf,
    rbuf,
    picks,
    sums,
    packs,
    zbuf,
    dpx,
    rmat,
    xs,
    fs,
    gmat,
    emat,
    stin,
    stsend,
    strecv,
    table,
    cst,
    gred,
    bupper,
    bmiddle,
    blower,
    lupper,
    lmiddle,
    llower,
    yupper,
    ymiddle,
    ylower,
    tok,
    trecv,
    ready_sem,
    pix_sem,
    x_sem,
    cw_sem,
    small_sem,
    s1s,
    s1r,
    zs,
    zr,
    sts,
    strs,
    tks,
    tkr,
):
    tm = lax.axis_index("tm")
    tl = lax.axis_index("tile")
    z = lax.div(tm, 2)
    c = lax.rem(tm, 2)
    below = lax.rem(tm + 7, 8)
    x = lax.div(tl, 4)
    y = lax.rem(tl, 4)

    def tile_at(place):
        return lax.rem(x + place[0], 4) * 4 + lax.rem(y + place[1], 4)


    barrier = pltpu.get_barrier_semaphore()

    def greet(device):
        pl.semaphore_signal(barrier, inc=1, device_id=device, device_id_type=MESH)

    for place in NEAR:
        greet((tm, tile_at(place)))
        greet((tm + 1 - 2 * c, tile_at(place)))
    for d in (2, 1, 3):
        for r in range(2):
            greet((lax.rem(z + d, 4) * 2 + lax.rem(c + r, 2), tl))
    greet((tm + 1 - 2 * c, tl))

    pix_cp = pltpu.make_async_copy(pix_hbm.at[0], pixv, pix_sem)
    pix_cp.start()
    def pack():
        r = iota((256, 240), 0)
        m = iota((256, 240), 1)
        slot = lax.rem(r, 32)
        col = 20 * lax.div(r, 64) + 10 * lax.div(lax.rem(r, 64), 32) + lax.rem(slot, 10)
        hit = (slot < 30) & (m == 80 * lax.div(slot, 10) + col)
        pick = jnp.where(hit, 1.0, 0.0).astype(BF16)
        frame_id = fid[0].astype(F32)
        spare = lax.rem(iota((256, 256), 0), 32) >= 30
        pix_cp.wait()
        for n in range(4):
            stack = jnp.concatenate(
                [pixv[k, 80 * n : 80 * n + 80, :] for k in range(3)], axis=0
            )
            rows = jnp.dot(pick, stack, preferred_element_type=F32)
            rows = jnp.where(spare, frame_id, rows).astype(BF16)
            for jj in range(4):
                for ch in range(2):
                    sbuf[ch, 4 * n + jj] = rows[
                        64 * jj : 64 * jj + 64, 128 * ch : 128 * ch + 128
                    ]

    pack()
    x_cps = []
    for f in range(2):
        for b in range(5):
            cp = pltpu.make_async_copy(
                x_hbm.at[f, :, pl.ds(BLK * b, BLK)], xb.at[f * 5 + b], x_sem.at[f * 5 + b]
            )
            cp.start()
            x_cps.append(cp)
    small_cps = []
    for i, (src, dst) in enumerate(
        ((gain_hbm, gain), (bias_hbm, bias), (ow_hbm, ow), (iw_hbm, iw))
    ):
        cp = pltpu.make_async_copy(src, dst, small_sem.at[i])
        cp.start()
        small_cps.append(cp)
    cw_cp = pltpu.make_async_copy(cw_hbm, cwv, cw_sem)
    cw_cp.start()
    def strip_copy(half, r, d):
        j = tl if d == 0 else tile_at(PEERS[d - 1])
        h = lax.rem(c + r, 2)
        rows = pl.ds(32 * half, 32)
        return remote(
            sbuf.at[h, j, rows],
            rbuf.at[r, d, rows],
            s1s.at[half, r, d],
            s1r.at[half, r, d],
            (2 * z + h, j),
        )

    strips = tuple((r, d) for d in range(1, 16) for r in range(2)) + ((1, 0),)

    def strips_sent(some):
        for half in range(2):
            for r, d in some:
                strip_copy(half, r, d).start()

    pl.semaphore_wait(barrier, 12 + 6 + 1)
    for place in ((2, 0), (1, 0), (3, 0)):
        pl.semaphore_signal(
            ready_sem, inc=1, device_id=(tm, tile_at(place)), device_id_type=MESH
        )
    strips_sent(strips[0:12] + strips[-1:])
    rbuf[0, 0] = sbuf[c, tl]

    pl.semaphore_wait(ready_sem, 3)
    strips_sent(strips[12:30])

    lam = iota((BLK, 128), 0)
    chan = iota((BLK, 128), 1)
    same = (lax.div(lax.rem(lam, 96), 3) == lax.div(chan, 3)) & (chan < 96)
    gmat[...] = jnp.where(same, 1.0, 0.0).astype(BF16)
    emat[...] = jnp.where(
        lax.rem(iota((128, BLK), 1), 96) == iota((128, BLK), 0), 1.0, 0.0
    ).astype(BF16)

    for cp in x_cps:
        cp.wait()

    def fold(v):
        return v.reshape(v.shape[0] // 8, 8, v.shape[1]).sum(axis=0)

    def stats():
        stin[...] = jnp.zeros((8, BLK), F32)
        for f in range(2):

            def stat_step(i, carry, f=f):
                s, ss = carry
                b = lax.div(i, 8)
                r = pl.multiple_of(lax.rem(i, 8) * 32, 32)
                v = xb[f * 5 + b, pl.ds(r, 32), :].astype(F32)
                return s + fold(v), ss + fold(v * v)

            zero = jnp.zeros((8, BLK), F32)
            s, ss = lax.fori_loop(0, 40, stat_step, (zero, zero))
            stin[2 * f : 2 * f + 1, :] = jnp.sum(s, axis=0, keepdims=True)
            stin[2 * f + 1 : 2 * f + 2, :] = jnp.sum(ss, axis=0, keepdims=True)

    stats()

    def stat_copy(which, d):
        return remote(
            stsend.at[which],
            strecv.at[which, d],
            sts.at[which, d],
            strs.at[which, d],
            (tm, tile_at(FARTHEST[d - 1])),
        )

    def stat_send(which):
        red = exact_dot(stin[...], gmat[...])
        stsend[which] = red
        strecv[which, 0] = red
        for d in range(1, 16):
            stat_copy(which, d).start()

    def stat_wait(which):
        for d in range(1, 16):
            stat_copy(which, d).wait_recv()
        return jnp.sum(strecv[which], axis=0)

    stat_send(0)

    def colours():
        owe = jnp.dot(ow[...], emat[0:96, :], preferred_element_type=F32)
        q = iota((32, BLK), 0)
        kq = lax.div(q, 10)
        wq = lax.rem(q, 10)
        wl = lax.div(iota((32, BLK), 1), 96)
        small = jnp.where(
            kq == 0,
            owe[0:1, :],
            jnp.where(kq == 1, owe[1:2, :], jnp.where(kq == 2, owe[2:3, :], 0.0)),
        )
        for half, b in DXH:
            core = jnp.where(wq + 10 * half == wl + 4 * b, small, 0.0).astype(BF16)
            for part in range(3):
                rmat[half, b, 32 * part : 32 * part + 32, :] = core
            rmat[half, b, 96:128, :] = jnp.zeros((32, BLK), BF16)

    for cp in small_cps:
        cp.wait()
    colours()


    spread = jnp.where(lax.div(lax.rem(iota((128, 16), 0), 64), 4) == iota((128, 16), 1), 1.0, 0.0)

    def taps_reduced():
        iwr = jnp.dot(spread.astype(BF16), iw[...], preferred_element_type=F32).T.astype(BF16)
        for i in range(9):
            gred[3 * i : 3 * i + 3] = jnp.dot(
                cwv[3 * i : 3 * i + 3].reshape(288, BLK), iwr, preferred_element_type=F32
            ).reshape(3, 96, 128)

    cw_cp.wait()
    taps_reduced()

    ln = iota((16, 128), 1)
    main = ln < 64
    b0 = lax.rem(ln, 2) == 0
    a0 = lax.rem(lax.div(ln, 2), 2) == 0

    def combine(mc, _):
        r = pl.multiple_of(mc * 16, 16)
        for dt in range(3):
            cols = []
            for dh in range(3):
                g = [gred[9 * dt + 3 * dh + dw, pl.ds(r, 16), :] for dw in range(3)]
                g01 = g[0] + g[1]
                g12 = g[1] + g[2]
                zero = jnp.zeros_like(g01)
                cols.append(
                    (
                        jnp.where(main, jnp.where(b0, g12, zero), jnp.where(b0, zero, g[0])),
                        jnp.where(main, jnp.where(b0, g01, g[2]), zero),
                        jnp.where(main, jnp.where(b0, g[0], g12), zero),
                        jnp.where(main, jnp.where(b0, zero, g01), jnp.where(b0, g[2], zero)),
                    )
                )
            for w in range(4):
                h0, h1, h2 = (cols[dh][w] for dh in range(3))
                h01 = h0 + h1
                h12 = h1 + h2
                for value, ref, t, at in (
                    (h2, bupper, 0, 128 * dt),
                    (h12, bupper, 1, 128 * dt),
                    (h01, bmiddle, 0, 256 * dt),
                    (h0, bmiddle, 1, 256 * dt),
                    (h2, bmiddle, 0, 256 * dt + 128),
                    (h12, bmiddle, 1, 256 * dt + 128),
                    (h01, blower, 0, 128 * dt),
                    (h0, blower, 1, 128 * dt),
                ):
                    row = pl.multiple_of(t * BLK + w * 96 + r, 16)
                    top = value.astype(BF16).astype(F32)
                    rest = value - top
                    first = a0 if at % 256 == 0 and ref is bmiddle or ref is bupper else ~a0
                    ref[pl.ds(row, 16), at : at + 128] = jnp.where(first, top, rest).astype(BF16)
        return 0

    def weights():
        lax.fori_loop(0, 6, combine, 0)

    weights()

    def frame_picks():
        for r in range(2):
            ids = rbuf[r, :, 16:32, :].astype(F32)
            ids = jnp.broadcast_to(ids[:, 15:16, :], (16, 16, 128)).reshape(256, 128)
            ids = jnp.concatenate([ids, ids], axis=1)
            at = iota((256, 256), 1)
            hit = (ids == lax.div(at, 16).astype(F32)) & (
                lax.rem(iota((256, 256), 0), 16) == lax.rem(at, 16)
            )
            picks[:, 256 * r : 256 * r + 256] = jnp.where(hit, 1.0, 0.0).T.astype(BF16)

    def frame_sums(half):
        stack = jnp.concatenate(
            [rbuf[:, :, 16 * g : 16 * g + 16, :].reshape(512, 128) for g in (2 * half, 2 * half + 1)],
            axis=1,
        )
        total = jnp.dot(picks[...], stack, preferred_element_type=F32)
        for g in range(2):
            v = total[:, 128 * g : 128 * g + 128].reshape(8, 2, 16, 128)
            if g == 1:
                v = jnp.where(iota(v.shape, 2) >= 14, 0.0, v)
            sums[half, :, :, 16 * g : 16 * g + 16, :] = v

    def packed(half):
        for owner in range(8):
            v = sums[half, owner]
            largest = jnp.max(jnp.maximum(v[0], v[1]), axis=0, keepdims=True)
            smallest = jnp.min(jnp.minimum(v[0], v[1]), axis=0, keepdims=True)
            largest = jnp.maximum(jnp.maximum(largest, -smallest), 1e-20)
            step = jnp.floor(jnp.log(largest) * EIGHTHS) + 2.0
            scale = RANGE * jnp.exp(step * (-1.0 / EIGHTHS))
            w = jnp.round(v * scale[None])
            w = jnp.where(iota(v.shape, 1) >= 30, step[None], w)
            packs[half, owner] = w.astype(jnp.int32).astype(jnp.int16)

    def unpacked(v):
        v = v.astype(jnp.int32).astype(F32)
        return v * (jnp.exp(v[:, 30:31, :] * (1.0 / EIGHTHS)) * (1.0 / RANGE))

    def z_copy(half, r, d):
        owner = lax.rem(z + d, 4) * 2 + lax.rem(c + r, 2)
        return remote(
            packs.at[half, owner],
            zbuf.at[half, r, d],
            zs.at[half, r, d],
            zr.at[half, r, d],
            (owner, tl),
        )

    partners = tuple((r, d) for d in (2, 1, 3, 0) for r in (1, 0) if r + d > 0)

    for half in range(2):
        for r, d in strips:
            strip_copy(half, r, d).wait_recv()
        if half == 0:
            frame_picks()
        frame_sums(half)
        packed(half)
        for r, d in partners:
            z_copy(half, r, d).start()

    tot = stat_wait(0) / COUNT
    rows = []
    for f in range(2):
        mean = tot[2 * f : 2 * f + 1]
        meansq = tot[2 * f + 1 : 2 * f + 2]
        rstd = lax.rsqrt(meansq - mean * mean + EPS)
        rows.append((mean, rstd))
    table[...] = jnp.zeros((8, 128), F32)
    for f in range(2):
        table[f : f + 1, :] = rows[f][0]
        table[6 + f : 7 + f, 0:96] = 0.5 * rows[f][1][:, 0:96] * gain[...]
    table[4:5, 0:96] = gain[...]
    table[5:6, 0:96] = 0.5 * bias[...]
    cst[...] = exact_dot(table[...], emat[...])

    def factor():
        for f in range(2):
            mean_l = cst[f : f + 1, :]
            a_l = cst[6 + f : 7 + f, :]
            hb_l = cst[5:6, :]
            g2_l = 0.5 * cst[4:5, :]

            def factor_step(i, _, f=f, mean_l=mean_l, a_l=a_l, hb_l=hb_l, g2_l=g2_l):
                b = lax.div(i, 8)
                r = pl.multiple_of(lax.rem(i, 8) * 32, 32)
                v = xb[f * 5 + b, pl.ds(r, 32), :].astype(F32) - mean_l
                u = v * a_l + hb_l
                h = jnp.tanh(u)
                w = (1.0 + u * (1.0 - h)) * ((1.0 + h) * g2_l)
                for i in range(3):
                    xs[f * 5 + b, i, pl.ds(r, 32), :] = v[:, 128 * i : 128 * i + 128]
                    fs[f * 5 + b, i, pl.ds(r, 32), :] = w[:, 128 * i : 128 * i + 128]
                return 0

            lax.fori_loop(0, 40, factor_step, 0)

    factor()

    def frame_rows(half):
        for r in range(2):
            dp = sums[half, tm] if r == 0 else unpacked(zbuf[half, 1, 0])
            for d in range(1, 4):
                dp = dp + unpacked(zbuf[half, r, d])
            for f in range(2):
                top = dp[f].astype(BF16).astype(F32)
                mid = (dp[f] - top).astype(BF16).astype(F32)
                rest = dp[f] - top - mid
                parts = jnp.concatenate([top, mid, rest, jnp.zeros_like(rest)], axis=0).T
                dpx[half, lax.rem(c + r, 2), 128 * f : 128 * f + 128, :] = parts.astype(BF16)

    def dxh(blocks, carry):
        for b in blocks:
            for rows_at in range(2):
                da = None
                for half in range(2):
                    if (half, b) in DXH:
                        v = jnp.dot(
                            dpx[half, rows_at], rmat[half, b], preferred_element_type=F32
                        )
                        da = v if da is None else da + v
                new = []
                for f in range(2):
                    at = pl.ds(128 * rows_at, 128)
                    s, sx = [], []
                    for i in range(3):
                        v = da[128 * f : 128 * f + 128, 128 * i : 128 * i + 128]
                        v = v * fs[f * 5 + b, i, at, :]
                        fs[f * 5 + b, i, at, :] = v
                        s.append(carry[6 * f + i] + fold(v))
                        sx.append(carry[6 * f + 3 + i] + fold(v * xs[f * 5 + b, i, at, :]))
                    new += s + sx
                carry = tuple(new)
        return carry

    carry = tuple(jnp.zeros((8, 128), F32) for _ in range(12))
    for half in range(2):
        for r, d in partners:
            z_copy(half, r, d).wait_recv()
        frame_rows(half)
        carry = dxh((0, 1) if half == 0 else (2, 3, 4), carry)

    def dxh_sums():
        for i in range(12):
            stin[i // 3 : i // 3 + 1, 128 * (i % 3) : 128 * (i % 3) + 128] = jnp.sum(
                carry[i], axis=0, keepdims=True
            )

    dxh_sums()
    stat_send(1)
    tot = stat_wait(1) / COUNT
    terms = []
    for f in range(2):
        rstd = rows[f][1]
        first = tot[2 * f : 2 * f + 1]
        second = tot[2 * f + 1 : 2 * f + 2] * rstd
        terms += [rstd, -rstd * rstd * second, -rstd * first, jnp.zeros_like(rstd)]
    cst[...] = exact_dot(jnp.concatenate(terms, axis=0), emat[...])

    def placed(left, f, b, tap, i, d):
        at = BLK * tap + 128 * i
        left[f, 64 * b : 64 * b + 64, at : at + 128] = d.astype(BF16)

    def left_side(f, rows):
        row = iota((64, 128), 0)
        for i in range(3):
            ls = slice(128 * i, 128 * i + 128)
            p_l = cst[4 * f : 4 * f + 1, ls]
            q_l = cst[4 * f + 1 : 4 * f + 2, ls]
            r_l = cst[4 * f + 2 : 4 * f + 3, ls]
            for b in range(5):
                fb = f * 5 + b
                for rho in rows:
                    sel = pl.ds(rho, 64, stride=4)
                    d = p_l * fs[fb, i, sel, :] + q_l * xs[fb, i, sel, :] + r_l
                    if rho == 0:
                        placed(lupper, f, b, 1, i, d)
                        d = jnp.where(row == 63, 0.0, pltpu.roll(d, 63, 0))
                        placed(llower, f, b, 1, i, d)
                    elif rho == 3:
                        placed(llower, f, b, 0, i, d)
                        d = jnp.where(row == 0, 0.0, pltpu.roll(d, 1, 0))
                        placed(lupper, f, b, 0, i, d)
                    else:
                        placed(lmiddle, f, b, rho - 1, i, d)

    def conv(f, first, last, left, weight, result):
        width = weight.shape[1] // 3
        at = slice(width * first, width * last + width)
        result[320 * f : 320 * f + 320, at] = jnp.dot(
            left[f], weight[:, at], preferred_element_type=F32
        )

    def conv_middle(f, first, last):
        conv(f, first, last, lmiddle, bmiddle, ymiddle)

    def conv_ends(f, first, last):
        conv(f, first, last, lupper, bupper, yupper)
        conv(f, first, last, llower, blower, ylower)

    ln = iota((64, 128), 1)
    lo64 = ln < 64
    odd = lax.rem(ln, 2) == 1
    upper = lax.rem(lax.div(ln, 2), 2) == 0

    def taken(f, dt, b):
        r = slice(64 * (5 * f + b), 64 * (5 * f + b) + 64)
        narrow = slice(128 * dt, 128 * dt + 128)
        return (
            yupper[r, narrow] + ymiddle[r, 256 * dt : 256 * dt + 128],
            ylower[r, narrow] + ymiddle[r, 256 * dt + 128 : 256 * dt + 256],
        )

    def tokens(group, t, terms):
        cc = []
        for b in range(5):
            u, v = taken(*terms[0], b)
            for term in terms[1:]:
                more = taken(*term, b)
                u, v = u + more[0], v + more[1]
            cc.append(jnp.where(upper, u + pltpu.roll(u, 126, 1), v + pltpu.roll(v, 2, 1)))
        r1 = pltpu.roll(cc[1], 64, 1)
        r3 = pltpu.roll(cc[3], 64, 1)
        v0 = jnp.where(
            lo64, cc[0] + jnp.where(odd, r1, 0.0), r1 + jnp.where(odd, cc[2], cc[0])
        )
        v1 = jnp.where(
            lo64, cc[2] + jnp.where(odd, r3, r1), r3 + jnp.where(odd, cc[4], cc[2])
        )
        v2 = jnp.where(lo64, cc[4] + jnp.where(odd, 0.0, r3), jnp.where(odd, cc[0], cc[4]))
        for i, v in enumerate((v0, v1, v2)):
            tok[group, 8 * t : 8 * t + 8, :, 128 * i : 128 * i + 128] = v.reshape(8, 8, 128)

    def own_copy(j, at):
        return remote(tok.at[0, j], trecv.at[0, at], tks.at[0, j], tkr.at[0, at], (tm, j))

    def span_copy(j, at):
        return remote(tok.at[1, j], trecv.at[1, at], tks.at[1, j], tkr.at[1, at], (below, j))

    def owners(t):
        return tuple(
            8 * t + 4 * lax.rem(x + a, 2) + lax.rem(y + b, 4) for b in (2, 1, 3, 0) for a in (1, 0)
        )

    def send_span(t):
        for j in owners(t):
            span_copy(j, tl).start()

    def send_own(t):
        for j in owners(t):

            @pl.when(j != tl)
            def _(j=j):
                own_copy(j, tl).start()

    left_side(0, (1, 2))
    conv_middle(0, 0, 1)
    left_side(0, (0, 3))
    conv_ends(0, 0, 1)
    tokens(1, 0, ((0, 0),))
    send_span(0)
    left_side(1, (1, 2))
    conv_middle(1, 0, 0)
    left_side(1, (0, 3))
    conv_ends(1, 0, 0)
    tokens(1, 1, ((0, 1), (1, 0)))
    send_span(1)
    conv_middle(0, 2, 2)
    conv_ends(0, 2, 2)
    conv_middle(1, 1, 2)
    conv_ends(1, 1, 2)
    tokens(0, 0, ((0, 2), (1, 1)))
    send_own(0)
    tokens(0, 1, ((1, 2),))
    send_own(1)
    trecv[0, tl] = tok[0, tl]

    for place in FARTHEST + ((0, 0),):
        j = tile_at(place)
        span_copy(j, j).wait_recv()
    for place in FARTHEST:
        j = tile_at(place)
        own_copy(j, j).wait_recv()

    def assemble():
        ln = iota((8, 128), 1)
        lo8 = ln < 64
        odd8 = lax.rem(ln, 2) == 1
        strips = []
        for j in range(16):
            strips.append(
                [
                    trecv[0, j, :, 128 * i : 128 * i + 128]
                    + jnp.where(tm < 7, trecv[1, j, :, 128 * i : 128 * i + 128], 0.0)
                    for i in range(3)
                ]
            )
        halo = [pltpu.roll(s[2], 64, 1) for s in strips]
        for j in range(16):
            if j > 0:
                strips[j][0] = strips[j][0] + jnp.where(lo8 & ~odd8, halo[j - 1], 0.0)
        done = []
        for j in range(16):
            v2 = strips[j][2]
            if j < 15:
                v2 = v2 + jnp.where(odd8, halo[j + 1], 0.0)
            done.append((strips[j][0], strips[j][1], v2))
        for pair in range(8):
            e = done[2 * pair]
            o = [pltpu.roll(v, 64, 1) for v in done[2 * pair + 1]]
            at = 640 * pair
            out[:, at : at + 128] = e[0]
            out[:, at + 128 : at + 256] = e[1]
            out[:, at + 256 : at + 384] = jnp.where(lo8, e[2], o[0])
            out[:, at + 384 : at + 512] = jnp.where(lo8, o[0], o[1])
            out[:, at + 512 : at + 640] = jnp.where(lo8, o[1], o[2])

    assemble()

    for half in range(2):
        for r, d in strips:
            strip_copy(half, r, d).wait_send()
        for r, d in partners:
            z_copy(half, r, d).wait_send()
        for d in range(1, 16):
            stat_copy(half, d).wait_send()
    for place in FARTHEST:
        own_copy(tile_at(place), tl).wait_send()
    for place in FARTHEST + ((0, 0),):
        span_copy(tile_at(place), tl).wait_send()


def body(pix_grad, frame_ids, pre_norm, gain, bias, out_weight, conv_weight, in_weight):
    hbm = pl.BlockSpec(memory_space=pltpu.HBM)
    smem = pl.BlockSpec(memory_space=pltpu.SMEM)
    dma = pltpu.SemaphoreType.DMA

    def kept(array):
        return pltpu.with_memory_space_constraint(array, pltpu.HBM)

    pix_grad = jnp.transpose(pix_grad, (0, 1, 3, 2))
    out_weight = out_weight.T
    gain = gain.reshape(1, 96)
    bias = bias.reshape(1, 96)
    return pl.pallas_call(
        kernel,
        out_shape=jax.ShapeDtypeStruct((8, 5120), F32),
        in_specs=[hbm, smem] + [hbm] * 6,
        out_specs=pl.BlockSpec(memory_space=pltpu.VMEM),
        scratch_shapes=[
            pltpu.VMEM((1, 96), F32),
            pltpu.VMEM((1, 96), F32),
            pltpu.VMEM((3, 96), BF16),
            pltpu.VMEM((16, 384), BF16),
            pltpu.VMEM((3, 320, 256), BF16),
            pltpu.VMEM((PIECES, 256, BLK), BF16),
            pltpu.VMEM((27, 96, 384), BF16),
            pltpu.VMEM((2, 16, 64, 128), BF16),
            pltpu.VMEM((2, 16, 64, 128), BF16),
            pltpu.VMEM((256, 512), BF16),
            pltpu.VMEM((2, 8, 2, 32, 128), F32),
            pltpu.VMEM((2, 8, 2, 32, 128), jnp.int16),
            pltpu.VMEM((2, 2, 4, 2, 32, 128), jnp.int16),
            pltpu.VMEM((2, 2, 256, 128), BF16),
            pltpu.VMEM((2, 5, 128, BLK), BF16),
            pltpu.VMEM((PIECES, 3, 256, 128), F32),
            pltpu.VMEM((PIECES, 3, 256, 128), F32),
            pltpu.VMEM((BLK, 128), BF16),
            pltpu.VMEM((128, BLK), BF16),
            pltpu.VMEM((8, BLK), F32),
            pltpu.VMEM((2, 8, 128), F32),
            pltpu.VMEM((2, 16, 8, 128), F32),
            pltpu.VMEM((8, 128), F32),
            pltpu.VMEM((8, BLK), F32),
            pltpu.VMEM((27, 96, 128), F32),
            pltpu.VMEM((2 * BLK, BLK), BF16),
            pltpu.VMEM((2 * BLK, 2 * BLK), BF16),
            pltpu.VMEM((2 * BLK, BLK), BF16),
            pltpu.VMEM((2, 320, 2 * BLK), BF16),
            pltpu.VMEM((2, 320, 2 * BLK), BF16),
            pltpu.VMEM((2, 320, 2 * BLK), BF16),
            pltpu.VMEM((640, BLK), F32),
            pltpu.VMEM((640, 2 * BLK), F32),
            pltpu.VMEM((640, BLK), F32),
            pltpu.VMEM((2, 16, 8, BLK), F32),
            pltpu.VMEM((2, 16, 8, BLK), F32),
            pltpu.SemaphoreType.REGULAR,
            dma,
            dma((PIECES,)),
            dma,
            dma((4,)),
            dma((2, 2, 16)),
            dma((2, 2, 16)),
            dma((2, 2, 4)),
            dma((2, 2, 4)),
            dma((2, 16)),
            dma((2, 16)),
            dma((2, 16)),
            dma((2, 16)),
        ],
        compiler_params=pltpu.CompilerParams(
            collective_id=0, has_side_effects=True, vmem_limit_bytes=50 * 1024 * 1024
        ),
    )(
        kept(pix_grad),
        frame_ids,
        kept(pre_norm),
        kept(gain),
        kept(bias),
        kept(out_weight),
        kept(conv_weight),
        kept(in_weight),
    )


def solution(mesh):
    return jax.shard_map(
        body,
        mesh=mesh,
        in_specs=(
            P(("tm", "tile"), None, None, None),
            P(("tm", "tile")),
            P("tm", None, "tile"),
            P(),
            P(),
            P(),
            P(),
            P(),
        ),
        out_specs=P(("tm", "tile"), None),
        check_vma=False,
    )
```

```python
import jax
import jax.numpy as jnp
from jax import lax
from jax.experimental import pallas as pl
from jax.experimental.pallas import tpu as pltpu
from jax.sharding import PartitionSpec as P

MESH = pl.DeviceIdType.MESH
F32 = jnp.float32
BF16 = jnp.bfloat16
COUNT = 256.0 * 320.0 * 3.0
EPS = 1e-05
EIGHTHS = 8.0 / 0.6931471805599453
RANGE = 32700.0
BLK = 384
NEAR = ((2, 0), (0, 2), (1, 0), (0, 1), (3, 0), (0, 3))
PEERS = NEAR + ((1, 2), (3, 2), (2, 1), (2, 3), (2, 2), (1, 1), (3, 3), (1, 3), (3, 1))
FARTHEST = (
    (2, 2), (1, 2), (3, 2), (2, 1), (2, 3), (1, 1), (3, 3), (1, 3),
    (3, 1), (2, 0), (0, 2), (0, 1), (1, 0), (0, 3), (3, 0),
)
DXH = ((0, 0), (0, 1), (0, 2), (1, 2), (1, 3), (1, 4))
PIECES = 10


def iota(shape, dim):
    return lax.broadcasted_iota(jnp.int32, shape, dim)


def exact_dot(v, ones):
    top = v.astype(BF16).astype(F32)
    mid = (v - top).astype(BF16).astype(F32)
    parts = jnp.concatenate([top, mid, v - top - mid], axis=0).astype(BF16)
    w = jnp.dot(parts, ones, preferred_element_type=F32)
    n = v.shape[0]
    return w[0:n] + (w[n : 2 * n] + w[2 * n : 3 * n])


def remote(src, dst, send_sem, recv_sem, device):
    return pltpu.make_async_remote_copy(
        src_ref=src,
        dst_ref=dst,
        send_sem=send_sem,
        recv_sem=recv_sem,
        device_id=device,
        device_id_type=MESH,
    )


def kernel(
    pix_hbm,
    fid,
    x_hbm,
    gain_hbm,
    bias_hbm,
    ow_hbm,
    cw_hbm,
    iw_hbm,
    out,
    gain,
    bias,
    ow,
    iw,
    pixv,
    xb,
    cwv,
    sbuf,
    rbuf,
    picks,
    sums,
    packs,
    zbuf,
    dpx,
    rmat,
    xs,
    fs,
    gmat,
    emat,
    stin,
    stsend,
    strecv,
    table,
    cst,
    gred,
    bupper,
    bmiddle,
    blower,
    lupper,
    lmiddle,
    llower,
    yupper,
    ymiddle,
    ylower,
    tok,
    trecv,
    ready_sem,
    pix_sem,
    x_sem,
    cw_sem,
    small_sem,
    s1s,
    s1r,
    zs,
    zr,
    sts,
    strs,
    tks,
    tkr,
):
    tm = lax.axis_index("tm")
    tl = lax.axis_index("tile")
    z = lax.div(tm, 2)
    c = lax.rem(tm, 2)
    below = lax.rem(tm + 7, 8)
    x = lax.div(tl, 4)
    y = lax.rem(tl, 4)

    def tile_at(place):
        return lax.rem(x + place[0], 4) * 4 + lax.rem(y + place[1], 4)


    barrier = pltpu.get_barrier_semaphore()

    def greet(device):
        pl.semaphore_signal(barrier, inc=1, device_id=device, device_id_type=MESH)

    for place in NEAR:
        greet((tm, tile_at(place)))
        greet((tm + 1 - 2 * c, tile_at(place)))
    for d in (2, 1, 3):
        for r in range(2):
            greet((lax.rem(z + d, 4) * 2 + lax.rem(c + r, 2), tl))
    greet((tm + 1 - 2 * c, tl))

    pix_cp = pltpu.make_async_copy(pix_hbm.at[0], pixv, pix_sem)
    pix_cp.start()
    def pack():
        r = iota((256, 240), 0)
        m = iota((256, 240), 1)
        slot = lax.rem(r, 32)
        col = 20 * lax.div(r, 64) + 10 * lax.div(lax.rem(r, 64), 32) + lax.rem(slot, 10)
        hit = (slot < 30) & (m == 80 * lax.div(slot, 10) + col)
        pick = jnp.where(hit, 1.0, 0.0).astype(BF16)
        frame_id = fid[0].astype(F32)
        spare = lax.rem(iota((256, 256), 0), 32) >= 30
        pix_cp.wait()
        for n in range(4):
            stack = jnp.concatenate(
                [pixv[k, 80 * n : 80 * n + 80, :] for k in range(3)], axis=0
            )
            rows = jnp.dot(pick, stack, preferred_element_type=F32)
            rows = jnp.where(spare, frame_id, rows).astype(BF16)
            for jj in range(4):
                for ch in range(2):
                    sbuf[ch, 4 * n + jj] = rows[
                        64 * jj : 64 * jj + 64, 128 * ch : 128 * ch + 128
                    ]

    pack()
    def strip_copy(half, r, d):
        j = tl if d == 0 else tile_at(PEERS[d - 1])
        h = lax.rem(c + r, 2)
        rows = pl.ds(32 * half, 32)
        return remote(
            sbuf.at[h, j, rows],
            rbuf.at[r, d, rows],
            s1s.at[half, r, d],
            s1r.at[half, r, d],
            (2 * z + h, j),
        )

    strips = tuple((r, d) for d in range(1, 16) for r in range(2)) + ((1, 0),)

    def strips_sent(some):
        for half in range(2):
            for r, d in some:
                strip_copy(half, r, d).start()

    pl.semaphore_wait(barrier, 12 + 6 + 1)
    for place in ((2, 0), (1, 0), (3, 0)):
        pl.semaphore_signal(
            ready_sem, inc=1, device_id=(tm, tile_at(place)), device_id_type=MESH
        )
    strips_sent(strips[0:12] + strips[-1:])
    rbuf[0, 0] = sbuf[c, tl]

    x_cps = []
    for f in range(2):
        for b in range(5):
            cp = pltpu.make_async_copy(
                x_hbm.at[f, :, pl.ds(BLK * b, BLK)], xb.at[f * 5 + b], x_sem.at[f * 5 + b]
            )
            cp.start()
            x_cps.append(cp)
    small_cps = []
    for i, (src, dst) in enumerate(
        ((gain_hbm, gain), (bias_hbm, bias), (ow_hbm, ow), (iw_hbm, iw))
    ):
        cp = pltpu.make_async_copy(src, dst, small_sem.at[i])
        cp.start()
        small_cps.append(cp)
    cw_cp = pltpu.make_async_copy(cw_hbm, cwv, cw_sem)
    cw_cp.start()

    pl.semaphore_wait(ready_sem, 3)
    strips_sent(strips[12:30])

    lam = iota((BLK, 128), 0)
    chan = iota((BLK, 128), 1)
    same = (lax.div(lax.rem(lam, 96), 3) == lax.div(chan, 3)) & (chan < 96)
    gmat[...] = jnp.where(same, 1.0, 0.0).astype(BF16)
    emat[...] = jnp.where(
        lax.rem(iota((128, BLK), 1), 96) == iota((128, BLK), 0), 1.0, 0.0
    ).astype(BF16)

    for cp in x_cps:
        cp.wait()

    def fold(v):
        return v.reshape(v.shape[0] // 8, 8, v.shape[1]).sum(axis=0)

    def stats():
        stin[...] = jnp.zeros((8, BLK), F32)
        for f in range(2):

            def stat_step(i, carry, f=f):
                s, ss = carry
                b = lax.div(i, 8)
                r = pl.multiple_of(lax.rem(i, 8) * 32, 32)
                v = xb[f * 5 + b, pl.ds(r, 32), :].astype(F32)
                return s + fold(v), ss + fold(v * v)

            zero = jnp.zeros((8, BLK), F32)
            s, ss = lax.fori_loop(0, 40, stat_step, (zero, zero))
            stin[2 * f : 2 * f + 1, :] = jnp.sum(s, axis=0, keepdims=True)
            stin[2 * f + 1 : 2 * f + 2, :] = jnp.sum(ss, axis=0, keepdims=True)

    stats()

    def stat_copy(which, d):
        return remote(
            stsend.at[which],
            strecv.at[which, d],
            sts.at[which, d],
            strs.at[which, d],
            (tm, tile_at(FARTHEST[d - 1])),
        )

    def stat_send(which):
        red = exact_dot(stin[...], gmat[...])
        stsend[which] = red
        strecv[which, 0] = red
        for d in range(1, 16):
            stat_copy(which, d).start()

    def stat_wait(which):
        for d in range(1, 16):
            stat_copy(which, d).wait_recv()
        return jnp.sum(strecv[which], axis=0)

    stat_send(0)

    def colours():
        owe = jnp.dot(ow[...], emat[0:96, :], preferred_element_type=F32)
        q = iota((32, BLK), 0)
        kq = lax.div(q, 10)
        wq = lax.rem(q, 10)
        wl = lax.div(iota((32, BLK), 1), 96)
        small = jnp.where(
            kq == 0,
            owe[0:1, :],
            jnp.where(kq == 1, owe[1:2, :], jnp.where(kq == 2, owe[2:3, :], 0.0)),
        )
        for half, b in DXH:
            core = jnp.where(wq + 10 * half == wl + 4 * b, small, 0.0).astype(BF16)
            for part in range(3):
                rmat[half, b, 32 * part : 32 * part + 32, :] = core
            rmat[half, b, 96:128, :] = jnp.zeros((32, BLK), BF16)

    for cp in small_cps:
        cp.wait()
    colours()


    spread = jnp.where(lax.div(lax.rem(iota((128, 16), 0), 64), 4) == iota((128, 16), 1), 1.0, 0.0)

    def taps_reduced():
        iwr = jnp.dot(spread.astype(BF16), iw[...], preferred_element_type=F32).T.astype(BF16)
        for i in range(9):
            gred[3 * i : 3 * i + 3] = jnp.dot(
                cwv[3 * i : 3 * i + 3].reshape(288, BLK), iwr, preferred_element_type=F32
            ).reshape(3, 96, 128)

    cw_cp.wait()
    taps_reduced()

    ln = iota((16, 128), 1)
    main = ln < 64
    b0 = lax.rem(ln, 2) == 0
    a0 = lax.rem(lax.div(ln, 2), 2) == 0

    def combine(mc, _):
        r = pl.multiple_of(mc * 16, 16)
        for dt in range(3):
            cols = []
            for dh in range(3):
                g = [gred[9 * dt + 3 * dh + dw, pl.ds(r, 16), :] for dw in range(3)]
                g01 = g[0] + g[1]
                g12 = g[1] + g[2]
                zero = jnp.zeros_like(g01)
                cols.append(
                    (
                        jnp.where(main, jnp.where(b0, g12, zero), jnp.where(b0, zero, g[0])),
                        jnp.where(main, jnp.where(b0, g01, g[2]), zero),
                        jnp.where(main, jnp.where(b0, g[0], g12), zero),
                        jnp.where(main, jnp.where(b0, zero, g01), jnp.where(b0, g[2], zero)),
                    )
                )
            for w in range(4):
                h0, h1, h2 = (cols[dh][w] for dh in range(3))
                h01 = h0 + h1
                h12 = h1 + h2
                for value, ref, t, at in (
                    (h2, bupper, 0, 128 * dt),
                    (h12, bupper, 1, 128 * dt),
                    (h01, bmiddle, 0, 256 * dt),
                    (h0, bmiddle, 1, 256 * dt),
                    (h2, bmiddle, 0, 256 * dt + 128),
                    (h12, bmiddle, 1, 256 * dt + 128),
                    (h01, blower, 0, 128 * dt),
                    (h0, blower, 1, 128 * dt),
                ):
                    row = pl.multiple_of(t * BLK + w * 96 + r, 16)
                    top = value.astype(BF16).astype(F32)
                    rest = value - top
                    first = a0 if at % 256 == 0 and ref is bmiddle or ref is bupper else ~a0
                    ref[pl.ds(row, 16), at : at + 128] = jnp.where(first, top, rest).astype(BF16)
        return 0

    def weights():
        lax.fori_loop(0, 6, combine, 0)

    weights()

    def frame_picks():
        for r in range(2):
            ids = rbuf[r, :, 16:32, :].astype(F32)
            ids = jnp.broadcast_to(ids[:, 15:16, :], (16, 16, 128)).reshape(256, 128)
            ids = jnp.concatenate([ids, ids], axis=1)
            at = iota((256, 256), 1)
            hit = (ids == lax.div(at, 16).astype(F32)) & (
                lax.rem(iota((256, 256), 0), 16) == lax.rem(at, 16)
            )
            picks[:, 256 * r : 256 * r + 256] = jnp.where(hit, 1.0, 0.0).T.astype(BF16)

    def frame_sums(half):
        stack = jnp.concatenate(
            [rbuf[:, :, 16 * g : 16 * g + 16, :].reshape(512, 128) for g in (2 * half, 2 * half + 1)],
            axis=1,
        )
        total = jnp.dot(picks[...], stack, preferred_element_type=F32)
        for g in range(2):
            v = total[:, 128 * g : 128 * g + 128].reshape(8, 2, 16, 128)
            if g == 1:
                v = jnp.where(iota(v.shape, 2) >= 14, 0.0, v)
            sums[half, :, :, 16 * g : 16 * g + 16, :] = v

    def packed(half):
        for owner in range(8):
            v = sums[half, owner]
            largest = jnp.max(jnp.maximum(v[0], v[1]), axis=0, keepdims=True)
            smallest = jnp.min(jnp.minimum(v[0], v[1]), axis=0, keepdims=True)
            largest = jnp.maximum(jnp.maximum(largest, -smallest), 1e-20)
            step = jnp.floor(jnp.log(largest) * EIGHTHS) + 2.0
            scale = RANGE * jnp.exp(step * (-1.0 / EIGHTHS))
            w = jnp.round(v * scale[None])
            w = jnp.where(iota(v.shape, 1) >= 30, step[None], w)
            packs[half, owner] = w.astype(jnp.int32).astype(jnp.int16)

    def unpacked(v):
        v = v.astype(jnp.int32).astype(F32)
        return v * (jnp.exp(v[:, 30:31, :] * (1.0 / EIGHTHS)) * (1.0 / RANGE))

    def z_copy(half, r, d):
        owner = lax.rem(z + d, 4) * 2 + lax.rem(c + r, 2)
        return remote(
            packs.at[half, owner],
            zbuf.at[half, r, d],
            zs.at[half, r, d],
            zr.at[half, r, d],
            (owner, tl),
        )

    partners = tuple((r, d) for d in (2, 1, 3, 0) for r in (1, 0) if r + d > 0)

    for half in range(2):
        for r, d in strips:
            strip_copy(half, r, d).wait_recv()
        if half == 0:
            frame_picks()
        frame_sums(half)
        packed(half)
        for r, d in partners:
            z_copy(half, r, d).start()

    tot = stat_wait(0) / COUNT
    rows = []
    for f in range(2):
        mean = tot[2 * f : 2 * f + 1]
        meansq = tot[2 * f + 1 : 2 * f + 2]
        rstd = lax.rsqrt(meansq - mean * mean + EPS)
        rows.append((mean, rstd))
    table[...] = jnp.zeros((8, 128), F32)
    for f in range(2):
        table[f : f + 1, :] = rows[f][0]
        table[6 + f : 7 + f, 0:96] = 0.5 * rows[f][1][:, 0:96] * gain[...]
    table[4:5, 0:96] = gain[...]
    table[5:6, 0:96] = 0.5 * bias[...]
    cst[...] = exact_dot(table[...], emat[...])

    def factor():
        for f in range(2):
            mean_l = cst[f : f + 1, :]
            a_l = cst[6 + f : 7 + f, :]
            hb_l = cst[5:6, :]
            g2_l = 0.5 * cst[4:5, :]

            def factor_step(i, _, f=f, mean_l=mean_l, a_l=a_l, hb_l=hb_l, g2_l=g2_l):
                b = lax.div(i, 8)
                r = pl.multiple_of(lax.rem(i, 8) * 32, 32)
                v = xb[f * 5 + b, pl.ds(r, 32), :].astype(F32) - mean_l
                u = v * a_l + hb_l
                h = jnp.tanh(u)
                w = (1.0 + u * (1.0 - h)) * ((1.0 + h) * g2_l)
                for i in range(3):
                    xs[f * 5 + b, i, pl.ds(r, 32), :] = v[:, 128 * i : 128 * i + 128]
                    fs[f * 5 + b, i, pl.ds(r, 32), :] = w[:, 128 * i : 128 * i + 128]
                return 0

            lax.fori_loop(0, 40, factor_step, 0)

    factor()

    def frame_rows(half):
        for r in range(2):
            dp = sums[half, tm] if r == 0 else unpacked(zbuf[half, 1, 0])
            for d in range(1, 4):
                dp = dp + unpacked(zbuf[half, r, d])
            for f in range(2):
                top = dp[f].astype(BF16).astype(F32)
                mid = (dp[f] - top).astype(BF16).astype(F32)
                rest = dp[f] - top - mid
                parts = jnp.concatenate([top, mid, rest, jnp.zeros_like(rest)], axis=0).T
                dpx[half, lax.rem(c + r, 2), 128 * f : 128 * f + 128, :] = parts.astype(BF16)

    def dxh(blocks, carry):
        for b in blocks:
            for rows_at in range(2):
                da = None
                for half in range(2):
                    if (half, b) in DXH:
                        v = jnp.dot(
                            dpx[half, rows_at], rmat[half, b], preferred_element_type=F32
                        )
                        da = v if da is None else da + v
                new = []
                for f in range(2):
                    at = pl.ds(128 * rows_at, 128)
                    s, sx = [], []
                    for i in range(3):
                        v = da[128 * f : 128 * f + 128, 128 * i : 128 * i + 128]
                        v = v * fs[f * 5 + b, i, at, :]
                        fs[f * 5 + b, i, at, :] = v
                        s.append(carry[6 * f + i] + fold(v))
                        sx.append(carry[6 * f + 3 + i] + fold(v * xs[f * 5 + b, i, at, :]))
                    new += s + sx
                carry = tuple(new)
        return carry

    carry = tuple(jnp.zeros((8, 128), F32) for _ in range(12))
    for half in range(2):
        for r, d in partners:
            z_copy(half, r, d).wait_recv()
        frame_rows(half)
        carry = dxh((0, 1) if half == 0 else (2, 3, 4), carry)

    def dxh_sums():
        for i in range(12):
            stin[i // 3 : i // 3 + 1, 128 * (i % 3) : 128 * (i % 3) + 128] = jnp.sum(
                carry[i], axis=0, keepdims=True
            )

    dxh_sums()
    stat_send(1)
    tot = stat_wait(1) / COUNT
    terms = []
    for f in range(2):
        rstd = rows[f][1]
        first = tot[2 * f : 2 * f + 1]
        second = tot[2 * f + 1 : 2 * f + 2] * rstd
        terms += [rstd, -rstd * rstd * second, -rstd * first, jnp.zeros_like(rstd)]
    cst[...] = exact_dot(jnp.concatenate(terms, axis=0), emat[...])

    def placed(left, f, b, tap, i, d):
        at = BLK * tap + 128 * i
        left[f, 64 * b : 64 * b + 64, at : at + 128] = d.astype(BF16)

    def left_side(f, rows):
        row = iota((64, 128), 0)
        for i in range(3):
            ls = slice(128 * i, 128 * i + 128)
            p_l = cst[4 * f : 4 * f + 1, ls]
            q_l = cst[4 * f + 1 : 4 * f + 2, ls]
            r_l = cst[4 * f + 2 : 4 * f + 3, ls]
            for b in range(5):
                fb = f * 5 + b
                for rho in rows:
                    sel = pl.ds(rho, 64, stride=4)
                    d = p_l * fs[fb, i, sel, :] + q_l * xs[fb, i, sel, :] + r_l
                    if rho == 0:
                        placed(lupper, f, b, 1, i, d)
                        d = jnp.where(row == 63, 0.0, pltpu.roll(d, 63, 0))
                        placed(llower, f, b, 1, i, d)
                    elif rho == 3:
                        placed(llower, f, b, 0, i, d)
                        d = jnp.where(row == 0, 0.0, pltpu.roll(d, 1, 0))
                        placed(lupper, f, b, 0, i, d)
                    else:
                        placed(lmiddle, f, b, rho - 1, i, d)

    def conv(f, first, last, left, weight, result):
        width = weight.shape[1] // 3
        at = slice(width * first, width * last + width)
        result[320 * f : 320 * f + 320, at] = jnp.dot(
            left[f], weight[:, at], preferred_element_type=F32
        )

    def conv_middle(f, first, last):
        conv(f, first, last, lmiddle, bmiddle, ymiddle)

    def conv_ends(f, first, last):
        conv(f, first, last, lupper, bupper, yupper)
        conv(f, first, last, llower, blower, ylower)

    ln = iota((64, 128), 1)
    lo64 = ln < 64
    odd = lax.rem(ln, 2) == 1
    upper = lax.rem(lax.div(ln, 2), 2) == 0

    def taken(f, dt, b):
        r = slice(64 * (5 * f + b), 64 * (5 * f + b) + 64)
        narrow = slice(128 * dt, 128 * dt + 128)
        return (
            yupper[r, narrow] + ymiddle[r, 256 * dt : 256 * dt + 128],
            ylower[r, narrow] + ymiddle[r, 256 * dt + 128 : 256 * dt + 256],
        )

    def tokens(group, t, terms):
        cc = []
        for b in range(5):
            u, v = taken(*terms[0], b)
            for term in terms[1:]:
                more = taken(*term, b)
                u, v = u + more[0], v + more[1]
            cc.append(jnp.where(upper, u + pltpu.roll(u, 126, 1), v + pltpu.roll(v, 2, 1)))
        r1 = pltpu.roll(cc[1], 64, 1)
        r3 = pltpu.roll(cc[3], 64, 1)
        v0 = jnp.where(
            lo64, cc[0] + jnp.where(odd, r1, 0.0), r1 + jnp.where(odd, cc[2], cc[0])
        )
        v1 = jnp.where(
            lo64, cc[2] + jnp.where(odd, r3, r1), r3 + jnp.where(odd, cc[4], cc[2])
        )
        v2 = jnp.where(lo64, cc[4] + jnp.where(odd, 0.0, r3), jnp.where(odd, cc[0], cc[4]))
        for i, v in enumerate((v0, v1, v2)):
            tok[group, 8 * t : 8 * t + 8, :, 128 * i : 128 * i + 128] = v.reshape(8, 8, 128)

    def own_copy(j, at):
        return remote(tok.at[0, j], trecv.at[0, at], tks.at[0, j], tkr.at[0, at], (tm, j))

    def span_copy(j, at):
        return remote(tok.at[1, j], trecv.at[1, at], tks.at[1, j], tkr.at[1, at], (below, j))

    def owners(t):
        return tuple(
            8 * t + 4 * lax.rem(x + a, 2) + lax.rem(y + b, 4) for b in (2, 1, 3, 0) for a in (1, 0)
        )

    def send_span(t):
        for j in owners(t):
            span_copy(j, tl).start()

    def send_own(t):
        for j in owners(t):

            @pl.when(j != tl)
            def _(j=j):
                own_copy(j, tl).start()

    left_side(0, (1, 2))
    conv_middle(0, 0, 1)
    left_side(0, (0, 3))
    conv_ends(0, 0, 1)
    tokens(1, 0, ((0, 0),))
    send_span(0)
    left_side(1, (1, 2))
    conv_middle(1, 0, 0)
    left_side(1, (0, 3))
    conv_ends(1, 0, 0)
    tokens(1, 1, ((0, 1), (1, 0)))
    send_span(1)
    conv_middle(0, 2, 2)
    conv_ends(0, 2, 2)
    conv_middle(1, 1, 2)
    conv_ends(1, 1, 2)
    tokens(0, 0, ((0, 2), (1, 1)))
    send_own(0)
    tokens(0, 1, ((1, 2),))
    send_own(1)
    trecv[0, tl] = tok[0, tl]

    for place in FARTHEST + ((0, 0),):
        j = tile_at(place)
        span_copy(j, j).wait_recv()
    for place in FARTHEST:
        j = tile_at(place)
        own_copy(j, j).wait_recv()

    def assemble():
        ln = iota((8, 128), 1)
        lo8 = ln < 64
        odd8 = lax.rem(ln, 2) == 1
        strips = []
        for j in range(16):
            strips.append(
                [
                    trecv[0, j, :, 128 * i : 128 * i + 128]
                    + jnp.where(tm < 7, trecv[1, j, :, 128 * i : 128 * i + 128], 0.0)
                    for i in range(3)
                ]
            )
        halo = [pltpu.roll(s[2], 64, 1) for s in strips]
        for j in range(16):
            if j > 0:
                strips[j][0] = strips[j][0] + jnp.where(lo8 & ~odd8, halo[j - 1], 0.0)
        done = []
        for j in range(16):
            v2 = strips[j][2]
            if j < 15:
                v2 = v2 + jnp.where(odd8, halo[j + 1], 0.0)
            done.append((strips[j][0], strips[j][1], v2))
        for pair in range(8):
            e = done[2 * pair]
            o = [pltpu.roll(v, 64, 1) for v in done[2 * pair + 1]]
            at = 640 * pair
            out[:, at : at + 128] = e[0]
            out[:, at + 128 : at + 256] = e[1]
            out[:, at + 256 : at + 384] = jnp.where(lo8, e[2], o[0])
            out[:, at + 384 : at + 512] = jnp.where(lo8, o[0], o[1])
            out[:, at + 512 : at + 640] = jnp.where(lo8, o[1], o[2])

    assemble()

    for half in range(2):
        for r, d in strips:
            strip_copy(half, r, d).wait_send()
        for r, d in partners:
            z_copy(half, r, d).wait_send()
        for d in range(1, 16):
            stat_copy(half, d).wait_send()
    for place in FARTHEST:
        own_copy(tile_at(place), tl).wait_send()
    for place in FARTHEST + ((0, 0),):
        span_copy(tile_at(place), tl).wait_send()


def body(pix_grad, frame_ids, pre_norm, gain, bias, out_weight, conv_weight, in_weight):
    hbm = pl.BlockSpec(memory_space=pltpu.HBM)
    smem = pl.BlockSpec(memory_space=pltpu.SMEM)
    dma = pltpu.SemaphoreType.DMA

    def kept(array):
        return pltpu.with_memory_space_constraint(array, pltpu.HBM)

    pix_grad = jnp.transpose(pix_grad, (0, 1, 3, 2))
    out_weight = out_weight.T
    gain = gain.reshape(1, 96)
    bias = bias.reshape(1, 96)
    return pl.pallas_call(
        kernel,
        out_shape=jax.ShapeDtypeStruct((8, 5120), F32),
        in_specs=[hbm, smem] + [hbm] * 6,
        out_specs=pl.BlockSpec(memory_space=pltpu.VMEM),
        scratch_shapes=[
            pltpu.VMEM((1, 96), F32),
            pltpu.VMEM((1, 96), F32),
            pltpu.VMEM((3, 96), BF16),
            pltpu.VMEM((16, 384), BF16),
            pltpu.VMEM((3, 320, 256), BF16),
            pltpu.VMEM((PIECES, 256, BLK), BF16),
            pltpu.VMEM((27, 96, 384), BF16),
            pltpu.VMEM((2, 16, 64, 128), BF16),
            pltpu.VMEM((2, 16, 64, 128), BF16),
            pltpu.VMEM((256, 512), BF16),
            pltpu.VMEM((2, 8, 2, 32, 128), F32),
            pltpu.VMEM((2, 8, 2, 32, 128), jnp.int16),
            pltpu.VMEM((2, 2, 4, 2, 32, 128), jnp.int16),
            pltpu.VMEM((2, 2, 256, 128), BF16),
            pltpu.VMEM((2, 5, 128, BLK), BF16),
            pltpu.VMEM((PIECES, 3, 256, 128), F32),
            pltpu.VMEM((PIECES, 3, 256, 128), F32),
            pltpu.VMEM((BLK, 128), BF16),
            pltpu.VMEM((128, BLK), BF16),
            pltpu.VMEM((8, BLK), F32),
            pltpu.VMEM((2, 8, 128), F32),
            pltpu.VMEM((2, 16, 8, 128), F32),
            pltpu.VMEM((8, 128), F32),
            pltpu.VMEM((8, BLK), F32),
            pltpu.VMEM((27, 96, 128), F32),
            pltpu.VMEM((2 * BLK, BLK), BF16),
            pltpu.VMEM((2 * BLK, 2 * BLK), BF16),
            pltpu.VMEM((2 * BLK, BLK), BF16),
            pltpu.VMEM((2, 320, 2 * BLK), BF16),
            pltpu.VMEM((2, 320, 2 * BLK), BF16),
            pltpu.VMEM((2, 320, 2 * BLK), BF16),
            pltpu.VMEM((640, BLK), F32),
            pltpu.VMEM((640, 2 * BLK), F32),
            pltpu.VMEM((640, BLK), F32),
            pltpu.VMEM((2, 16, 8, BLK), F32),
            pltpu.VMEM((2, 16, 8, BLK), F32),
            pltpu.SemaphoreType.REGULAR,
            dma,
            dma((PIECES,)),
            dma,
            dma((4,)),
            dma((2, 2, 16)),
            dma((2, 2, 16)),
            dma((2, 2, 4)),
            dma((2, 2, 4)),
            dma((2, 16)),
            dma((2, 16)),
            dma((2, 16)),
            dma((2, 16)),
        ],
        compiler_params=pltpu.CompilerParams(
            collective_id=0, has_side_effects=True, vmem_limit_bytes=50 * 1024 * 1024
        ),
    )(
        kept(pix_grad),
        frame_ids,
        kept(pre_norm),
        kept(gain),
        kept(bias),
        kept(out_weight),
        kept(conv_weight),
        kept(in_weight),
    )


def solution(mesh):
    return jax.shard_map(
        body,
        mesh=mesh,
        in_specs=(
            P(("tm", "tile"), None, None, None),
            P(("tm", "tile")),
            P("tm", None, "tile"),
            P(),
            P(),
            P(),
            P(),
            P(),
        ),
        out_specs=P(("tm", "tile"), None),
        check_vma=False,
    )
```
